32 devices in a mesh: dp: 16 (over z, x, core), tp: 2 (over y).
Axes of the slice: x: 2, y: 2, z: 4, core: 2. Of those that a mesh axis runs over, the one named last changes fastest.
Arguments:
- tokens: bfloat16 [32768, 768], P(('dp', 'tp')), may hold values from -6 to 6
- neighbours: bfloat16 [512, 256, 768], P('dp', 'tp'), may hold values from -6 to 6
- nbr_index: int32 [16, 32], P('dp'), may hold values from 0 to 31, each once within a row
- lengths: int32 [16, 2], P('dp'), may hold values from 256 to 1024, as said below
- w_qkv: bfloat16 [768, 3, 768], P(None, None, 'tp'), may hold values from -0.21875 to 0.21875
- qv_bias: bfloat16 [2, 768], P(None, 'tp'), may hold values from -4 to 4
- w_out: bfloat16 [768, 768], P('tp'), may hold values from -2.5 to 2.5
- cross_q: bfloat16 [768, 768], P(None, 'tp'), may hold values from -0.21875 to 0.21875
- cross_kv: bfloat16 [768, 2, 768], P(None, None, 'tp'), may hold values from -0.21875 to 0.21875
- cross_bias: bfloat16 [2, 768], P(None, 'tp'), may hold values from -4 to 4
- cross_out: bfloat16 [768, 768], P('tp'), may hold values from -1.75 to 1.75
- out_bias: bfloat16 [2, 768], P(None, 'tp'), may hold values from -4 to 4
- ln_gain: bfloat16 [3, 768], P(None, 'tp'), may hold values from 0.5 to 1.5
- ln_bias: bfloat16 [3, 768], P(None, 'tp'), may hold values from -4 to 4
- fc_in: bfloat16 [768, 3072], P('tp'), may hold values from -0.21875 to 0.21875
- fc_in_bias: bfloat16 [3072], P('tp'), may hold values from -4 to 4
- fc_out: bfloat16 [3072, 768], P('tp'), may hold values from -0.109375 to 0.109375
- fc_out_bias: bfloat16 [768], P('tp'), may hold values from -4 to 4
- cotangent: bfloat16 [32768, 768], P(('dp', 'tp')), may hold values from -6 to 6
Outputs:
- block_out: bfloat16 [32768, 768], P(('dp', 'tp'))
- tokens_grad: float32 [32768, 768], P(('dp', 'tp'))
- neighbours_grad: float32 [512, 256, 768], P('dp', 'tp')
- w_qkv_grad: float32 [768, 3, 768], P(None, None, 'tp')
- qv_bias_grad: float32 [2, 768], P(None, 'tp')
- w_out_grad: float32 [768, 768], P('tp')
- cross_q_grad: float32 [768, 768], P(None, 'tp')
- cross_kv_grad: float32 [768, 2, 768], P(None, None, 'tp')
- cross_bias_grad: float32 [2, 768], P(None, 'tp')
- cross_out_grad: float32 [768, 768], P('tp')
- out_bias_grad: float32 [2, 768], P(None, 'tp')
- ln_gain_grad: float32 [3, 768], P(None, 'tp')
- ln_bias_grad: float32 [3, 768], P(None, 'tp')
- fc_in_grad: float32 [768, 3072], P('tp')
- fc_in_bias_grad: float32 [3072], P('tp')
- fc_out_grad: float32 [3072, 768], P('tp')
- fc_out_bias_grad: float32 [768], P('tp')
The draws below stay inside these ranges and needn't reach their ends.
Inputs may be any that keep to these rules, and one draw needn't show every extreme that they name: `lengths`: each group has 2 slots of 1024 token positions; positions of a slot from its length on are padding. In every group one slot is full. `nbr_index`: each row is a permutation of its group's 32 neighbour blocks.
All inputs are finite; a program needn't handle non-finite values.
Results may differ from the reference program's by a relative error of at most 0.025.
Values may be sent and summed in bfloat16 or wider, within the bound.
A program may use at most 320 MiB of HBM per device.

```python
import jax
import jax.numpy as jnp
from jax import lax

HEADS = 12
HEAD_DIM = 64
D = 768
FF = 3072
SPAN = 64
LEN = 1024
SEQS = 2
GROUPS = 16
NBR = 256
SPANS = 32
TOKENS = 32768
NBLOCKS = 512


def draw_lengths(key, part):
    key = jax.random.fold_in(key, 11)
    first_key, second_key = jax.random.split(key)
    drawn = jax.random.randint(first_key, (GROUPS, SEQS), LEN // 4, LEN + 1)
    full_slot = jax.random.randint(second_key, (GROUPS, 1), 0, SEQS)
    slots = jnp.arange(SEQS, dtype=jnp.int32)[None, :]
    return jnp.where(slots == full_slot, LEN, drawn).astype(jnp.int32)


def block_levels(own_key, shape, cuts, least, largest):
    level = 1.0
    for dim, shards_of in cuts:
        draws = jax.random.uniform(jax.random.fold_in(jax.random.fold_in(own_key, 6), dim), (shards_of,), jnp.float32, least / len(cuts), largest / len(cuts))
        level = level * jnp.repeat(jnp.exp(draws), shape[dim] // shards_of).reshape((-1,) + (1,) * (len(shape) - 1 - dim))
    return level


def gaussian(key, extent, width, limit, shards=(), kind=jnp.bfloat16):
    factor_of = block_levels(key, extent, shards, -0.22, 0.18) if shards else 1.0
    result = jax.random.normal(key, extent, jnp.float32) * width * factor_of
    return jnp.minimum(jnp.maximum(result, -limit), limit).astype(kind)


def setup_inputs(seed: int = 0) -> dict:
    splits = jax.random.split(jax.random.key(seed), 20)
    tokens = gaussian(splits[0], (TOKENS, D), 1.0, 6.0, ((0, 32),))
    neighbours = gaussian(splits[1], (NBLOCKS, NBR, D), 1.0, 6.0, ((0, 16), (1, 2)))
    nbr_index = jax.vmap(lambda own: jax.random.permutation(own, SPANS))(jax.random.split(splits[2], GROUPS)).reshape((GROUPS, SPANS)).astype(jnp.int32)
    lengths = draw_lengths(jax.random.fold_in(splits[19], 71), 0)
    w_qkv = gaussian(splits[4], (D, 3, D), D ** -0.5, 0.21875, ((2, 2),))
    qv_bias = gaussian(splits[5], (2, D), 0.3, 4.0, ((1, 2),))
    w_out = gaussian(splits[6], (D, D), (max(D // 128, 1)) ** -0.5, 2.5, ((0, 2),))
    cross_q = gaussian(splits[7], (D, D), D ** -0.5, 0.21875, ((1, 2),))
    cross_kv = gaussian(splits[8], (D, 2, D), D ** -0.5, 0.21875, ((2, 2),))
    cross_bias = gaussian(splits[9], (2, D), 0.3, 4.0, ((1, 2),))
    cross_out = gaussian(splits[10], (D, D), (max(D // 64, 1)) ** -0.5, 1.75, ((0, 2),))
    out_bias = gaussian(splits[11], (2, D), 0.3, 4.0, ((1, 2),))
    ln_gain = jnp.clip(1.0 + 0.1 * jax.random.normal(splits[12], (3, D), jnp.float32), 0.5, 1.5).astype(jnp.bfloat16)
    ln_bias = gaussian(splits[13], (3, D), 0.3, 4.0, ((1, 2),))
    fc_in = gaussian(splits[14], (D, FF), D ** -0.5, 0.21875, ((0, 2),))
    fc_in_bias = gaussian(splits[15], (FF,), 0.3, 4.0, ((0, 2),))
    fc_out = gaussian(splits[16], (FF, D), FF ** -0.5, 0.109375, ((0, 2),))
    fc_out_bias = gaussian(splits[17], (D,), 0.3, 4.0, ((0, 2),))
    cotangent = gaussian(splits[18], (TOKENS, D), 1.0, 6.0, ((0, 32),))
    return dict(tokens=tokens, neighbours=neighbours, nbr_index=nbr_index, lengths=lengths, w_qkv=w_qkv, qv_bias=qv_bias, w_out=w_out, cross_q=cross_q, cross_kv=cross_kv, cross_bias=cross_bias, cross_out=cross_out, out_bias=out_bias, ln_gain=ln_gain, ln_bias=ln_bias, fc_in=fc_in, fc_in_bias=fc_in_bias, fc_out=fc_out, fc_out_bias=fc_out_bias, cotangent=cotangent)


@jax.custom_vjp
def low(v):
    return lax.optimization_barrier(v.astype(jnp.bfloat16)).astype(jnp.float32)

@jax.custom_vjp
def low_back(v):
    return v

def low_keep(v):
    return (low(v), None)

def low_pass(kept, grad):
    return (grad,)

def back_keep(v):
    return (v, None)

def back_low(kept, grad):
    return (low(grad),)
low.defvjp(low_keep, low_pass)
low_back.defvjp(back_keep, back_low)
eps_norm = 1e-05
highest = lax.Precision.HIGHEST

def layer_norm(row_data, norm_gain, norm_bias):
    average = lax.optimization_barrier(jnp.mean(row_data, axis=-1, keepdims=True))
    centred = row_data - average
    spread = lax.optimization_barrier(jnp.mean(centred * centred, axis=-1, keepdims=True))
    return centred * lax.rsqrt(spread + eps_norm) * norm_gain + norm_bias

def rounded(values):
    return low(low_back(values))

def self_sequence(packed):
    queries, key_rows, values, length = packed
    places = jnp.arange(LEN, dtype=jnp.int32)
    products = jnp.einsum('qhd,khd->hqk', queries, key_rows, precision=highest)
    scores = low_back(0.125 * products)
    allowed = (places[None, :] <= places[:, None]) & (places[None, :] < length)
    scores = jnp.where(allowed[None], scores, -1000000000.0)
    weights = low(jax.nn.softmax(scores, axis=-1))
    return jnp.einsum('hqk,khd->qhd', weights, values, precision=highest)

def cross_group(packed):
    queries, key_rows, values = packed
    products = jnp.einsum('cmhd,cnhd->chmn', queries, key_rows, precision=highest)
    weights = low(jax.nn.softmax(low_back(0.125 * products), axis=-1))
    return jnp.einsum('chmn,cnhd->cmhd', weights, values, precision=highest)

def make_forward(nbr_index, lengths):
    group_count = lengths.shape[0]
    seq_count = group_count * SEQS
    group_first = jnp.arange(group_count, dtype=jnp.int32)[:, None] * SPANS
    block_order = (nbr_index.astype(jnp.int32) + group_first).reshape(-1)
    seq_lengths = lengths.astype(jnp.int32).reshape(-1)
    head_shape = (seq_count, LEN, HEADS, HEAD_DIM)

    def forward(inputs, nbr_rows, wqkv, qv_b, wout, crossq, crosskv, cross_b, crossout, out_b, gains, shifts, w_in, b_in, w_back, b_back):
        total_rows = inputs.shape[0]
        rows_one = low(layer_norm(inputs, gains[0], shifts[0]))
        qkv_all = jnp.einsum('td,dkc->tkc', rows_one, wqkv, precision=highest)
        queries = rounded(qkv_all[:, 0] + qv_b[0]).reshape(head_shape)
        key_rows = rounded(qkv_all[:, 1]).reshape(head_shape)
        values = rounded(qkv_all[:, 2] + qv_b[1]).reshape(head_shape)
        self_ctx = lax.map(jax.checkpoint(self_sequence), (queries, key_rows, values, seq_lengths))
        self_ctx = rounded(self_ctx.reshape(total_rows, D))
        resid_one = inputs + low_back(jnp.dot(self_ctx, wout, precision=highest)) + out_b[0]
        rows_two = low(layer_norm(resid_one, gains[1], shifts[1]))
        cross_queries = rounded(jnp.dot(rows_two, crossq, precision=highest) + cross_b[0])
        key_value = jnp.einsum('bnd,dkc->bnkc', nbr_rows, crosskv, precision=highest)
        span_shape = (group_count, SPANS, NBR, HEADS, HEAD_DIM)
        cross_keys = rounded(key_value[:, :, 0])[block_order].reshape(span_shape)
        cross_values = rounded(key_value[:, :, 1] + cross_b[1])[block_order].reshape(span_shape)
        shaped = cross_queries.reshape(seq_count, LEN, D)
        padding = jnp.zeros((seq_count, SPAN - 1, D), shaped.dtype)
        shifted = jnp.concatenate([shaped[:, SPAN - 1:], padding], axis=1)
        shifted = shifted.reshape(group_count, SPANS, SPAN, HEADS, HEAD_DIM)
        context = lax.map(jax.checkpoint(cross_group), (shifted, cross_keys, cross_values))
        context = context.reshape(seq_count, LEN, D)
        context = jnp.concatenate([padding, context[:, :LEN - SPAN + 1]], axis=1)
        cross_ctx = rounded(context.reshape(total_rows, D))
        resid_two = resid_one + low_back(jnp.dot(cross_ctx, crossout, precision=highest)) + out_b[1]
        rows_three = low(layer_norm(resid_two, gains[2], shifts[2]))
        hidden_pre = low_back(jnp.dot(rows_three, w_in, precision=highest) + b_in)
        hidden_act = low(jax.nn.gelu(hidden_pre, approximate=True))
        return resid_two + jnp.dot(hidden_act, w_back, precision=highest) + b_back
    return forward

def reference(tokens, neighbours, nbr_index, lengths, w_qkv, qv_bias, w_out, cross_q, cross_kv, cross_bias, cross_out, out_bias, ln_gain, ln_bias, fc_in, fc_in_bias, fc_out, fc_out_bias, cotangent):
    forward = make_forward(nbr_index, lengths)
    wide = jnp.float32
    block_out, backward = jax.vjp(forward, tokens.astype(wide), neighbours.astype(wide), w_qkv.astype(wide), qv_bias.astype(wide), w_out.astype(wide), cross_q.astype(wide), cross_kv.astype(wide), cross_bias.astype(wide), cross_out.astype(wide), out_bias.astype(wide), ln_gain.astype(wide), ln_bias.astype(wide), fc_in.astype(wide), fc_in_bias.astype(wide), fc_out.astype(wide), fc_out_bias.astype(wide))
    grads = backward(cotangent.astype(wide))
    return (block_out.astype(jnp.bfloat16), grads[0], grads[1], grads[2], grads[3], grads[4], grads[5], grads[6], grads[7], grads[8], grads[9], grads[10], grads[11], grads[12], grads[13], grads[14], grads[15])
```

```python
import functools

import jax
import jax.numpy as jnp
from jax import lax
from jax.experimental import pallas as pl
from jax.experimental.pallas import tpu as pltpu
from jax.sharding import PartitionSpec as P

HEAD = 64
SPAN = 64
LEN = 1024
NBR = 256
EPS = 1e-05
BF = jnp.bfloat16
F32 = jnp.float32
DEAD = -1e30
VMEM_LIMIT = 60 * 1024 * 1024

NN = (((1,), (0,)), ((), ()))
NT = (((1,), (1,)), ((), ()))
TN = (((0,), (0,)), ((), ()))


def mm(a, b, dims=NN):
    return lax.dot_general(a, b, dims, preferred_element_type=F32)


def iota(shape, dim):
    return lax.broadcasted_iota(jnp.int32, shape, dim)


def cost(flops, nbytes, exps=0):
    return pl.CostEstimate(flops=flops, bytes_accessed=nbytes, transcendentals=exps)


def params(n=1):
    return pltpu.CompilerParams(
        dimension_semantics=("arbitrary",) * n, vmem_limit_bytes=VMEM_LIMIT
    )


def self_fwd_kernel(len_ref, q_ref, k_ref, v_ref, o_ref, lse_ref):
    bq = 256
    length = len_ref[0]
    low = iota((LEN, 128), 1) < HEAD
    q = q_ref[...] * 0.125
    k = k_ref[...]
    v = v_ref[...]
    one = jnp.ones_like(v)
    zero = jnp.zeros_like(q)
    qs = (jnp.where(low, q, zero), jnp.where(low, zero, q))
    vs = (jnp.where(low, v, one), jnp.where(low, one, v))
    dead = jnp.where(iota((1, LEN), 1) < length, 0.0, DEAD).astype(F32)
    tri = iota((bq, bq), 1) <= iota((bq, bq), 0)
    low_q = low[:bq]
    for i in range(LEN // bq):
        nk = (i + 1) * bq
        outs, lses = [], []
        for h in range(2):
            s = mm(qs[h][i * bq : nk], k[:nk], NT) + dead[:, :nk]
            last = jnp.where(tri, s[:, nk - bq :], DEAD)
            s = jnp.concatenate([s[:, : nk - bq], last], axis=1) if i else last
            m = jnp.max(s, axis=1, keepdims=True)
            p = jnp.exp(s - m).astype(BF)
            o = mm(p, vs[h][:nk])
            total = pltpu.roll(o, HEAD, 1)
            outs.append(o / total)
            lses.append(m + jnp.log(total))
        o_ref[i * bq : nk, :] = jnp.where(low_q, outs[0], outs[1]).astype(BF)
        both = jnp.where(low_q, lses[0], lses[1]).T
        lse_ref[0, 0:1, i * bq : nk] = both[0:1]
        lse_ref[0, 1:2, i * bq : nk] = both[HEAD : HEAD + 1]


def self_fwd(qkv, length):
    pairs = qkv.shape[1] // 3 // 128
    block = lambda part: pl.BlockSpec((LEN, 128), lambda i, n: (0, part * pairs + i))
    return pl.pallas_call(
        self_fwd_kernel,
        grid_spec=pltpu.PrefetchScalarGridSpec(
            num_scalar_prefetch=1,
            grid=(pairs,),
            in_specs=[block(0), block(1), block(2)],
            out_specs=[
                pl.BlockSpec((LEN, 128), lambda i, n: (0, i)),
                pl.BlockSpec((1, 8, LEN), lambda i, n: (i, 0, 0)),
            ],
        ),
        out_shape=[
            jax.ShapeDtypeStruct((LEN, pairs * 128), BF),
            jax.ShapeDtypeStruct((pairs, 8, LEN), F32),
        ],
        compiler_params=params(),
        cost_estimate=cost(pairs * 2 * 4 * LEN * LEN * 128, pairs * 8 * LEN * 128),
    )(length, qkv, qkv, qkv)


def self_bwd_kernel(len_ref, q_ref, k_ref, v_ref, f_ref, o_ref, lse_ref, d_ref, dq_ref):
    bk = 256
    length = len_ref[0]
    low = iota((LEN, 128), 1) < HEAD
    q = q_ref[...] * 0.125
    k = k_ref[...]
    v = v_ref[...]
    f = f_ref[...]
    zero = jnp.zeros_like(q)
    qs = (jnp.where(low, q, zero), jnp.where(low, zero, q))
    fs = (jnp.where(low, f, zero), jnp.where(low, zero, f))
    prod = (f.astype(F32) * o_ref[...].astype(F32)).T
    deltas = (
        jnp.sum(prod[:HEAD], axis=0, keepdims=True),
        jnp.sum(prod[HEAD:], axis=0, keepdims=True),
    )
    k_t = k.T
    tri = iota((bk, bk), 0) <= iota((bk, bk), 1)
    for j in range(LEN // bk):
        lo = j * bk
        live = lo + iota((bk, 1), 0) < length
        dk = jnp.zeros((bk, 128), F32)
        dv = jnp.zeros((bk, 128), F32)
        for h in range(2):
            s = mm(k[lo : lo + bk], qs[h][lo:], NT)
            p = jnp.exp(s - lse_ref[0, h : h + 1, lo:])
            first = jnp.where(tri, p[:, :bk], 0.0)
            p = jnp.concatenate([first, p[:, bk:]], axis=1) if lo + bk < LEN else first
            if j:
                p = jnp.where(live, p, 0.0)
            dp = mm(v[lo : lo + bk], fs[h][lo:], NT)
            ds = (p * (dp - deltas[h][:, lo:])).astype(BF)
            dv += mm(p.astype(BF), fs[h][lo:])
            dk += mm(ds, qs[h][lo:])
            part = mm(k_t[h * HEAD : (h + 1) * HEAD, lo : lo + bk], ds)
            rows = slice(h * HEAD, (h + 1) * HEAD)
            if j:
                dq_ref[rows, lo:] += part
            else:
                dq_ref[rows, :] = part
        d_ref[1, lo : lo + bk, :] = dk.astype(BF)
        d_ref[2, lo : lo + bk, :] = dv.astype(BF)
    d_ref[0] = (dq_ref[...].T * 0.125).astype(BF)


def self_bwd(qkv, back, ctx, lse, length):
    pairs = qkv.shape[1] // 3 // 128
    block = lambda part: pl.BlockSpec((LEN, 128), lambda i, n: (0, part * pairs + i))
    return pl.pallas_call(
        self_bwd_kernel,
        grid_spec=pltpu.PrefetchScalarGridSpec(
            num_scalar_prefetch=1,
            grid=(pairs,),
            in_specs=[
                block(0),
                block(1),
                block(2),
                pl.BlockSpec((LEN, 128), lambda i, n: (0, i)),
                pl.BlockSpec((LEN, 128), lambda i, n: (0, i)),
                pl.BlockSpec((1, 8, LEN), lambda i, n: (i, 0, 0)),
            ],
            out_specs=pl.BlockSpec((3, LEN, 128), lambda i, n: (0, 0, i)),
            scratch_shapes=[pltpu.VMEM((128, LEN), F32)],
        ),
        out_shape=jax.ShapeDtypeStruct((3, LEN, pairs * 128), BF),
        compiler_params=params(),
        cost_estimate=cost(pairs * 2 * 10 * LEN * LEN * 128, pairs * 16 * LEN * 128),
    )(length, qkv, qkv, qkv, back, ctx, lse)


def spread(rows, mask):
    four = jnp.concatenate([rows] * 4, axis=0)
    return jnp.where(mask, four, jnp.zeros_like(four))


def gathered(rows, lanes):
    out = jnp.where(lanes == 0, rows[:SPAN], 0.0)
    for g in range(1, 4):
        out = jnp.where(lanes == g, rows[g * SPAN : (g + 1) * SPAN], out)
    return out


def cross_fwd_kernel(q_ref, own_ref, oth_ref, o_ref):
    width = q_ref.shape[1]
    mask = iota((256, 256), 0) // SPAN == iota((256, 256), 1) // HEAD
    lanes = iota((SPAN, 256), 1) // HEAD
    for t in range(width // 256):
        lo = t * 256
        q4 = spread(q_ref[:, lo : lo + 256] * 0.125, mask)
        k = jnp.concatenate([own_ref[:, lo : lo + 256], oth_ref[:, lo : lo + 256]], axis=0)
        lo += width
        v = jnp.concatenate([own_ref[:, lo : lo + 256], oth_ref[:, lo : lo + 256]], axis=0)
        s = mm(q4, k, NT)
        p = jnp.exp(s - jnp.max(s, axis=1, keepdims=True))
        total = jnp.sum(p, axis=1, keepdims=True)
        o = mm(p.astype(BF), v) / total
        o_ref[:, t * 256 : (t + 1) * 256] = gathered(o, lanes).astype(BF)


def cross_fwd(q, own, oth):
    width = q.shape[1]
    spans = q.shape[0] // SPAN
    rows = own.shape[0] // spans
    return pl.pallas_call(
        cross_fwd_kernel,
        grid=(spans,),
        in_specs=[
            pl.BlockSpec((SPAN, width), lambda i: (i, 0)),
            pl.BlockSpec((rows, 2 * width), lambda i: (i, 0)),
            pl.BlockSpec((rows, 2 * width), lambda i: (i, 0)),
        ],
        out_specs=pl.BlockSpec((SPAN, width), lambda i: (i, 0)),
        out_shape=jax.ShapeDtypeStruct(q.shape, BF),
        compiler_params=params(),
        cost_estimate=cost(spans * 3 * 4 * 256**3, spans * 1000000),
    )(q, own, oth)


def cross_bwd_kernel(q_ref, own_ref, oth_ref, e_ref, dq_ref, down_ref, doth_ref):
    width = q_ref.shape[1]
    half = own_ref.shape[0]
    mask = iota((256, 256), 0) // SPAN == iota((256, 256), 1) // HEAD
    lanes = iota((SPAN, 256), 1) // HEAD
    for t in range(width // 256):
        at = slice(t * 256, (t + 1) * 256)
        at_v = slice(width + t * 256, width + (t + 1) * 256)
        q4 = spread(q_ref[:, at] * 0.125, mask)
        e4 = spread(e_ref[:, at], mask)
        k = jnp.concatenate([own_ref[:, at], oth_ref[:, at]], axis=0)
        v = jnp.concatenate([own_ref[:, at_v], oth_ref[:, at_v]], axis=0)
        s = mm(k, q4, NT)
        p = jnp.exp(s - jnp.max(s, axis=0, keepdims=True))
        p = p * (1.0 / jnp.sum(p, axis=0, keepdims=True))
        dp = mm(v, e4, NT)
        delta = jnp.sum(p * dp, axis=0, keepdims=True)
        ds = (p * (dp - delta)).astype(BF)
        dk = mm(ds, q4).astype(BF)
        dv = mm(p.astype(BF), e4).astype(BF)
        down_ref[:, at] = dk[:half]
        doth_ref[:, at] = dk[half:]
        down_ref[:, at_v] = dv[:half]
        doth_ref[:, at_v] = dv[half:]
        dq_ref[:, at] = (gathered(mm(ds, k, TN), lanes) * 0.125).astype(BF)


def cross_bwd(q, own, oth, e):
    width = q.shape[1]
    spans = q.shape[0] // SPAN
    rows = own.shape[0] // spans
    row = pl.BlockSpec((SPAN, width), lambda i: (i, 0))
    kv = pl.BlockSpec((rows, 2 * width), lambda i: (i, 0))
    return pl.pallas_call(
        cross_bwd_kernel,
        grid=(spans,),
        in_specs=[row, kv, kv, row],
        out_specs=[row, kv, kv],
        out_shape=[
            jax.ShapeDtypeStruct(q.shape, BF),
            jax.ShapeDtypeStruct(own.shape, BF),
            jax.ShapeDtypeStruct(oth.shape, BF),
        ],
        compiler_params=params(),
        cost_estimate=cost(spans * 3 * 10 * 256**3, spans * 2000000),
    )(q, own, oth, e)


def pick_kernel(keep_ref, send_ref, a_ref, b_ref, keep_out, send_out):
    keep_out[...] = a_ref[...]
    send_out[...] = b_ref[...]


def pick_blocks(neighbours, keep, send):
    count = keep.shape[0]
    one = (1,) + neighbours.shape[1:]
    out = pl.BlockSpec(one, lambda i, a, b: (i, 0, 0))
    return pl.pallas_call(
        pick_kernel,
        grid_spec=pltpu.PrefetchScalarGridSpec(
            num_scalar_prefetch=2,
            grid=(count,),
            in_specs=[
                pl.BlockSpec(one, lambda i, a, b: (a[i], 0, 0)),
                pl.BlockSpec(one, lambda i, a, b: (b[i], 0, 0)),
            ],
            out_specs=[out, out],
        ),
        out_shape=[jax.ShapeDtypeStruct((count,) + neighbours.shape[1:], BF)] * 2,
        compiler_params=params(),
        cost_estimate=cost(0, 4 * neighbours.size),
    )(keep, send, neighbours, neighbours)


def place_kernel(order_ref, a_ref, b_ref, out_ref):
    half = pl.num_programs(0) // 2

    @pl.when(pl.program_id(0) < half)
    def _():
        out_ref[...] = a_ref[...]

    @pl.when(pl.program_id(0) >= half)
    def _():
        out_ref[...] = b_ref[...].astype(F32)


def place_blocks(order, mine, theirs):
    count = order.shape[0]
    half = count // 2
    one = (1,) + mine.shape[1:]
    return pl.pallas_call(
        place_kernel,
        grid_spec=pltpu.PrefetchScalarGridSpec(
            num_scalar_prefetch=1,
            grid=(count,),
            in_specs=[
                pl.BlockSpec(one, lambda i, o: (jnp.minimum(i, half - 1), 0, 0)),
                pl.BlockSpec(one, lambda i, o: (jnp.maximum(i - half, 0), 0, 0)),
            ],
            out_specs=pl.BlockSpec(one, lambda i, o: (o[i], 0, 0)),
        ),
        out_shape=jax.ShapeDtypeStruct((count,) + mine.shape[1:], F32),
        compiler_params=params(),
        cost_estimate=cost(0, 8 * mine.size),
    )(order, mine, theirs)


GELU_A = 0.7978845608028654
GELU_B = 0.044715


def feed_kernel(
    h_ref, g_ref, r_ref, win_ref, bin_ref, wout_ref, bout_ref,
    out_ref, dh_ref, gin_ref, gout_ref, gbin_ref, h_t, acc, dacc,
):
    step = pl.program_id(0)

    @pl.when(step == 0)
    def _():
        h_t[...] = h_ref[...].T

    win = win_ref[...]
    wout = wout_ref[...]
    pre = mm(h_ref[...], win) + bin_ref[...]
    dact = mm(g_ref[...], wout, NT)
    square = pre * pre
    th = jnp.tanh(GELU_A * pre * (1.0 + GELU_B * square))
    half = 0.5 * (1.0 + th)
    act = (pre * half).astype(BF)
    slope = half + 0.5 * pre * (1.0 - th * th) * (GELU_A * (1.0 + 3.0 * GELU_B * square))
    dpre_wide = dact * slope
    dpre = dpre_wide.astype(BF)
    gbin_ref[0:1, :] = jnp.sum(dpre.astype(F32), axis=0, keepdims=True)
    gout_ref[...] = mm(act, g_ref[...], TN).astype(BF)
    gin_ref[0] = mm(h_t[...], dpre).astype(BF)
    part = mm(act, wout)
    dpart = mm(dpre, win, NT)

    @pl.when(step == 0)
    def _():
        acc[...] = part
        dacc[...] = dpart

    @pl.when(step > 0)
    def _():
        acc[...] += part
        dacc[...] += dpart

    @pl.when(step == pl.num_programs(0) - 1)
    def _():
        out_ref[...] = (r_ref[...] + acc[...] + bout_ref[...]).astype(BF)
        dh_ref[...] = dacc[...]


def feed(h, g, r, w_in, b_in, w_out, b_out):
    rows, d = h.shape
    ff = w_in.shape[1]
    bf = 384
    per = d // bf
    whole = pl.BlockSpec((rows, d), lambda i: (0, 0))
    return pl.pallas_call(
        feed_kernel,
        grid=(ff // bf,),
        in_specs=[
            whole,
            whole,
            whole,
            pl.BlockSpec((d, bf), lambda i: (0, i)),
            pl.BlockSpec((1, bf), lambda i: (0, i)),
            pl.BlockSpec((bf, d), lambda i: (i, 0)),
            pl.BlockSpec((1, d), lambda i: (0, 0)),
        ],
        out_specs=[
            whole,
            whole,
            pl.BlockSpec((1, d, bf), lambda i: (lax.div(i, per), 0, lax.rem(i, per))),
            pl.BlockSpec((bf, d), lambda i: (i, 0)),
            pl.BlockSpec((8, bf), lambda i: (0, i)),
        ],
        out_shape=[
            jax.ShapeDtypeStruct((rows, d), BF),
            jax.ShapeDtypeStruct((rows, d), F32),
            jax.ShapeDtypeStruct((ff // d, d, d), BF),
            jax.ShapeDtypeStruct((ff, d), BF),
            jax.ShapeDtypeStruct((8, ff), F32),
        ],
        scratch_shapes=[
            pltpu.VMEM((d, rows), BF),
            pltpu.VMEM((rows, d), F32),
            pltpu.VMEM((rows, d), F32),
        ],
        compiler_params=params(),
        cost_estimate=cost(12 * rows * d * ff, 8 * d * ff),
    )(h, g, r, w_in, b_in, w_out, b_out)


def norm(rows, gain, bias):
    mean = jnp.mean(rows, axis=-1, keepdims=True)
    centred = rows - mean
    spread_ = jnp.mean(centred * centred, axis=-1, keepdims=True)
    return centred * lax.rsqrt(spread_ + EPS) * gain + bias


def norm_back(rows, gain, grad):
    mean = jnp.mean(rows, axis=-1, keepdims=True)
    centred = rows - mean
    rstd = lax.rsqrt(jnp.mean(centred * centred, axis=-1, keepdims=True) + EPS)
    hat = centred * rstd
    scaled = grad * gain
    inner = jnp.mean(scaled * hat, axis=-1, keepdims=True)
    back = rstd * (scaled - jnp.mean(scaled, axis=-1, keepdims=True) - hat * inner)
    return back, jnp.sum(grad * hat, axis=0), jnp.sum(grad, axis=0)


class Links:
    def __init__(self, dp, tp):
        self.dp = dp
        self.bits = dp.bit_length() - 1
        self.me = lax.axis_index("dp")
        self.half = lax.axis_index("tp")
        self.swap = [(i, tp - 1 - i) for i in range(tp)]

    def other(self, x):
        return lax.ppermute(x, "tp", self.swap)

    def across(self, x, bit):
        return lax.ppermute(x, "dp", [(i, i ^ (1 << bit)) for i in range(self.dp)])

    def flag(self, bit):
        return (self.me >> bit) & 1

    def joined(self, mine, theirs, flag, axis=0):
        return jnp.where(
            flag == 0,
            jnp.concatenate([mine, theirs], axis=axis),
            jnp.concatenate([theirs, mine], axis=axis),
        )

    def fetch(self, w):
        rows = w.shape[0] // 4
        core, chip = self.flag(0), self.flag(1)
        part = lax.dynamic_slice_in_dim(w, (2 * core + chip) * rows, rows, 0)
        part = self.other(part)
        part = self.joined(part, self.across(part, 1), chip)
        return self.joined(part, self.across(part, 0), core)


class Chain:
    def __init__(self, rows, cols, order):
        self.rows, self.cols, self.order = rows, cols, order
        self.shapes, self.plan = [], []
        size, parts, split = rows, 2, []
        for step in order:
            if step == "tp":
                self.plan.append(("tp", None, size))
                self.shapes.append((1, size, cols))
                parts = 1
            elif (size // 2) % 16 == 0:
                size //= 2
                self.plan.append(("split", step, size))
                self.shapes.append((parts, size, cols))
                split.append((step, size))
            else:
                self.plan.append(("add", step, size))
                self.shapes.append((parts, size, cols))
        self.last = size
        self.back = list(reversed(split))
        self.count = len(self.plan) + len(self.back)

    def scratch(self):
        return [pltpu.VMEM((2, self.rows // 2, self.cols), BF)] + [
            pltpu.VMEM(shape, BF) for shape in self.shapes
        ]

    def bind(self, own, oth, out, acc, recv, send_sem, recv_sem, local_sem):
        self.own, self.oth, self.out, self.acc, self.recv = own, oth, out, acc, recv
        self.send_sem, self.recv_sem, self.local_sem = send_sem, recv_sem, local_sem
        me = lax.axis_index("dp")
        self.me = me
        flag = lambda bit: lax.rem(lax.div(me, 1 << bit), 2)
        self.flag = flag
        self.offsets, at = [], 0
        first = True
        for kind, bit, size in self.plan:
            self.offsets.append(at)
            if kind == "split" and not first:
                at = at + flag(bit) * size
            first = False
        self.at = at
        self.start_of = flag(self.order[0]) * (self.rows // 2)
        self.both = [True] * len(self.plan)
        seen = False
        for i, (kind, _, _) in enumerate(self.plan):
            self.both[i] = not seen
            seen = seen or kind == "tp"
        return self

    def partner(self, bit):
        return {"dp": self.me + (1 - 2 * self.flag(bit)) * (1 << bit)}

    def remote(self, src, dst, sem, where):
        return pltpu.make_async_remote_copy(
            src_ref=src,
            dst_ref=dst,
            send_sem=self.send_sem.at[sem],
            recv_sem=self.recv_sem.at[sem],
            device_id=where,
            device_id_type=pl.DeviceIdType.MESH,
        )

    def copies(self, i):
        n = len(self.plan)
        ds = lambda at, size: pl.ds(pl.multiple_of(at, 16), size)
        if i == 0:
            _, bit, size = self.plan[0]
            f = self.flag(bit)
            keep, send = ds(f * size, size), ds((1 - f) * size, size)
            where = self.partner(bit)
            return [
                self.remote(self.own.at[send], self.recv[0].at[0], 0, where),
                self.remote(self.oth.at[send], self.recv[0].at[1], self.count, where),
            ], [
                pltpu.make_async_copy(self.own.at[keep], self.acc.at[0], self.local_sem.at[0]),
                pltpu.make_async_copy(self.oth.at[keep], self.acc.at[1], self.local_sem.at[1]),
            ]
        if i < n:
            kind, bit, size = self.plan[i]
            at = self.offsets[i]
            if kind == "tp":
                where = {"tp": 1 - lax.axis_index("tp")}
                return [self.remote(self.acc.at[1, ds(at, size)], self.recv[i].at[0], i, where)], []
            if kind == "split":
                at = at + (1 - self.flag(bit)) * size
            src = self.acc.at[:, ds(at, size)] if self.both[i] else self.acc.at[0:1, ds(at, size)]
            return [self.remote(src, self.recv[i], i, self.partner(bit))], []
        k = i - n
        here = self.start_of + self.at
        mine = self.acc.at[0, ds(self.at, self.last)]
        if k == 0:
            dst = self.out.at[ds(here, self.last)]
            return [self.remote(mine, dst, i, self.partner(self.back[0][0]))], [
                pltpu.make_async_copy(mine, dst, self.local_sem.at[2])
            ]
        for bit, size in self.back[:k]:
            here = here - self.flag(bit) * size
        size = 2 * self.back[k - 1][1]
        region = self.out.at[ds(here, size)]
        return [self.remote(region, region, i, self.partner(self.back[k][0]))], []

    def start(self, i):
        remote, local = self.copies(i)
        for copy in remote + local:
            copy.start()

    def finish(self, i):
        remote, local = self.copies(i)
        for copy in remote + local:
            copy.wait()
        if i >= len(self.plan):
            return
        kind, bit, size = self.plan[i]
        at = self.offsets[i]
        if kind == "split" and i:
            at = at + self.flag(bit) * size
        parts = self.shapes[i][0]
        acc, recv = self.acc, self.recv[i]
        rows = next(r for r in (96, 48, 32, 16) if size % r == 0)

        def body(j, carry):
            to = pl.ds(pl.multiple_of(at + j * rows, 16), rows)
            fr = pl.ds(pl.multiple_of(j * rows, 16), rows)
            for part in range(parts):
                acc[part, to, :] = acc[part, to, :] + recv[part, fr, :]
            return carry

        lax.fori_loop(0, size // rows, body, 0)


def greet(bits):
    me = lax.axis_index("dp")
    barrier = pltpu.get_barrier_semaphore()
    for bit in range(bits):
        to = me + (1 - 2 * lax.rem(lax.div(me, 1 << bit), 2)) * (1 << bit)
        pl.semaphore_signal(
            barrier, inc=1, device_id={"dp": to}, device_id_type=pl.DeviceIdType.MESH
        )
    pl.semaphore_signal(
        barrier,
        inc=1,
        device_id={"tp": 1 - lax.axis_index("tp")},
        device_id_type=pl.DeviceIdType.MESH,
    )
    pl.semaphore_wait(barrier, bits + 1)


def reduce_kernel(chains, bits, *refs):
    n = len(chains)
    ins, outs, rest = refs[: 2 * n], refs[2 * n : 3 * n], list(refs[3 * n :])
    send_sem, recv_sem, local_sem = rest[-3:]
    for c, chain in enumerate(chains):
        size = 1 + len(chain.plan)
        acc, *recv = rest[:size]
        rest = rest[size:]
        chain.bind(
            ins[2 * c], ins[2 * c + 1], outs[c], acc, recv,
            send_sem.at[c], recv_sem.at[c], local_sem.at[c],
        )
    greet(bits)
    for chain in chains:
        chain.start(0)
    for i in range(max(c.count for c in chains)):
        for chain in chains:
            if i < chain.count:
                chain.finish(i)
                if i + 1 < chain.count:
                    chain.start(i + 1)


def reduce_all(grads, dp, orders):
    bits = dp.bit_length() - 1
    chains = [Chain(g[0].shape[0], g[0].shape[1], o) for g, o in zip(grads, orders)]
    most = max(c.count for c in chains) + 1
    flat = [x for g in grads for x in g]
    anywhere = pl.BlockSpec(memory_space=pl.ANY)
    return pl.pallas_call(
        functools.partial(reduce_kernel, chains, bits),
        in_specs=[anywhere] * len(flat),
        out_specs=[anywhere] * len(grads),
        out_shape=[jax.ShapeDtypeStruct(g[0].shape, BF) for g in grads],
        scratch_shapes=[s for c in chains for s in c.scratch()]
        + [
            pltpu.SemaphoreType.DMA((len(chains), most)),
            pltpu.SemaphoreType.DMA((len(chains), most)),
            pltpu.SemaphoreType.DMA((len(chains), 3)),
        ],
        compiler_params=pltpu.CompilerParams(
            collective_id=0, has_side_effects=True, vmem_limit_bytes=VMEM_LIMIT
        ),
        cost_estimate=cost(0, sum(2 * x.size for x in flat)),
    )(*flat)


def shift_earlier(x):
    pad = jnp.zeros((SPAN - 1, x.shape[1]), x.dtype)
    return jnp.concatenate([x[SPAN - 1 :], pad], axis=0)


def shift_later(x):
    pad = jnp.zeros((SPAN - 1, x.shape[1]), x.dtype)
    return jnp.concatenate([pad, x[: x.shape[0] - SPAN + 1]], axis=0)


def on_device(
    tokens, neighbours, nbr_index, lengths, w_qkv, qv_bias, w_out, cross_q, cross_kv,
    cross_bias, cross_out, out_bias, ln_gain, ln_bias, fc_in, fc_in_bias, fc_out,
    fc_out_bias, cotangent,
):
    tp = lax.axis_size("tp")
    link = Links(lax.axis_size("dp"), tp)
    half = link.half
    d = tokens.shape[1]
    hc = w_qkv.shape[2]
    spans = nbr_index.shape[1] // tp
    length = lax.dynamic_slice_in_dim(lengths[0], half, 1)

    small = jnp.concatenate(
        [x.reshape(-1) for x in (fc_in_bias, fc_out_bias, out_bias, ln_gain, ln_bias, qv_bias, cross_bias)]
    ).reshape(-1, 128)
    small_oth = link.other(small).reshape(-1)
    small = small.reshape(-1)
    ffh = fc_in_bias.shape[0]

    def whole(at, count, width, natural=True):
        a = small[at : at + count * width].reshape(count, width)
        b = small_oth[at : at + count * width].reshape(count, width)
        if natural:
            return link.joined(a, b, half, 1).astype(F32), at + count * width
        return (a.astype(F32), b.astype(F32)), at + count * width

    b_in, at = whole(0, 1, ffh)
    b_out, at = whole(at, 1, hc)
    out_b, at = whole(at, 2, hc)
    gains, at = whole(at, 3, hc)
    shifts, at = whole(at, 3, hc)
    qv_b, at = whole(at, 2, hc, False)
    cross_b, at = whole(at, 2, hc, False)

    qkv_own = w_qkv.reshape(d, 3 * hc)
    qkv_oth = link.fetch(qkv_own)
    wo = jnp.concatenate([w_out, link.fetch(w_out)], axis=0)
    cq_w = jnp.concatenate([cross_q, link.fetch(cross_q)], axis=1)
    kv_own = cross_kv.reshape(d, 2 * hc)
    kv_oth = link.fetch(kv_own)
    kv_w = jnp.concatenate([kv_own[:, :hc], kv_oth[:, :hc], kv_own[:, hc:], kv_oth[:, hc:]], axis=1)
    co_w = jnp.concatenate([cross_out, link.fetch(cross_out)], axis=0)
    fin = link.joined(fc_in, link.fetch(fc_in), half)
    fout = link.joined(fc_out, link.fetch(fc_out), half)

    order = nbr_index[0]
    keep = lax.dynamic_slice_in_dim(order, half * spans, spans)
    send = lax.dynamic_slice_in_dim(order, (1 - half) * spans, spans)
    nbr_own, nbr_send = pick_blocks(neighbours, keep, send)
    nbr_oth = link.other(nbr_send)
    nbr_own = nbr_own.reshape(-1, d)
    nbr_oth = nbr_oth.reshape(-1, d)

    tok = tokens.astype(F32)
    h1 = norm(tok, gains[0], shifts[0]).astype(BF)

    def project(w, which):
        bias = jnp.concatenate([qv_b[which][0], jnp.zeros((hc,), F32), qv_b[which][1]])
        return (mm(h1, w) + bias).astype(BF)

    p_own = project(qkv_own, 0)
    ctx_own, lse_own = self_fwd(p_own, length)
    p_oth = project(qkv_oth, 1)
    ctx_oth, lse_oth = self_fwd(p_oth, length)
    ctx = jnp.concatenate([ctx_own, ctx_oth], axis=1)
    r1 = tok + mm(ctx, wo) + out_b[0]
    h2 = norm(r1, gains[1], shifts[1]).astype(BF)
    cb = [jnp.concatenate([cross_b[0][i], cross_b[1][i]]) for i in range(2)]
    cq = shift_earlier((mm(h2, cq_w) + cb[0]).astype(BF))
    kv_b = jnp.concatenate([jnp.zeros((d,), F32), cb[1]])
    ckv_own = (mm(nbr_own, kv_w) + kv_b).astype(BF)
    ckv_oth = (mm(nbr_oth, kv_w) + kv_b).astype(BF)
    cctx = shift_later(cross_fwd(cq, ckv_own, ckv_oth))
    r2 = r1 + mm(cctx, co_w) + out_b[1]
    h3 = norm(r2, gains[2], shifts[2]).astype(BF)
    block_out, d_h3, g_in, g_out, g_bin = feed(h3, cotangent, r2, fin, b_in, fout, b_out)

    cot = cotangent.astype(F32)
    split = lambda x: [
        lax.dynamic_slice_in_dim(x, at * (x.shape[-2] // tp), x.shape[-2] // tp, x.ndim - 2).reshape(-1, d)
        for at in (half, 1 - half)
    ]
    back3, gain3, shift3 = norm_back(r2, gains[2], d_h3)
    d_r2 = cot + back3
    z2 = d_r2.astype(BF)
    e = mm(z2, co_w, NT).astype(BF)
    g_co = mm(cctx, z2, TN).astype(BF)
    d_cq, d_own, d_oth = cross_bwd(cq, ckv_own, ckv_oth, shift_earlier(e))
    d_cq = shift_later(d_cq)
    n_oth = mm(d_oth, kv_w, NT).astype(BF).reshape(spans, -1, d)
    n_back = link.other(n_oth)
    n_own = mm(d_own, kv_w, NT).reshape(spans, -1, d)
    nbr_grad = place_blocks(jnp.concatenate([keep, send]), n_own, n_back)
    g_kv = (mm(nbr_own, d_own, TN) + mm(nbr_oth, d_oth, TN)).astype(BF)
    g_cq = mm(h2, d_cq, TN).astype(BF)
    back2, gain2, shift2 = norm_back(r1, gains[1], mm(d_cq, cq_w, NT))
    d_r1 = d_r2 + back2
    z1 = d_r1.astype(BF)
    f = mm(z1, wo, NT).astype(BF)
    g_wo = mm(ctx, z1, TN).astype(BF)
    dq_own = self_bwd(p_own, f[:, :hc], ctx_own, lse_own, length)
    dq_oth = self_bwd(p_oth, f[:, hc:], ctx_oth, lse_oth, length)
    flat = lambda x: jnp.concatenate([x[0], x[1], x[2]], axis=1)
    dq_own_f, dq_oth_f = flat(dq_own), flat(dq_oth)
    g_qkv = [
        jnp.concatenate([mm(h1, part[i], TN).astype(BF) for i in range(3)], axis=0)
        for part in (dq_own, dq_oth)
    ]
    sides = (slice(0, hc), slice(hc, d))
    g_kvs = [jnp.concatenate([g_kv[:, s], g_kv[:, d:][:, s]], axis=0) for s in sides]
    g_rest = [
        jnp.concatenate(
            [g_cq[:, s], g_wo[s][:, :hc], g_wo[s][:, hc:], g_co[s][:, :hc], g_co[s][:, hc:]], axis=0
        )
        for s in sides
    ]
    others = list(range(2, link.bits))
    x_first = [0, 1] + others + ["tp"]
    z_first = [0] + others + [1, "tp"]
    y_first = [0, "tp", 1] + others
    s_in, s_out, s_qkv, s_kv, s_rest = reduce_all(
        [split(g_in), split(g_out), g_qkv, g_kvs, g_rest],
        link.dp,
        [x_first, z_first, y_first, z_first, x_first],
    )
    wide_rows = lambda x, n: jnp.concatenate(
        [x[i * (x.shape[0] // n) : (i + 1) * (x.shape[0] // n)] for i in range(n)], axis=1
    ).astype(F32)
    fc_in_grad = wide_rows(s_in, s_in.shape[0] // hc)
    fc_out_grad = s_out.astype(F32)
    qkv_grad = wide_rows(s_qkv, 3).reshape(d, 3, hc)
    cross_kv_grad = wide_rows(s_kv, 2).reshape(d, 2, hc)
    cross_q_grad = s_rest[:d].astype(F32)
    wo_grad = wide_rows(s_rest[d : 2 * d], 2)
    co_grad = wide_rows(s_rest[2 * d :], 2)
    d_h1 = mm(dq_own_f, qkv_own, NT) + mm(dq_oth_f, qkv_oth, NT)
    back1, gain1, shift1 = norm_back(tok, gains[0], d_h1)
    tokens_grad = d_r1 + back1

    wide = lambda x: jnp.sum(x.astype(F32), axis=0)
    natural = [
        g_bin[0],
        wide(cot),
        wide(d_r1),
        wide(d_r2),
        gain1,
        gain2,
        gain3,
        shift1,
        shift2,
        shift3,
    ]
    relative = [wide(dq_own[0]), wide(dq_oth[0]), wide(dq_own[2]), wide(dq_oth[2])]
    cqs, cvs = wide(d_cq), wide(d_own[:, d:]) + wide(d_oth[:, d:])
    relative += [cqs[:hc], cqs[hc:], cvs[:hc], cvs[hc:]]
    for i in range(0, len(relative), 2):
        natural.append(link.joined(relative[i], relative[i + 1], half))
    sums = lax.psum(jnp.concatenate(natural).reshape(-1, 128), ("dp", "tp")).reshape(-1)
    ff = ffh * tp
    gb_in = lax.dynamic_slice_in_dim(sums[:ff], half * ffh, ffh)
    rest = lax.dynamic_slice_in_dim(sums[ff:].reshape(-1, d), half * hc, hc, 1)
    return (
        block_out,
        tokens_grad,
        nbr_grad,
        qkv_grad,
        rest[9:11],
        wo_grad,
        cross_q_grad,
        cross_kv_grad,
        rest[11:13],
        co_grad,
        rest[1:3],
        rest[3:6],
        rest[6:9],
        fc_in_grad,
        gb_in,
        fc_out_grad,
        rest[0],
    )


def solution(mesh):
    return jax.shard_map(
        on_device,
        mesh=mesh,
        in_specs=(
            P(("dp", "tp"), None),
            P("dp", "tp", None),
            P("dp", None),
            P("dp", None),
            P(None, None, "tp"),
            P(None, "tp"),
            P("tp", None),
            P(None, "tp"),
            P(None, None, "tp"),
            P(None, "tp"),
            P("tp", None),
            P(None, "tp"),
            P(None, "tp"),
            P(None, "tp"),
            P("tp", None),
            P("tp"),
            P("tp", None),
            P("tp"),
            P(("dp", "tp"), None),
        ),
        out_specs=(
            P(("dp", "tp"), None),
            P(("dp", "tp"), None),
            P("dp", "tp", None),
            P(None, None, "tp"),
            P(None, "tp"),
            P("tp", None),
            P(None, "tp"),
            P(None, None, "tp"),
            P(None, "tp"),
            P("tp", None),
            P(None, "tp"),
            P(None, "tp"),
            P(None, "tp"),
            P("tp", None),
            P("tp"),
            P("tp", None),
            P("tp"),
        ),
        check_vma=False,
    )
```

```python
import functools

import jax
import jax.numpy as jnp
from jax import lax
from jax.experimental import pallas as pl
from jax.experimental.pallas import tpu as pltpu
from jax.sharding import PartitionSpec as P

HEAD = 64
SPAN = 64
LEN = 1024
NBR = 256
EPS = 1e-05
BF = jnp.bfloat16
F32 = jnp.float32
DEAD = -1e30
LN2 = 0.6931471805599453
SCORE = 0.125 / LN2
VMEM_LIMIT = 60 * 1024 * 1024

NN = (((1,), (0,)), ((), ()))
NT = (((1,), (1,)), ((), ()))
TN = (((0,), (0,)), ((), ()))


def mm(a, b, dims=NN):
    return lax.dot_general(a, b, dims, preferred_element_type=F32)


def iota(shape, dim):
    return lax.broadcasted_iota(jnp.int32, shape, dim)


def cost(flops, nbytes, exps=0):
    return pl.CostEstimate(flops=flops, bytes_accessed=nbytes, transcendentals=exps)


def params(n=1):
    return pltpu.CompilerParams(
        dimension_semantics=("arbitrary",) * n, vmem_limit_bytes=VMEM_LIMIT
    )


def three(x):
    hi = x.astype(BF)
    rest = x - hi.astype(F32)
    mid = rest.astype(BF)
    return hi.astype(F32), mid.astype(F32), rest - mid.astype(F32)


def self_fwd_kernel(len_ref, q_ref, k_ref, v_ref, o_ref, lse_ref):
    bq = 512
    length = len_ref[0]
    low = iota((LEN, 128), 1) < HEAD
    lane = iota((LEN, 128), 1)
    q, k, v = (ref[...] for ref in (q_ref, k_ref, v_ref))
    one = jnp.ones((LEN, 128), BF)
    zero = jnp.zeros((LEN, 128), BF)
    dead = jnp.where(iota((LEN, 128), 0) < length, 0.0, DEAD).astype(BF)
    at = lambda x, first: jnp.where(lane == first, x, zero)
    qs = (jnp.where(low, q, at(one, HEAD)), jnp.where(low, at(one, 0), q))
    ks = (jnp.where(low, k, at(dead, HEAD)), jnp.where(low, at(dead, 0), k))
    vs = (jnp.where(low, v, one), jnp.where(low, one, v))
    tri = iota((bq, bq), 1) <= iota((bq, bq), 0)
    low_q = low[:bq]
    for i in range(LEN // bq):
        lo, hi = i * bq, (i + 1) * bq
        outs, tops = [], []
        for h in range(2):
            here = jnp.where(tri, mm(qs[h][lo:hi], ks[h][lo:hi], NT), DEAD)
            m = jnp.max(here, axis=1, keepdims=True)
            if i:
                left = mm(qs[h][lo:hi], ks[h][:lo], NT)
                m = jnp.maximum(m, jnp.max(left, axis=1, keepdims=True))
            o = mm(jnp.exp2(here - m).astype(BF), vs[h][lo:hi])
            if i:
                o += mm(jnp.exp2(left - m).astype(BF), vs[h][:lo])
            outs.append(o)
            tops.append(m)
        a, b = outs
        o_ref[lo:hi, :] = (jnp.where(low_q, a, b) / pltpu.roll(jnp.where(low_q, b, a), HEAD, 1)).astype(BF)
        lse_ref[lo:hi, :] = jnp.where(low_q, tops[1], tops[0]) + jnp.log2(jnp.where(low_q, b, a))


def self_fwd(qkv, length):
    pairs = qkv.shape[1] // 3 // 128
    block = lambda part: pl.BlockSpec((LEN, 128), lambda i, n: (0, part * pairs + i))
    return pl.pallas_call(
        self_fwd_kernel,
        grid_spec=pltpu.PrefetchScalarGridSpec(
            num_scalar_prefetch=1,
            grid=(pairs,),
            in_specs=[block(0), block(1), block(2)],
            out_specs=[block(0), block(0)],
        ),
        out_shape=[
            jax.ShapeDtypeStruct((LEN, pairs * 128), BF),
            jax.ShapeDtypeStruct((LEN, pairs * 128), F32),
        ],
        compiler_params=params(),
        cost_estimate=cost(pairs * 2 * 4 * LEN * LEN * 128, pairs * 8 * LEN * 128),
    )(length, qkv, qkv, qkv)


def self_bwd_kernel(len_ref, q_ref, k_ref, v_ref, f_ref, o_ref, lse_ref, d_ref, dq_ref):
    bk = 256
    length = len_ref[0]
    lane = iota((LEN, 128), 1)
    low = lane < HEAD
    q, k, v, f = (ref[...] for ref in (q_ref, k_ref, v_ref, f_ref))
    zero = jnp.zeros((LEN, 128), BF)
    place = lax.rem(lane, HEAD)
    prod = f.astype(F32) * o_ref[...].astype(F32)
    crossed = jnp.where((iota((128, 128), 0) < HEAD) == (iota((128, 128), 1) < HEAD), 0.0, 1.0).astype(BF)
    prod_hi = prod.astype(BF)
    delta = mm(prod_hi, crossed) + mm((prod - prod_hi.astype(F32)).astype(BF), crossed)

    def free(x, last):
        hi, mid, rest = three(-x)
        out = jnp.where(place == 0, hi, jnp.where(place == 1, mid, jnp.where(place == 2, rest, last)))
        return out.astype(BF)

    q_free = free(lse_ref[...], jnp.where(place == 3, 1.0, 0.0))
    f_free = free(delta, jnp.zeros((LEN, 128), F32))
    dead = jnp.where(iota((LEN, 128), 0) < length, 0.0, DEAD)
    ones = jnp.where(place < 3, 1.0, 0.0)
    k_free = jnp.where(place == 3, dead, ones).astype(BF)
    v_free = ones.astype(BF)
    pick = lambda x, y: (jnp.where(low, x, y), jnp.where(low, y, x))
    qx, fx, kx, vx = pick(q, q_free), pick(f, f_free), pick(k, k_free), pick(v, v_free)
    qs, fs, ks = pick(q, zero), pick(f, zero), pick(k, zero)
    tri = iota((bk, bk), 0) <= iota((bk, bk), 1)
    for j in range(LEN // bk):
        lo, hi = j * bk, (j + 1) * bk
        ps, dss = [], []
        for h in range(2):
            p = jnp.exp2(mm(kx[h][lo:hi], qx[h][lo:], NT))
            first = jnp.where(tri, p[:, :bk], 0.0)
            p = jnp.concatenate([first, p[:, bk:]], axis=1) if hi < LEN else first
            ds = (p * mm(vx[h][lo:hi], fx[h][lo:], NT)).astype(BF)
            ps.append(p.astype(BF))
            dss.append(ds)
        dv = mm(jnp.concatenate(ps, axis=1), jnp.concatenate([fs[0][lo:], fs[1][lo:]], axis=0))
        dk = mm(jnp.concatenate(dss, axis=1), jnp.concatenate([qs[0][lo:], qs[1][lo:]], axis=0))
        kk = jnp.concatenate([ks[0][lo:hi], ks[1][lo:hi]], axis=0)
        part = mm(jnp.concatenate(dss, axis=0), kk, TN)
        if j:
            dq_ref[lo:, :] += part
        else:
            dq_ref[...] = part
        d_ref[1, lo:hi, :] = (dk * LN2).astype(BF)
        d_ref[2, lo:hi, :] = dv.astype(BF)
    d_ref[0] = (dq_ref[...] * 0.125).astype(BF)


def self_bwd(qkv, back, ctx, lse, length):
    pairs = qkv.shape[1] // 3 // 128
    block = lambda part: pl.BlockSpec((LEN, 128), lambda i, n: (0, part * pairs + i))
    return pl.pallas_call(
        self_bwd_kernel,
        grid_spec=pltpu.PrefetchScalarGridSpec(
            num_scalar_prefetch=1,
            grid=(pairs,),
            in_specs=[block(0), block(1), block(2), block(0), block(0), block(0)],
            out_specs=pl.BlockSpec((3, LEN, 128), lambda i, n: (0, 0, i)),
            scratch_shapes=[pltpu.VMEM((LEN, 128), F32)],
        ),
        out_shape=jax.ShapeDtypeStruct((3, LEN, pairs * 128), BF),
        compiler_params=params(),
        cost_estimate=cost(pairs * 2 * 10 * LEN * LEN * 128, pairs * 16 * LEN * 128),
    )(length, qkv, qkv, qkv, back, ctx, lse)


PER_STEP = 4


def own_heads():
    return jnp.where(iota((256, 256), 0) // SPAN == iota((256, 256), 1) // HEAD, 1.0, 0.0).astype(BF)


def spread(rows, mask):
    return jnp.concatenate([rows] * 4, axis=0) * mask


def gathered(rows, lanes):
    out = jnp.where(lanes == 0, rows[:SPAN], 0.0)
    for g in range(1, 4):
        out = jnp.where(lanes == g, rows[g * SPAN : (g + 1) * SPAN], out)
    return out


def fours(count, width, rows):
    for u in range(count):
        for t in range(width // 256):
            yield slice(u * SPAN, (u + 1) * SPAN), slice(u * rows, (u + 1) * rows), t * 256


def cross_fwd_kernel(q_ref, own_ref, oth_ref, o_ref):
    width = q_ref.shape[1]
    rows = own_ref.shape[0] // PER_STEP
    mask = own_heads()
    lanes = iota((SPAN, 256), 1) // HEAD
    one = jnp.ones((2 * rows, 128), BF)
    both = lambda at, lo: jnp.concatenate(
        [own_ref[at, lo : lo + 256], oth_ref[at, lo : lo + 256]], axis=0
    )
    jobs = list(fours(PER_STEP, width, rows))
    scores = [mm(spread(q_ref[q, lo : lo + 256], mask), both(kv, lo), NT) for q, kv, lo in jobs]
    probs = [jnp.exp2(s - jnp.max(s, axis=1, keepdims=True)).astype(BF) for s in scores]
    for p, (q, kv, lo) in zip(probs, jobs):
        o = mm(p, both(kv, width + lo))
        total = 1.0 / mm(p, one)
        o = o * jnp.concatenate([total, total], axis=1)
        o_ref[q, lo : lo + 256] = gathered(o, lanes).astype(BF)


def cross_fwd(q, own, oth):
    width = q.shape[1]
    spans = q.shape[0] // SPAN
    rows = own.shape[0] // spans
    row = pl.BlockSpec((PER_STEP * SPAN, width), lambda i: (i, 0))
    kv = pl.BlockSpec((PER_STEP * rows, 2 * width), lambda i: (i, 0))
    return pl.pallas_call(
        cross_fwd_kernel,
        grid=(spans // PER_STEP,),
        in_specs=[row, kv, kv],
        out_specs=row,
        out_shape=jax.ShapeDtypeStruct(q.shape, BF),
        compiler_params=params(),
        cost_estimate=cost(spans * 3 * 4 * 256**3, spans * 1000000),
    )(q, own, oth)


def cross_bwd_kernel(q_ref, own_ref, oth_a_ref, oth_b_ref, e_ref, dq_ref, down_ref, doth_ref):
    width = q_ref.shape[1]
    rows = own_ref.shape[0] // PER_STEP
    early = pl.program_id(0) < pl.num_programs(0) // 2
    oth = jnp.where(early, oth_a_ref[...], oth_b_ref[...])
    mask = own_heads()
    lanes = iota((SPAN, 256), 1) // HEAD
    both = lambda at, lo: jnp.concatenate([own_ref[at, lo : lo + 256], oth[at, lo : lo + 256]], axis=0)
    jobs = list(fours(PER_STEP, width, rows))
    q4 = [spread(q_ref[q, lo : lo + 256], mask) for q, kv, lo in jobs]
    e4 = [spread(e_ref[q, lo : lo + 256], mask) for q, kv, lo in jobs]
    scores = [mm(both(kv, lo), x, NT) for x, (q, kv, lo) in zip(q4, jobs)]
    backs = [mm(both(kv, width + lo), x, NT) for x, (q, kv, lo) in zip(e4, jobs)]
    for s, dp, x, y, (q, kv, lo) in zip(scores, backs, q4, e4, jobs):
        p = jnp.exp2(s - jnp.max(s, axis=0, keepdims=True))
        p = p * (1.0 / jnp.sum(p, axis=0, keepdims=True))
        delta = jnp.sum(p * dp, axis=0, keepdims=True)
        ds = (p * (dp - delta)).astype(BF)
        dk = (mm(ds, x) * LN2).astype(BF)
        dv = mm(p.astype(BF), y).astype(BF)
        down_ref[kv, lo : lo + 256] = dk[:rows]
        doth_ref[kv, lo : lo + 256] = dk[rows:]
        down_ref[kv, width + lo : width + lo + 256] = dv[:rows]
        doth_ref[kv, width + lo : width + lo + 256] = dv[rows:]
        dq_ref[q, lo : lo + 256] = (gathered(mm(ds, both(kv, lo), TN), lanes) * 0.125).astype(BF)


def cross_bwd(q, own, oth_a, oth_b, e):
    width = q.shape[1]
    spans = q.shape[0] // SPAN
    rows = own.shape[0] // spans
    steps = spans // PER_STEP
    row = pl.BlockSpec((PER_STEP * SPAN, width), lambda i: (i, 0))
    shape = (PER_STEP * rows, 2 * width)
    kv = pl.BlockSpec(shape, lambda i: (i, 0))
    return pl.pallas_call(
        cross_bwd_kernel,
        grid=(steps,),
        in_specs=[
            row,
            kv,
            pl.BlockSpec(shape, lambda i: (jnp.minimum(i, steps // 2 - 1), 0)),
            pl.BlockSpec(shape, lambda i: (jnp.maximum(i - steps // 2, 0), 0)),
            row,
        ],
        out_specs=[row, kv, kv],
        out_shape=[
            jax.ShapeDtypeStruct(q.shape, BF),
            jax.ShapeDtypeStruct(own.shape, BF),
            jax.ShapeDtypeStruct(own.shape, BF),
        ],
        compiler_params=params(),
        cost_estimate=cost(spans * 3 * 10 * 256**3, spans * 2000000),
    )(q, own, oth_a, oth_b, e)


def pick_kernel(keep_ref, send_ref, blocks_ref, keep_out, send_out, sems):
    count = keep_out.shape[0]
    copies = []
    for i in range(count):
        copies.append(
            pltpu.make_async_copy(blocks_ref.at[send_ref[i]], send_out.at[i], sems.at[0, i])
        )
    for i in range(count):
        copies.append(
            pltpu.make_async_copy(blocks_ref.at[keep_ref[i]], keep_out.at[i], sems.at[1, i])
        )
    for copy in copies:
        copy.start()
    for copy in copies:
        copy.wait()


def pick_blocks(neighbours, keep, send):
    count = keep.shape[0]
    smem = pl.BlockSpec(memory_space=pltpu.SMEM)
    anywhere = pl.BlockSpec(memory_space=pl.ANY)
    vmem = pl.BlockSpec(memory_space=pltpu.VMEM)
    return pl.pallas_call(
        pick_kernel,
        in_specs=[smem, smem, anywhere],
        out_specs=[vmem, vmem],
        out_shape=[jax.ShapeDtypeStruct((count,) + neighbours.shape[1:], BF)] * 2,
        scratch_shapes=[pltpu.SemaphoreType.DMA((2, count))],
        compiler_params=pltpu.CompilerParams(vmem_limit_bytes=VMEM_LIMIT),
        cost_estimate=cost(0, 4 * neighbours.size),
    )(keep, send, neighbours)


def pack_kernel(where_ref, qkv, kv, cq, wo, co, fin, fout, first, second, third, sems):
    core, p = where_ref[0], where_ref[1]
    d, hc = cq.shape
    e8, w8, o8 = d // 8, wo.shape[0] // 8, fout.shape[0] // 8
    take = lambda at, n: pl.ds(pl.multiple_of(at * n, 16), n)
    jobs = [(qkv.at[take(core, d // 2)], first)]
    to = 0
    for ref, count, n in ((kv, 2, e8), (cq, 1, e8), (wo, 2, w8), (co, 2, w8)):
        for i in range(count):
            jobs.append((ref.at[take(p, n), pl.ds(i * hc, hc)], second.at[pl.ds(to, n)]))
            to += n
    to = 0
    for i in range(fin.shape[1] // d):
        jobs.append((fin.at[take(p, w8), pl.ds(i * d, d)], third.at[pl.ds(to, w8)]))
        to += w8
    jobs.append((fout.at[take(p, o8)], third.at[pl.ds(to, o8)]))
    copies = [pltpu.make_async_copy(a, b, sems.at[i]) for i, (a, b) in enumerate(jobs)]
    for copy in copies:
        copy.start()
    for copy in copies:
        copy.wait()


def pack_weights(where, qkv, kv, cq, wo, co, fin, fout):
    anywhere = pl.BlockSpec(memory_space=pl.ANY)
    vmem = pl.BlockSpec(memory_space=pltpu.VMEM)
    d, hc = cq.shape
    n_in = fin.shape[1] // d
    return pl.pallas_call(
        pack_kernel,
        in_specs=[pl.BlockSpec(memory_space=pltpu.SMEM)] + [anywhere] * 7,
        out_specs=[vmem, vmem, vmem],
        out_shape=[
            jax.ShapeDtypeStruct((d // 2, 3 * hc), BF),
            jax.ShapeDtypeStruct((3 * (d // 8) + 4 * (wo.shape[0] // 8), hc), BF),
            jax.ShapeDtypeStruct((n_in * (fin.shape[0] // 8) + fout.shape[0] // 8, d), BF),
        ],
        scratch_shapes=[pltpu.SemaphoreType.DMA((9 + n_in,))],
        compiler_params=pltpu.CompilerParams(vmem_limit_bytes=VMEM_LIMIT),
        cost_estimate=cost(0, 4 * 1024 * 1024),
    )(where, qkv, kv, cq, wo, co, fin, fout)


def place_kernel(order_ref, mine_ref, theirs_ref, out_ref, wide, sems):
    count = mine_ref.shape[0]
    copies = []
    for i in range(count):
        copy = pltpu.make_async_copy(mine_ref.at[i], out_ref.at[order_ref[i]], sems.at[i])
        copy.start()
        copies.append(copy)
    for i in range(count):
        wide[i] = theirs_ref[i].astype(F32)
        copy = pltpu.make_async_copy(
            wide.at[i], out_ref.at[order_ref[count + i]], sems.at[count + i]
        )
        copy.start()
        copies.append(copy)
    for copy in copies:
        copy.wait()


def place_blocks(order, mine, theirs):
    count = order.shape[0]
    return pl.pallas_call(
        place_kernel,
        in_specs=[
            pl.BlockSpec(memory_space=pltpu.SMEM),
            pl.BlockSpec(memory_space=pltpu.VMEM),
            pl.BlockSpec(memory_space=pltpu.VMEM),
        ],
        out_specs=pl.BlockSpec(memory_space=pl.ANY),
        out_shape=jax.ShapeDtypeStruct((count,) + mine.shape[1:], F32),
        scratch_shapes=[
            pltpu.VMEM(mine.shape, F32),
            pltpu.SemaphoreType.DMA((count,)),
        ],
        compiler_params=pltpu.CompilerParams(vmem_limit_bytes=VMEM_LIMIT),
        cost_estimate=cost(0, 8 * mine.size),
    )(order, mine, theirs)


GELU_A = 0.7978845608028654
GELU_B = 0.044715


def feed_kernel(
    half_ref, h_ref, g_ref, r_ref, aa_ref, ab_ref, ba_ref, bb_ref, bina_ref, binb_ref,
    wouta_ref, woutb_ref, bout_ref,
    out_ref, dh_ref, keep_ref, send_ref, gbina_ref, gbinb_ref, h_t, acc, dacc, act_s, dpre_s,
):
    step = pl.program_id(0)
    hc = aa_ref.shape[0]
    bf = aa_ref.shape[1]

    @pl.when(step == 0)
    def _():
        h_t[...] = h_ref[...].T

    win = jnp.concatenate(
        [
            jnp.concatenate([aa_ref[...], ab_ref[...]], axis=1),
            jnp.concatenate([ba_ref[...], bb_ref[...]], axis=1),
        ],
        axis=0,
    )
    here = half_ref[0] == 0
    wa, wb = wouta_ref[...], woutb_ref[...]
    wout = jnp.concatenate([jnp.where(here, wa, wb), jnp.where(here, wb, wa)], axis=0)
    bias = jnp.concatenate([bina_ref[...], binb_ref[...]], axis=1)
    rows = h_ref.shape[0]
    first = step == 0
    total = jnp.zeros(bias.shape, F32)
    for lo in range(0, rows, 256):
        at = slice(lo, lo + 256)
        pre = mm(h_ref[at], win) + bias
        dact = mm(g_ref[at], wout, NT)
        square = pre * pre
        th = jnp.tanh(pre * (GELU_A + GELU_A * GELU_B * square))
        half = 0.5 + 0.5 * th
        act = (pre * half).astype(BF)
        slope = half + pre * (half - half * th) * (GELU_A + 3.0 * GELU_A * GELU_B * square)
        dpre = (dact * slope).astype(BF)
        total += jnp.sum(dpre.astype(F32), axis=0, keepdims=True)
        act_s[at] = act
        dpre_s[at] = dpre
        acc[at] = jnp.where(first, 0.0, acc[at]) + mm(act, wout)
        dacc[at] = jnp.where(first, 0.0, dacc[at]) + mm(dpre, win, NT)
    gbina_ref[0:1, :] = total[:, :bf]
    gbinb_ref[0:1, :] = total[:, bf:]
    gout = mm(act_s[...], g_ref[...], TN).astype(BF)
    gin = mm(h_t[...], dpre_s[...]).astype(BF)

    def put(into_in, into_out):
        into_in[0], into_in[1] = gin[:hc], gin[hc:]
        into_out[0] = jnp.where(here, gout[:bf], gout[bf:])
        into_out[1] = jnp.where(here, gout[bf:], gout[:bf])

    @pl.when(half_ref[1] == 0)
    def _():
        put(keep_ref, send_ref)

    @pl.when(half_ref[1] != 0)
    def _():
        put(send_ref, keep_ref)

    @pl.when(step == pl.num_programs(0) - 1)
    def _():
        out_ref[...] = (r_ref[...] + acc[...] + bout_ref[...]).astype(BF)
        dh_ref[...] = dacc[...]


def feed(where, h, g, r, win_own, win_oth, b_in, wout_own, wout_oth, b_out):
    rows, d = h.shape
    hc = win_own.shape[0]
    ff = win_own.shape[1]
    bf = 384
    n = ff // 2 // bf
    lower = lambda i, p: i
    upper = lambda i, p: n + i
    whole = pl.BlockSpec((rows, d), lambda i, p: (0, 0))
    side = lambda height, which: pl.BlockSpec((height, bf), lambda i, p: (0, which(i, p)))
    grad = pl.BlockSpec((2, bf, d), lambda i, p: (0, i, 0))
    wout = pl.BlockSpec((bf, d), lambda i, p: (i, 0))
    gb = pl.BlockSpec((8, bf), lambda i, p: (0, i))
    return pl.pallas_call(
        feed_kernel,
        grid_spec=pltpu.PrefetchScalarGridSpec(
            num_scalar_prefetch=1,
            grid=(n,),
            in_specs=[
                whole, whole, whole,
                side(hc, lower), side(hc, upper), side(hc, lower), side(hc, upper), side(1, lower), side(1, upper),
                wout, wout,
                pl.BlockSpec((1, d), lambda i, p: (0, 0)),
            ],
            out_specs=[whole, whole, grad, grad, gb, gb],
            scratch_shapes=[
                pltpu.VMEM((d, rows), BF),
                pltpu.VMEM((rows, d), F32),
                pltpu.VMEM((rows, d), F32),
                pltpu.VMEM((rows, 2 * bf), BF),
                pltpu.VMEM((rows, 2 * bf), BF),
            ],
        ),
        out_shape=[
            jax.ShapeDtypeStruct((rows, d), BF),
            jax.ShapeDtypeStruct((rows, d), F32),
            jax.ShapeDtypeStruct((2, ff // 2, d), BF),
            jax.ShapeDtypeStruct((2, ff // 2, d), BF),
            jax.ShapeDtypeStruct((8, ff // 2), F32),
            jax.ShapeDtypeStruct((8, ff // 2), F32),
        ],
        compiler_params=params(),
        cost_estimate=cost(12 * rows * d * ff, 8 * d * ff),
    )(where, h, g, r, win_own, win_own, win_oth, win_oth, b_in, b_in, wout_own, wout_oth, b_out)


def norm(rows, gain, bias):
    mean = jnp.mean(rows, axis=-1, keepdims=True)
    centred = rows - mean
    spread_ = jnp.mean(centred * centred, axis=-1, keepdims=True)
    return centred * lax.rsqrt(spread_ + EPS) * gain + bias


def norm_back(rows, gain, grad):
    mean = jnp.mean(rows, axis=-1, keepdims=True)
    centred = rows - mean
    rstd = lax.rsqrt(jnp.mean(centred * centred, axis=-1, keepdims=True) + EPS)
    hat = centred * rstd
    scaled = grad * gain
    inner = jnp.mean(scaled * hat, axis=-1, keepdims=True)
    back = rstd * (scaled - jnp.mean(scaled, axis=-1, keepdims=True) - hat * inner)
    return back, jnp.sum(grad * hat, axis=0), jnp.sum(grad, axis=0)


class Links:
    def __init__(self, dp, tp):
        self.dp = dp
        self.bits = dp.bit_length() - 1
        self.me = lax.axis_index("dp")
        self.core = self.me & 1
        self.half = lax.axis_index("tp")
        self.swap = [(i, tp - 1 - i) for i in range(tp)]
        rest = list(range(1, self.bits))
        turned = [2, 1] + rest[2:] if self.bits > 2 else rest
        self.steps = list(zip(rest, turned))

    def other(self, x):
        return lax.ppermute(x, "tp", self.swap)

    def across(self, x, step):
        return lax.ppermute(x, "dp", [(i, i ^ (1 << step[i & 1])) for i in range(self.dp)])

    def flag(self, step):
        return (self.me >> jnp.where(self.core == 0, step[0], step[1])) & 1

    def joined(self, mine, theirs, flag, axis=0):
        first = flag == 0
        return jnp.concatenate(
            [jnp.where(first, mine, theirs), jnp.where(first, theirs, mine)], axis=axis
        )

    def piece(self):
        return self.core * 4 + self.flag(self.steps[1]) * 2 + self.flag(self.steps[0])

    def spread(self, x, i):
        step = ([*self.steps[:2], (0, 0)])[i]
        return self.joined(x, self.across(x, step), self.flag(step))

    def fold(self, x, step):
        flag = self.flag(step)
        rows = x[0].shape[1] // 2
        part = lambda at: add(*(lax.dynamic_slice_in_dim(y, at * rows, rows, 1) for y in x))
        return part(flag), self.across(part(1 - flag), step)

    def meet(self, x):
        send = add(*(y[1:] for y in x))
        return add(*(y[:1] for y in x)), self.other(send)

    def halves(self, a, b):
        return jnp.where(self.core == 0, a, b), jnp.where(self.core == 0, b, a)

    def plane_sum(self):
        yield lambda x: (x[0], self.across(x[1], (0, 0)))
        for step in self.steps:
            yield functools.partial(self.fold, step=step)

    def plane_share(self):
        for step in reversed(self.steps):
            yield lambda x, step=step: self.joined(x, self.across(x, step), self.flag(step))
        yield lambda x: (x, self.across(x, (0, 0)))

    def pair(self, x):
        mine, theirs = x
        return jnp.where(self.core == 0, mine, theirs), jnp.where(self.core == 0, theirs, mine)


def add(a, b):
    return (a.astype(F32) + b.astype(F32)).astype(BF)


def tie(*arrays):
    return lax.optimization_barrier(arrays)


class Flow:
    def __init__(self, x, todo):
        self.x, self.todo = x, list(todo)

    def next(self):
        if self.todo:
            self.x = self.todo.pop(0)(self.x)


def advance(flows, *arrays):
    done = lax.optimization_barrier(([f.x for f in flows], *arrays))
    for f, x in zip(flows, done[0]):
        f.x = x
        f.next()
    return done[1] if len(arrays) == 1 else done[1:]


def shift_earlier(x):
    pad = jnp.zeros((SPAN - 1, x.shape[1]), x.dtype)
    return jnp.concatenate([x[SPAN - 1 :], pad], axis=0)


def shift_later(x):
    pad = jnp.zeros((SPAN - 1, x.shape[1]), x.dtype)
    return jnp.concatenate([pad, x[: x.shape[0] - SPAN + 1]], axis=0)


def on_device(
    tokens, neighbours, nbr_index, lengths, w_qkv, qv_bias, w_out, cross_q, cross_kv,
    cross_bias, cross_out, out_bias, ln_gain, ln_bias, fc_in, fc_in_bias, fc_out,
    fc_out_bias, cotangent,
):
    tp = lax.axis_size("tp")
    link = Links(lax.axis_size("dp"), tp)
    half = link.half
    d = tokens.shape[1]
    hc = w_qkv.shape[2]
    ffh = fc_in_bias.shape[0]
    ff = ffh * tp
    spans = nbr_index.shape[1] // tp
    length = lax.dynamic_slice_in_dim(lengths[0], half, 1)
    core = link.core

    small = jnp.concatenate(
        [fc_in_bias.reshape(-1, hc), fc_out_bias.reshape(1, hc), out_bias, ln_gain, ln_bias, qv_bias, cross_bias],
        axis=0,
    )
    small_oth = link.other(small)
    qkv_own = w_qkv.reshape(d, 3 * hc)
    eighth, w8, f8 = d // 8, hc // 8, hc // 8
    place = jnp.stack([core, link.piece()])
    first, second, third = pack_weights(
        place, qkv_own, cross_kv.reshape(d, 2 * hc), cross_q, w_out, cross_out, fc_in, fc_out
    )
    first = link.other(first)
    second = link.other(second)[None]

    order = nbr_index[0]
    keep = lax.dynamic_slice_in_dim(order, half * spans, spans)
    send = lax.dynamic_slice_in_dim(order, (1 - half) * spans, spans)
    nbr_own, nbr_send = pick_blocks(neighbours, keep, send)

    def whole(at, count, natural=True):
        a, b = small[at : at + count], small_oth[at : at + count]
        if natural:
            return link.joined(a, b, half, 1).astype(F32)
        return a.astype(F32), b.astype(F32)

    at = ffh // hc
    b_in = link.joined(small[:at].reshape(1, ffh), small_oth[:at].reshape(1, ffh), half, 1).astype(F32)
    b_out = whole(at, 1)
    out_b = whole(at + 1, 2)
    gains = whole(at + 3, 3)
    shifts = whole(at + 6, 3)
    qv_b = whole(at + 9, 2, False)
    cross_b = whole(at + 11, 2, False)

    tok = tokens.astype(F32)
    h1 = norm(tok, gains[0], shifts[0]).astype(BF)

    def project(w, which):
        bias = jnp.concatenate([qv_b[which][0], jnp.zeros((hc,), F32), qv_b[which][1]])
        scale = jnp.concatenate([jnp.full((hc,), SCORE, F32), jnp.ones((2 * hc,), F32)])
        return ((mm(h1, w) + bias) * scale).astype(BF)

    p_own = project(qkv_own, 0)
    ctx_own, lse_own = self_fwd(p_own, length)
    first, ctx_own, second, third, nbr_send = tie(first, ctx_own, second, third, nbr_send)
    qkv_pair = link.across(first, (0, 0))
    second = link.spread(second, 0)
    cutoff = spans // 2
    nbr_a = link.other(nbr_send[:cutoff])
    qkv_oth = link.joined(first, qkv_pair, core)
    p_oth = project(qkv_oth, 1)
    p_oth, second = tie(p_oth, second)
    second = link.spread(second, 1)
    ctx_oth, lse_oth = self_fwd(p_oth, length)
    ctx_oth, second, nbr_a, nbr_send, third = tie(ctx_oth, second, nbr_a, nbr_send, third)
    second = link.spread(second, 2)
    third = link.other(third)[None]
    nbr_b = link.other(nbr_send[cutoff:])

    rows = lambda lo, n: second[:, lo : lo + n].reshape(8 * n, hc)
    ctx = jnp.concatenate([ctx_own, ctx_oth], axis=1)
    pair = lambda at: jnp.concatenate([rows(at, w8), rows(at + w8, w8)], axis=1)
    wo = jnp.concatenate([w_out, pair(3 * eighth)], axis=0)
    co_w = jnp.concatenate([cross_out, pair(3 * eighth + 2 * w8)], axis=0)
    cq_w = jnp.concatenate([cross_q, rows(2 * eighth, eighth)], axis=1)
    kv_w = jnp.concatenate(
        [cross_kv[:, 0], rows(0, eighth), cross_kv[:, 1], rows(eighth, eighth)], axis=1
    )
    r1 = tok + mm(ctx, wo) + out_b[0]
    h2 = norm(r1, gains[1], shifts[1]).astype(BF)
    cb = [jnp.concatenate([cross_b[0][i], cross_b[1][i]]) for i in range(2)]
    cq = shift_earlier(((mm(h2, cq_w) + cb[0]) * SCORE).astype(BF))
    kv_b = jnp.concatenate([jnp.zeros((d,), F32), cb[1]])
    nbr_own = nbr_own.reshape(-1, d)
    ckv_own = (mm(nbr_own, kv_w) + kv_b).astype(BF)
    cq, ckv_own, third = tie(cq, ckv_own, third)
    third = link.spread(third, 0)
    half_rows = ckv_own.shape[0] // 2
    nbr_a = nbr_a.reshape(-1, d)
    ckv_a = (mm(nbr_a, kv_w) + kv_b).astype(BF)
    cq_rows = cutoff * SPAN
    c_a = cross_fwd(cq[:cq_rows], ckv_own[:half_rows], ckv_a)
    c_a, third, nbr_b = tie(c_a, third, nbr_b)
    third = link.spread(third, 1)
    nbr_b = nbr_b.reshape(-1, d)
    ckv_b = (mm(nbr_b, kv_w) + kv_b).astype(BF)
    c_b = cross_fwd(cq[cq_rows:], ckv_own[half_rows:], ckv_b)
    c_b, third = tie(c_b, third)
    third = link.spread(third, 2)
    cctx = shift_later(jnp.concatenate([c_a, c_b], axis=0))
    r2 = r1 + mm(cctx, co_w) + out_b[1]
    h3 = norm(r2, gains[2], shifts[2]).astype(BF)
    turn = lambda x: link.joined(x[:, :hc], x[:, hc:], half, 1)
    win_oth = jnp.concatenate(
        [third[:, i * f8 : (i + 1) * f8].reshape(hc, d) for i in range(ff // d)], axis=1
    )
    wout_oth = third[:, (ff // d) * f8 :].reshape(ffh, d)
    block_out, d_h3, fc_keep, fc_send, gb_low, gb_high = feed(
        jnp.stack([half, core]), turn(h3), cotangent, r2, fc_in, win_oth, b_in, fc_out, wout_oth, b_out
    )

    plane, share = link.plane_sum, link.plane_share

    share_steps = list(share())

    def sum_flow(keep, send):
        steps = list(plane())
        steps[3:3] = [link.meet]
        return Flow((keep, send), steps + [lambda x: share_steps[0](add(*x)[0])] + share_steps[1:])

    fc = sum_flow(fc_keep, fc_send)
    fc.next()
    cot = cotangent.astype(F32)
    back3, gain3, shift3 = norm_back(r2, gains[2], turn(d_h3))
    d_r2 = cot + back3
    z2 = d_r2.astype(BF)
    e = mm(z2, co_w, NT).astype(BF)
    e, z2 = advance([fc], e, z2)
    d_cq, d_own, d_oth = cross_bwd(cq, ckv_own, ckv_a, ckv_b, shift_earlier(e))
    g_co = mm(cctx, z2, TN).astype(BF)
    d_cq, d_own, d_oth, g_co = advance([fc], d_cq, d_own, d_oth, g_co)
    n_oth = mm(d_oth, kv_w, NT).astype(BF).reshape(spans, -1, d)
    d_cq = shift_later(d_cq)
    back2, gain2, shift2 = norm_back(r1, gains[1], mm(d_cq, cq_w, NT))
    d_r1 = d_r2 + back2
    z1 = d_r1.astype(BF)
    f = mm(z1, wo, NT).astype(BF)
    n_oth, f, d_own = advance([fc], n_oth, f, d_own)
    n_back = link.other(n_oth)
    o_rows = d_oth.shape[0] // 2
    g_kv = (
        mm(nbr_own, d_own, TN) + mm(nbr_a, d_oth[:o_rows], TN) + mm(nbr_b, d_oth[o_rows:], TN)
    ).astype(BF)
    g_kv, d_cq, z1, d_own, f = advance([fc], g_kv, d_cq, z1, d_own, f)
    g_cq = mm(h2, d_cq, TN).astype(BF)
    g_wo = mm(ctx, z1, TN).astype(BF)
    sides = (slice(0, hc), slice(hc, d))
    both = lambda parts: jnp.stack([jnp.concatenate(p, axis=0) for p in parts])
    g_cross = both([[g_kv[:, s], g_kv[:, d:][:, s]] for s in sides]), both(
        [[g_cq[:, s], g_co[s][:, :hc], g_co[s][:, hc:]] for s in sides]
    )
    g_cross, g_wo, f, d_own = tie(link.halves(*g_cross), g_wo, f, d_own)
    cross = sum_flow(*g_cross)
    cross.next()
    n_own = mm(d_own, kv_w, NT).reshape(spans, -1, d)
    n_own, g_wo, f = advance([fc, cross], n_own, g_wo, f)
    dq_oth = self_bwd(p_oth, f[:, hc:], ctx_oth, lse_oth, length)
    dq_oth, f = advance([fc, cross], dq_oth, f)
    dq_own = self_bwd(p_own, f[:, :hc], ctx_own, lse_own, length)
    dq_own, d_own, g_wo = advance([fc, cross], dq_own, d_own, g_wo)
    g_qkv = [[mm(h1, part[i], TN).astype(BF) for part in (dq_own, dq_oth)] for i in range(3)]
    g_self = both([[q, k] for q, k in zip(g_qkv[0], g_qkv[1])]), both(
        [[v, g_wo[s][:, :hc], g_wo[s][:, hc:]] for v, s in zip(g_qkv[2], sides)]
    )
    g_self, dq_own, dq_oth = tie(link.halves(*g_self), dq_own, dq_oth)
    own = sum_flow(*g_self)
    own.next()
    flat = lambda x: jnp.concatenate([x[0], x[1], x[2]], axis=1)
    d_h1 = mm(flat(dq_own), qkv_own, NT) + mm(flat(dq_oth), qkv_oth, NT)
    d_h1, n_own = advance([fc, cross, own], d_h1, n_own)
    back1, gain1, shift1 = norm_back(tok, gains[0], d_h1)
    tokens_grad = d_r1 + back1

    wide = lambda x: jnp.sum(x.astype(F32), axis=0)
    natural = [
        gb_low[0], gb_high[0], wide(cot), wide(d_r1), wide(d_r2), gain1, gain2, gain3, shift1, shift2, shift3,
    ]
    relative = [wide(dq_own[0]), wide(dq_oth[0]), wide(dq_own[2]), wide(dq_oth[2])]
    cqs, cvs = wide(d_cq), wide(d_own[:, d:]) + wide(d_oth[:, d:])
    relative += [cqs[:hc], cqs[hc:], cvs[:hc], cvs[hc:]]
    for i in range(0, len(relative), 2):
        natural.append(link.joined(relative[i], relative[i + 1], half))
    natural = [x[i : i + d] for x in natural for i in range(0, x.shape[0], d)]
    height = len(natural) + -len(natural) % 8
    row = iota((height, d), 0)
    table = jnp.zeros((height, d), F32)
    for i, x in enumerate(natural):
        table = jnp.where(row == i, x[None], table)
    natural = table
    every = [lambda x, b=b: x + link.across(x, (b, b)) for b in range(link.bits)]
    every.append(lambda x: x + link.other(x))
    nbr_grad = place_blocks(order_of(keep, send), n_own, n_back)
    tokens_grad, natural, nbr_grad = advance([fc, cross, own], tokens_grad, natural, nbr_grad)
    while fc.todo:
        advance([fc, cross, own])
    sums = Flow(natural, every)
    sums.next()
    wide_rows = lambda x, n: jnp.concatenate(
        [x[i * (x.shape[0] // n) : (i + 1) * (x.shape[0] // n)] for i in range(n)], axis=1
    )
    s_in, s_out = link.pair(fc.x)
    steps_in = s_in.shape[0] // hc
    fc_in_grad = jnp.concatenate(
        [wide_rows(s_in[:, :hc], steps_in), wide_rows(s_in[:, hc:], steps_in)], axis=1
    ).astype(F32)
    fc_in_grad, s_out = advance([cross, own, sums], fc_in_grad, s_out)
    fc_out_grad = s_out.astype(F32)
    fc_out_grad = advance([cross, own, sums], fc_out_grad)
    while cross.todo:
        advance([cross, own, sums])
    advance([cross, own, sums])
    s_kv, s_rest = link.pair(cross.x)
    cross_kv_grad = jnp.stack([s_kv[:d], s_kv[d:]], axis=1).astype(F32)
    cross_q_grad = s_rest[:d].astype(F32)
    co_grad = wide_rows(s_rest[d:], 2).astype(F32)
    while own.todo or sums.todo:
        cross_kv_grad, cross_q_grad, co_grad = advance([own, sums], cross_kv_grad, cross_q_grad, co_grad)
    s_qk, s_vw = link.pair(own.x)
    qkv_grad = jnp.stack([s_qk[:d], s_qk[d:], s_vw[:d]], axis=1).astype(F32)
    wo_grad = wide_rows(s_vw[d:], 2).astype(F32)
    sums = sums.x
    gb_in = lax.dynamic_slice_in_dim(sums[: ff // d].reshape(-1), half * ffh, ffh)
    rest = lax.dynamic_slice_in_dim(sums[ff // d : ff // d + 13], half * hc, hc, 1)
    return (
        block_out,
        tokens_grad,
        nbr_grad,
        qkv_grad,
        rest[9:11],
        wo_grad,
        cross_q_grad,
        cross_kv_grad,
        rest[11:13],
        co_grad,
        rest[1:3],
        rest[3:6],
        rest[6:9],
        fc_in_grad,
        gb_in,
        fc_out_grad,
        rest[0],
    )


def order_of(keep, send):
    return jnp.concatenate([keep, send])


def solution(mesh):
    return jax.shard_map(
        on_device,
        mesh=mesh,
        in_specs=(
            P(("dp", "tp"), None),
            P("dp", "tp", None),
            P("dp", None),
            P("dp", None),
            P(None, None, "tp"),
            P(None, "tp"),
            P("tp", None),
            P(None, "tp"),
            P(None, None, "tp"),
            P(None, "tp"),
            P("tp", None),
            P(None, "tp"),
            P(None, "tp"),
            P(None, "tp"),
            P("tp", None),
            P("tp"),
            P("tp", None),
            P("tp"),
            P(("dp", "tp"), None),
        ),
        out_specs=(
            P(("dp", "tp"), None),
            P(("dp", "tp"), None),
            P("dp", "tp", None),
            P(None, None, "tp"),
            P(None, "tp"),
            P("tp", None),
            P(None, "tp"),
            P(None, None, "tp"),
            P(None, "tp"),
            P("tp", None),
            P(None, "tp"),
            P(None, "tp"),
            P(None, "tp"),
            P("tp", None),
            P("tp"),
            P("tp", None),
            P("tp"),
        ),
        check_vma=False,
    )
```

```python
import functools

import jax
import jax.numpy as jnp
from jax import lax
from jax.experimental import pallas as pl
from jax.experimental.pallas import tpu as pltpu
from jax.sharding import PartitionSpec as P

HEAD = 64
SPAN = 64
LEN = 1024
NBR = 256
EPS = 1e-05
BF = jnp.bfloat16
F32 = jnp.float32
DEAD = -1e30
LN2 = 0.6931471805599453
SCORE = 0.125 / LN2
VMEM_LIMIT = 60 * 1024 * 1024

NN = (((1,), (0,)), ((), ()))
NT = (((1,), (1,)), ((), ()))
TN = (((0,), (0,)), ((), ()))


def mm(a, b, dims=NN):
    return lax.dot_general(a, b, dims, preferred_element_type=F32)


def iota(shape, dim):
    return lax.broadcasted_iota(jnp.int32, shape, dim)


def cost(flops, nbytes, exps=0):
    return pl.CostEstimate(flops=flops, bytes_accessed=nbytes, transcendentals=exps)


def params(n=1):
    return pltpu.CompilerParams(
        dimension_semantics=("arbitrary",) * n, vmem_limit_bytes=VMEM_LIMIT
    )


def three(x):
    hi = x.astype(BF)
    rest = x - hi.astype(F32)
    mid = rest.astype(BF)
    return hi.astype(F32), mid.astype(F32), rest - mid.astype(F32)


def self_fwd_kernel(len_ref, q_ref, k_ref, v_ref, o_ref, lse_ref):
    bq = 512
    length = len_ref[0]
    low = iota((LEN, 128), 1) < HEAD
    lane = iota((LEN, 128), 1)
    q, k, v = (ref[...] for ref in (q_ref, k_ref, v_ref))
    one = jnp.ones((LEN, 128), BF)
    zero = jnp.zeros((LEN, 128), BF)
    dead = jnp.where(iota((LEN, 128), 0) < length, 0.0, DEAD).astype(BF)
    at = lambda x, first: jnp.where(lane == first, x, zero)
    qs = (jnp.where(low, q, at(one, HEAD)), jnp.where(low, at(one, 0), q))
    ks = (jnp.where(low, k, at(dead, HEAD)), jnp.where(low, at(dead, 0), k))
    vs = (jnp.where(low, v, one), jnp.where(low, one, v))
    tri = iota((bq, bq), 1) <= iota((bq, bq), 0)
    low_q = low[:bq]
    for i in range(LEN // bq):
        lo, hi = i * bq, (i + 1) * bq
        outs, tops = [], []
        for h in range(2):
            here = jnp.where(tri, mm(qs[h][lo:hi], ks[h][lo:hi], NT), DEAD)
            m = jnp.max(here, axis=1, keepdims=True)
            if i:
                left = mm(qs[h][lo:hi], ks[h][:lo], NT)
                m = jnp.maximum(m, jnp.max(left, axis=1, keepdims=True))
            o = mm(jnp.exp2(here - m).astype(BF), vs[h][lo:hi])
            if i:
                o += mm(jnp.exp2(left - m).astype(BF), vs[h][:lo])
            outs.append(o)
            tops.append(m)
        a, b = outs
        o_ref[lo:hi, :] = (jnp.where(low_q, a, b) / pltpu.roll(jnp.where(low_q, b, a), HEAD, 1)).astype(BF)
        lse_ref[lo:hi, :] = jnp.where(low_q, tops[1], tops[0]) + jnp.log2(jnp.where(low_q, b, a))


def self_fwd(qkv, length):
    pairs = qkv.shape[1] // 3 // 128
    block = lambda part: pl.BlockSpec((LEN, 128), lambda i, n: (0, part * pairs + i))
    return pl.pallas_call(
        self_fwd_kernel,
        grid_spec=pltpu.PrefetchScalarGridSpec(
            num_scalar_prefetch=1,
            grid=(pairs,),
            in_specs=[block(0), block(1), block(2)],
            out_specs=[block(0), block(0)],
        ),
        out_shape=[
            jax.ShapeDtypeStruct((LEN, pairs * 128), BF),
            jax.ShapeDtypeStruct((LEN, pairs * 128), F32),
        ],
        compiler_params=params(),
        cost_estimate=cost(pairs * 2 * 4 * LEN * LEN * 128, pairs * 8 * LEN * 128),
    )(length, qkv, qkv, qkv)


def self_bwd_kernel(len_ref, q_ref, k_ref, v_ref, f_ref, o_ref, lse_ref, d_ref, dq_ref):
    bk = 256
    length = len_ref[0]
    lane = iota((LEN, 128), 1)
    low = lane < HEAD
    q, k, v, f = (ref[...] for ref in (q_ref, k_ref, v_ref, f_ref))
    zero = jnp.zeros((LEN, 128), BF)
    place = lax.rem(lane, HEAD)
    prod = f.astype(F32) * o_ref[...].astype(F32)
    crossed = jnp.where((iota((128, 128), 0) < HEAD) == (iota((128, 128), 1) < HEAD), 0.0, 1.0).astype(BF)
    prod_hi = prod.astype(BF)
    delta = mm(prod_hi, crossed) + mm((prod - prod_hi.astype(F32)).astype(BF), crossed)

    def free(x, last):
        hi, mid, rest = three(-x)
        out = jnp.where(place == 0, hi, jnp.where(place == 1, mid, jnp.where(place == 2, rest, last)))
        return out.astype(BF)

    q_free = free(lse_ref[...], jnp.where(place == 3, 1.0, 0.0))
    f_free = free(delta, jnp.zeros((LEN, 128), F32))
    dead = jnp.where(iota((LEN, 128), 0) < length, 0.0, DEAD)
    ones = jnp.where(place < 3, 1.0, 0.0)
    k_free = jnp.where(place == 3, dead, ones).astype(BF)
    v_free = ones.astype(BF)
    pick = lambda x, y: (jnp.where(low, x, y), jnp.where(low, y, x))
    qx, fx, kx, vx = pick(q, q_free), pick(f, f_free), pick(k, k_free), pick(v, v_free)
    qs, fs, ks = pick(q, zero), pick(f, zero), pick(k, zero)
    tri = iota((bk, bk), 0) <= iota((bk, bk), 1)
    for j in range(LEN // bk):
        lo, hi = j * bk, (j + 1) * bk
        ps, dss = [], []
        for h in range(2):
            p = jnp.exp2(mm(kx[h][lo:hi], qx[h][lo:], NT))
            first = jnp.where(tri, p[:, :bk], 0.0)
            p = jnp.concatenate([first, p[:, bk:]], axis=1) if hi < LEN else first
            ds = (p * mm(vx[h][lo:hi], fx[h][lo:], NT)).astype(BF)
            ps.append(p.astype(BF))
            dss.append(ds)
        dv = mm(jnp.concatenate(ps, axis=1), jnp.concatenate([fs[0][lo:], fs[1][lo:]], axis=0))
        dk = mm(jnp.concatenate(dss, axis=1), jnp.concatenate([qs[0][lo:], qs[1][lo:]], axis=0))
        kk = jnp.concatenate([ks[0][lo:hi], ks[1][lo:hi]], axis=0)
        part = mm(jnp.concatenate(dss, axis=0), kk, TN)
        if j:
            dq_ref[lo:, :] += part
        else:
            dq_ref[...] = part
        d_ref[1, lo:hi, :] = (dk * LN2).astype(BF)
        d_ref[2, lo:hi, :] = dv.astype(BF)
    d_ref[0] = (dq_ref[...] * 0.125).astype(BF)


def self_bwd(qkv, back, ctx, lse, length):
    pairs = qkv.shape[1] // 3 // 128
    block = lambda part: pl.BlockSpec((LEN, 128), lambda i, n: (0, part * pairs + i))
    return pl.pallas_call(
        self_bwd_kernel,
        grid_spec=pltpu.PrefetchScalarGridSpec(
            num_scalar_prefetch=1,
            grid=(pairs,),
            in_specs=[block(0), block(1), block(2), block(0), block(0), block(0)],
            out_specs=pl.BlockSpec((3, LEN, 128), lambda i, n: (0, 0, i)),
            scratch_shapes=[pltpu.VMEM((LEN, 128), F32)],
        ),
        out_shape=jax.ShapeDtypeStruct((3, LEN, pairs * 128), BF),
        compiler_params=params(),
        cost_estimate=cost(pairs * 2 * 10 * LEN * LEN * 128, pairs * 16 * LEN * 128),
    )(length, qkv, qkv, qkv, back, ctx, lse)


PER_STEP = 4


def own_heads():
    return jnp.where(iota((256, 256), 0) // SPAN == iota((256, 256), 1) // HEAD, 1.0, 0.0).astype(BF)


def spread(rows, mask):
    return jnp.concatenate([rows] * 4, axis=0) * mask


def gathered(rows, lanes):
    out = jnp.where(lanes == 0, rows[:SPAN], 0.0)
    for g in range(1, 4):
        out = jnp.where(lanes == g, rows[g * SPAN : (g + 1) * SPAN], out)
    return out


def fours(count, width, rows):
    for u in range(count):
        for t in range(width // 256):
            yield slice(u * SPAN, (u + 1) * SPAN), slice(u * rows, (u + 1) * rows), t * 256


def cross_fwd_kernel(q_ref, own_ref, oth_ref, o_ref):
    width = q_ref.shape[1]
    rows = own_ref.shape[0] // PER_STEP
    mask = own_heads()
    lanes = iota((SPAN, 256), 1) // HEAD
    one = jnp.ones((2 * rows, 128), BF)
    both = lambda at, lo: jnp.concatenate(
        [own_ref[at, lo : lo + 256], oth_ref[at, lo : lo + 256]], axis=0
    )
    jobs = list(fours(PER_STEP, width, rows))
    scores = [mm(spread(q_ref[q, lo : lo + 256], mask), both(kv, lo), NT) for q, kv, lo in jobs]
    probs = [jnp.exp2(s - jnp.max(s, axis=1, keepdims=True)).astype(BF) for s in scores]
    for p, (q, kv, lo) in zip(probs, jobs):
        o = mm(p, both(kv, width + lo))
        total = 1.0 / mm(p, one)
        o = o * jnp.concatenate([total, total], axis=1)
        o_ref[q, lo : lo + 256] = gathered(o, lanes).astype(BF)


def cross_fwd(q, own, oth):
    width = q.shape[1]
    spans = q.shape[0] // SPAN
    rows = own.shape[0] // spans
    row = pl.BlockSpec((PER_STEP * SPAN, width), lambda i: (i, 0))
    kv = pl.BlockSpec((PER_STEP * rows, 2 * width), lambda i: (i, 0))
    return pl.pallas_call(
        cross_fwd_kernel,
        grid=(spans // PER_STEP,),
        in_specs=[row, kv, kv],
        out_specs=row,
        out_shape=jax.ShapeDtypeStruct(q.shape, BF),
        compiler_params=params(),
        cost_estimate=cost(spans * 3 * 4 * 256**3, spans * 1000000),
    )(q, own, oth)


def cross_bwd_kernel(q_ref, own_ref, oth_a_ref, oth_b_ref, e_ref, dq_ref, down_ref, doth_ref):
    width = q_ref.shape[1]
    rows = own_ref.shape[0] // PER_STEP
    early = pl.program_id(0) < pl.num_programs(0) // 2
    oth = jnp.where(early, oth_a_ref[...], oth_b_ref[...])
    mask = own_heads()
    lanes = iota((SPAN, 256), 1) // HEAD
    both = lambda at, lo: jnp.concatenate([own_ref[at, lo : lo + 256], oth[at, lo : lo + 256]], axis=0)
    jobs = list(fours(PER_STEP, width, rows))
    q4 = [spread(q_ref[q, lo : lo + 256], mask) for q, kv, lo in jobs]
    e4 = [spread(e_ref[q, lo : lo + 256], mask) for q, kv, lo in jobs]
    scores = [mm(both(kv, lo), x, NT) for x, (q, kv, lo) in zip(q4, jobs)]
    backs = [mm(both(kv, width + lo), x, NT) for x, (q, kv, lo) in zip(e4, jobs)]
    for s, dp, x, y, (q, kv, lo) in zip(scores, backs, q4, e4, jobs):
        p = jnp.exp2(s - jnp.max(s, axis=0, keepdims=True))
        p = p * (1.0 / jnp.sum(p, axis=0, keepdims=True))
        delta = jnp.sum(p * dp, axis=0, keepdims=True)
        ds = (p * (dp - delta)).astype(BF)
        dk = (mm(ds, x) * LN2).astype(BF)
        dv = mm(p.astype(BF), y).astype(BF)
        down_ref[kv, lo : lo + 256] = dk[:rows]
        doth_ref[kv, lo : lo + 256] = dk[rows:]
        down_ref[kv, width + lo : width + lo + 256] = dv[:rows]
        doth_ref[kv, width + lo : width + lo + 256] = dv[rows:]
        dq_ref[q, lo : lo + 256] = (gathered(mm(ds, both(kv, lo), TN), lanes) * 0.125).astype(BF)


def cross_bwd(q, own, oth_a, oth_b, e):
    width = q.shape[1]
    spans = q.shape[0] // SPAN
    rows = own.shape[0] // spans
    steps = spans // PER_STEP
    row = pl.BlockSpec((PER_STEP * SPAN, width), lambda i: (i, 0))
    shape = (PER_STEP * rows, 2 * width)
    kv = pl.BlockSpec(shape, lambda i: (i, 0))
    return pl.pallas_call(
        cross_bwd_kernel,
        grid=(steps,),
        in_specs=[
            row,
            kv,
            pl.BlockSpec(shape, lambda i: (jnp.minimum(i, steps // 2 - 1), 0)),
            pl.BlockSpec(shape, lambda i: (jnp.maximum(i - steps // 2, 0), 0)),
            row,
        ],
        out_specs=[row, kv, kv],
        out_shape=[
            jax.ShapeDtypeStruct(q.shape, BF),
            jax.ShapeDtypeStruct(own.shape, BF),
            jax.ShapeDtypeStruct(own.shape, BF),
        ],
        compiler_params=params(),
        cost_estimate=cost(spans * 3 * 10 * 256**3, spans * 2000000),
    )(q, own, oth_a, oth_b, e)


def pick_kernel(keep_ref, send_ref, blocks_ref, keep_out, send_out, sems):
    count = keep_out.shape[0]
    copies = []
    for i in range(count):
        copies.append(
            pltpu.make_async_copy(blocks_ref.at[send_ref[i]], send_out.at[i], sems.at[0, i])
        )
    for i in range(count):
        copies.append(
            pltpu.make_async_copy(blocks_ref.at[keep_ref[i]], keep_out.at[i], sems.at[1, i])
        )
    for copy in copies:
        copy.start()
    for copy in copies:
        copy.wait()


def pick_blocks(neighbours, keep, send):
    count = keep.shape[0]
    smem = pl.BlockSpec(memory_space=pltpu.SMEM)
    anywhere = pl.BlockSpec(memory_space=pl.ANY)
    vmem = pl.BlockSpec(memory_space=pltpu.VMEM)
    return pl.pallas_call(
        pick_kernel,
        in_specs=[smem, smem, anywhere],
        out_specs=[vmem, vmem],
        out_shape=[jax.ShapeDtypeStruct((count,) + neighbours.shape[1:], BF)] * 2,
        scratch_shapes=[pltpu.SemaphoreType.DMA((2, count))],
        compiler_params=pltpu.CompilerParams(vmem_limit_bytes=VMEM_LIMIT),
        cost_estimate=cost(0, 4 * neighbours.size),
    )(keep, send, neighbours)


def pack_kernel(where_ref, qkv, kv, cq, wo, co, fin, fout, first, second, third, sems):
    core, p = where_ref[0], where_ref[1]
    d, hc = cq.shape
    e8, w8, o8 = d // 8, wo.shape[0] // 8, fout.shape[0] // 8
    take = lambda at, n: pl.ds(pl.multiple_of(at * n, 16), n)
    jobs = [(qkv.at[take(core, d // 2)], first)]
    to = 0
    for ref, count, n in ((kv, 2, e8), (cq, 1, e8), (wo, 2, w8), (co, 2, w8)):
        for i in range(count):
            jobs.append((ref.at[take(p, n), pl.ds(i * hc, hc)], second.at[pl.ds(to, n)]))
            to += n
    to = 0
    for i in range(fin.shape[1] // d):
        jobs.append((fin.at[take(p, w8), pl.ds(i * d, d)], third.at[pl.ds(to, w8)]))
        to += w8
    jobs.append((fout.at[take(p, o8)], third.at[pl.ds(to, o8)]))
    copies = [pltpu.make_async_copy(a, b, sems.at[i]) for i, (a, b) in enumerate(jobs)]
    for copy in copies:
        copy.start()
    for copy in copies:
        copy.wait()


def pack_weights(where, qkv, kv, cq, wo, co, fin, fout):
    anywhere = pl.BlockSpec(memory_space=pl.ANY)
    vmem = pl.BlockSpec(memory_space=pltpu.VMEM)
    d, hc = cq.shape
    n_in = fin.shape[1] // d
    return pl.pallas_call(
        pack_kernel,
        in_specs=[pl.BlockSpec(memory_space=pltpu.SMEM)] + [anywhere] * 7,
        out_specs=[vmem, vmem, vmem],
        out_shape=[
            jax.ShapeDtypeStruct((d // 2, 3 * hc), BF),
            jax.ShapeDtypeStruct((3 * (d // 8) + 4 * (wo.shape[0] // 8), hc), BF),
            jax.ShapeDtypeStruct((n_in * (fin.shape[0] // 8) + fout.shape[0] // 8, d), BF),
        ],
        scratch_shapes=[pltpu.SemaphoreType.DMA((9 + n_in,))],
        compiler_params=pltpu.CompilerParams(vmem_limit_bytes=VMEM_LIMIT),
        cost_estimate=cost(0, 4 * 1024 * 1024),
    )(where, qkv, kv, cq, wo, co, fin, fout)


def place_kernel(order_ref, mine_ref, theirs_ref, out_ref, wide, sems):
    count = mine_ref.shape[0]
    copies = []
    for i in range(count):
        copy = pltpu.make_async_copy(mine_ref.at[i], out_ref.at[order_ref[i]], sems.at[i])
        copy.start()
        copies.append(copy)
    for i in range(count):
        wide[i] = theirs_ref[i].astype(F32)
        copy = pltpu.make_async_copy(
            wide.at[i], out_ref.at[order_ref[count + i]], sems.at[count + i]
        )
        copy.start()
        copies.append(copy)
    for copy in copies:
        copy.wait()


def place_blocks(order, mine, theirs):
    count = order.shape[0]
    return pl.pallas_call(
        place_kernel,
        in_specs=[
            pl.BlockSpec(memory_space=pltpu.SMEM),
            pl.BlockSpec(memory_space=pltpu.VMEM),
            pl.BlockSpec(memory_space=pltpu.VMEM),
        ],
        out_specs=pl.BlockSpec(memory_space=pl.ANY),
        out_shape=jax.ShapeDtypeStruct((count,) + mine.shape[1:], F32),
        scratch_shapes=[
            pltpu.VMEM(mine.shape, F32),
            pltpu.SemaphoreType.DMA((count,)),
        ],
        compiler_params=pltpu.CompilerParams(vmem_limit_bytes=VMEM_LIMIT),
        cost_estimate=cost(0, 8 * mine.size),
    )(order, mine, theirs)


GELU_A = 0.7978845608028654
GELU_B = 0.044715


def feed_kernel(
    half_ref, h_ref, g_ref, r_ref, aa_ref, ab_ref, ba_ref, bb_ref, bina_ref, binb_ref,
    wouta_ref, woutb_ref, bout_ref,
    out_ref, dh_ref, keep_ref, send_ref, gbina_ref, gbinb_ref, h_t, acc, dacc, act_s, dpre_s,
):
    step = pl.program_id(0)
    hc = aa_ref.shape[0]
    bf = aa_ref.shape[1]

    @pl.when(step == 0)
    def _():
        h_t[...] = h_ref[...].T

    win = jnp.concatenate(
        [
            jnp.concatenate([aa_ref[...], ab_ref[...]], axis=1),
            jnp.concatenate([ba_ref[...], bb_ref[...]], axis=1),
        ],
        axis=0,
    )
    here = half_ref[0] == 0
    wa, wb = wouta_ref[...], woutb_ref[...]
    wout = jnp.concatenate([jnp.where(here, wa, wb), jnp.where(here, wb, wa)], axis=0)
    bias = jnp.concatenate([bina_ref[...], binb_ref[...]], axis=1)
    rows = h_ref.shape[0]
    first = step == 0
    total = jnp.zeros(bias.shape, F32)
    for lo in range(0, rows, 256):
        at = slice(lo, lo + 256)
        pre = mm(h_ref[at], win) + bias
        dact = mm(g_ref[at], wout, NT)
        square = pre * pre
        th = jnp.tanh(pre * (GELU_A + GELU_A * GELU_B * square))
        half = 0.5 + 0.5 * th
        act = (pre * half).astype(BF)
        slope = half + pre * (half - half * th) * (GELU_A + 3.0 * GELU_A * GELU_B * square)
        dpre = (dact * slope).astype(BF)
        total += jnp.sum(dpre.astype(F32), axis=0, keepdims=True)
        act_s[at] = act
        dpre_s[at] = dpre
        acc[at] = jnp.where(first, 0.0, acc[at]) + mm(act, wout)
        dacc[at] = jnp.where(first, 0.0, dacc[at]) + mm(dpre, win, NT)
    gbina_ref[0:1, :] = total[:, :bf]
    gbinb_ref[0:1, :] = total[:, bf:]
    gout = mm(act_s[...], g_ref[...], TN).astype(BF)
    gin = mm(h_t[...], dpre_s[...]).astype(BF)

    def put(into_in, into_out):
        into_in[0], into_in[1] = gin[:hc], gin[hc:]
        into_out[0] = jnp.where(here, gout[:bf], gout[bf:])
        into_out[1] = jnp.where(here, gout[bf:], gout[:bf])

    @pl.when(half_ref[1] == 0)
    def _():
        put(keep_ref, send_ref)

    @pl.when(half_ref[1] != 0)
    def _():
        put(send_ref, keep_ref)

    @pl.when(step == pl.num_programs(0) - 1)
    def _():
        out_ref[...] = (r_ref[...] + acc[...] + bout_ref[...]).astype(BF)
        dh_ref[...] = dacc[...]


def feed(where, h, g, r, win_own, win_oth, b_in, wout_own, wout_oth, b_out):
    rows, d = h.shape
    hc = win_own.shape[0]
    ff = win_own.shape[1]
    bf = 384
    n = ff // 2 // bf
    lower = lambda i, p: i
    upper = lambda i, p: n + i
    whole = pl.BlockSpec((rows, d), lambda i, p: (0, 0))
    side = lambda height, which: pl.BlockSpec((height, bf), lambda i, p: (0, which(i, p)))
    grad = pl.BlockSpec((2, bf, d), lambda i, p: (0, i, 0))
    wout = pl.BlockSpec((bf, d), lambda i, p: (i, 0))
    gb = pl.BlockSpec((8, bf), lambda i, p: (0, i))
    return pl.pallas_call(
        feed_kernel,
        grid_spec=pltpu.PrefetchScalarGridSpec(
            num_scalar_prefetch=1,
            grid=(n,),
            in_specs=[
                whole, whole, whole,
                side(hc, lower), side(hc, upper), side(hc, lower), side(hc, upper), side(1, lower), side(1, upper),
                wout, wout,
                pl.BlockSpec((1, d), lambda i, p: (0, 0)),
            ],
            out_specs=[whole, whole, grad, grad, gb, gb],
            scratch_shapes=[
                pltpu.VMEM((d, rows), BF),
                pltpu.VMEM((rows, d), F32),
                pltpu.VMEM((rows, d), F32),
                pltpu.VMEM((rows, 2 * bf), BF),
                pltpu.VMEM((rows, 2 * bf), BF),
            ],
        ),
        out_shape=[
            jax.ShapeDtypeStruct((rows, d), BF),
            jax.ShapeDtypeStruct((rows, d), F32),
            jax.ShapeDtypeStruct((2, ff // 2, d), BF),
            jax.ShapeDtypeStruct((2, ff // 2, d), BF),
            jax.ShapeDtypeStruct((8, ff // 2), F32),
            jax.ShapeDtypeStruct((8, ff // 2), F32),
        ],
        compiler_params=params(),
        cost_estimate=cost(12 * rows * d * ff, 8 * d * ff),
    )(where, h, g, r, win_own, win_own, win_oth, win_oth, b_in, b_in, wout_own, wout_oth, b_out)


def norm(rows, gain, bias):
    mean = jnp.mean(rows, axis=-1, keepdims=True)
    centred = rows - mean
    spread_ = jnp.mean(centred * centred, axis=-1, keepdims=True)
    return centred * lax.rsqrt(spread_ + EPS) * gain + bias


def norm_back(rows, gain, grad):
    mean = jnp.mean(rows, axis=-1, keepdims=True)
    centred = rows - mean
    rstd = lax.rsqrt(jnp.mean(centred * centred, axis=-1, keepdims=True) + EPS)
    hat = centred * rstd
    scaled = grad * gain
    inner = jnp.mean(scaled * hat, axis=-1, keepdims=True)
    back = rstd * (scaled - jnp.mean(scaled, axis=-1, keepdims=True) - hat * inner)
    return back, jnp.sum(grad * hat, axis=0), jnp.sum(grad, axis=0)


class Links:
    def __init__(self, dp, tp):
        self.dp = dp
        self.bits = dp.bit_length() - 1
        self.me = lax.axis_index("dp")
        self.core = self.me & 1
        self.half = lax.axis_index("tp")
        self.swap = [(i, tp - 1 - i) for i in range(tp)]
        rest = list(range(1, self.bits))
        turned = [2, 1] + rest[2:] if self.bits > 2 else rest
        self.steps = list(zip(rest, turned))

    def other(self, x):
        return lax.ppermute(x, "tp", self.swap)

    def across(self, x, step):
        return lax.ppermute(x, "dp", [(i, i ^ (1 << step[i & 1])) for i in range(self.dp)])

    def flag(self, step):
        return (self.me >> jnp.where(self.core == 0, step[0], step[1])) & 1

    def joined(self, mine, theirs, flag, axis=0):
        first = flag == 0
        return jnp.concatenate(
            [jnp.where(first, mine, theirs), jnp.where(first, theirs, mine)], axis=axis
        )

    def piece(self):
        return self.core * 4 + self.flag(self.steps[1]) * 2 + self.flag(self.steps[0])

    def spread(self, x, i):
        step = ([*self.steps[:2], (0, 0)])[i]
        return self.joined(x, self.across(x, step), self.flag(step))

    def fold(self, x, step):
        flag = self.flag(step)
        rows = x[0].shape[1] // 2
        part = lambda at: add(*(lax.dynamic_slice_in_dim(y, at * rows, rows, 1) for y in x))
        return part(flag), self.across(part(1 - flag), step)

    def meet(self, x):
        send = add(*(y[1:] for y in x))
        return add(*(y[:1] for y in x)), self.other(send)

    def halves(self, a, b):
        return jnp.where(self.core == 0, a, b), jnp.where(self.core == 0, b, a)

    def plane_sum(self):
        yield lambda x: (x[0], self.across(x[1], (0, 0)))
        for step in self.steps:
            yield functools.partial(self.fold, step=step)

    def plane_share(self):
        for step in reversed(self.steps):
            yield lambda x, step=step: self.joined(x, self.across(x, step), self.flag(step))
        yield lambda x: (x, self.across(x, (0, 0)))

    def pair(self, x):
        mine, theirs = x
        return jnp.where(self.core == 0, mine, theirs), jnp.where(self.core == 0, theirs, mine)


def add(a, b):
    return (a.astype(F32) + b.astype(F32)).astype(BF)


def tie(*arrays):
    return lax.optimization_barrier(arrays)


class Flow:
    def __init__(self, x, todo):
        self.x, self.todo = x, list(todo)

    def next(self):
        if self.todo:
            self.x = self.todo.pop(0)(self.x)


def advance(flows, *arrays):
    done = lax.optimization_barrier(([f.x for f in flows], *arrays))
    for f, x in zip(flows, done[0]):
        f.x = x
        f.next()
    return done[1] if len(arrays) == 1 else done[1:]


def shift_earlier(x):
    pad = jnp.zeros((SPAN - 1, x.shape[1]), x.dtype)
    return jnp.concatenate([x[SPAN - 1 :], pad], axis=0)


def shift_later(x):
    pad = jnp.zeros((SPAN - 1, x.shape[1]), x.dtype)
    return jnp.concatenate([pad, x[: x.shape[0] - SPAN + 1]], axis=0)


def on_device(
    tokens, neighbours, nbr_index, lengths, w_qkv, qv_bias, w_out, cross_q, cross_kv,
    cross_bias, cross_out, out_bias, ln_gain, ln_bias, fc_in, fc_in_bias, fc_out,
    fc_out_bias, cotangent,
):
    tp = lax.axis_size("tp")
    link = Links(lax.axis_size("dp"), tp)
    half = link.half
    d = tokens.shape[1]
    hc = w_qkv.shape[2]
    ffh = fc_in_bias.shape[0]
    ff = ffh * tp
    spans = nbr_index.shape[1] // tp
    length = lax.dynamic_slice_in_dim(lengths[0], half, 1)
    core = link.core

    small = jnp.concatenate(
        [fc_in_bias.reshape(-1, hc), fc_out_bias.reshape(1, hc), out_bias, ln_gain, ln_bias, qv_bias, cross_bias],
        axis=0,
    )
    small_oth = link.other(small)
    qkv_own = w_qkv.reshape(d, 3 * hc)
    eighth, w8, f8 = d // 8, hc // 8, hc // 8
    place = jnp.stack([core, link.piece()])
    first, second, third = pack_weights(
        place, qkv_own, cross_kv.reshape(d, 2 * hc), cross_q, w_out, cross_out, fc_in, fc_out
    )
    first = link.other(first)
    second = link.other(second)[None]

    order = nbr_index[0]
    keep = lax.dynamic_slice_in_dim(order, half * spans, spans)
    send = lax.dynamic_slice_in_dim(order, (1 - half) * spans, spans)
    nbr_own, nbr_send = pick_blocks(neighbours, keep, send)

    def whole(at, count, natural=True):
        a, b = small[at : at + count], small_oth[at : at + count]
        if natural:
            return link.joined(a, b, half, 1).astype(F32)
        return a.astype(F32), b.astype(F32)

    at = ffh // hc
    b_in = link.joined(small[:at].reshape(1, ffh), small_oth[:at].reshape(1, ffh), half, 1).astype(F32)
    b_out = whole(at, 1)
    out_b = whole(at + 1, 2)
    gains = whole(at + 3, 3)
    shifts = whole(at + 6, 3)
    qv_b = whole(at + 9, 2, False)
    cross_b = whole(at + 11, 2, False)

    tok = tokens.astype(F32)
    h1 = norm(tok, gains[0], shifts[0]).astype(BF)

    def project(w, which):
        bias = jnp.concatenate([qv_b[which][0], jnp.zeros((hc,), F32), qv_b[which][1]])
        scale = jnp.concatenate([jnp.full((hc,), SCORE, F32), jnp.ones((2 * hc,), F32)])
        return ((mm(h1, w) + bias) * scale).astype(BF)

    p_own = project(qkv_own, 0)
    ctx_own, lse_own = self_fwd(p_own, length)
    first, ctx_own, second, third, nbr_send = tie(first, ctx_own, second, third, nbr_send)
    qkv_pair = link.across(first, (0, 0))
    second = link.spread(second, 0)
    cutoff = spans // 2
    nbr_a = link.other(nbr_send[:cutoff])
    qkv_oth = link.joined(first, qkv_pair, core)
    p_oth = project(qkv_oth, 1)
    p_oth, second = tie(p_oth, second)
    second = link.spread(second, 1)
    ctx_oth, lse_oth = self_fwd(p_oth, length)
    ctx_oth, second, nbr_a, nbr_send, third = tie(ctx_oth, second, nbr_a, nbr_send, third)
    second = link.spread(second, 2)
    third = link.other(third)[None]
    nbr_b = link.other(nbr_send[cutoff:])

    rows = lambda lo, n: second[:, lo : lo + n].reshape(8 * n, hc)
    ctx = jnp.concatenate([ctx_own, ctx_oth], axis=1)
    pair = lambda at: jnp.concatenate([rows(at, w8), rows(at + w8, w8)], axis=1)
    wo = jnp.concatenate([w_out, pair(3 * eighth)], axis=0)
    co_w = jnp.concatenate([cross_out, pair(3 * eighth + 2 * w8)], axis=0)
    cq_w = jnp.concatenate([cross_q, rows(2 * eighth, eighth)], axis=1)
    kv_w = jnp.concatenate(
        [cross_kv[:, 0], rows(0, eighth), cross_kv[:, 1], rows(eighth, eighth)], axis=1
    )
    r1 = tok + mm(ctx, wo) + out_b[0]
    h2 = norm(r1, gains[1], shifts[1]).astype(BF)
    cb = [jnp.concatenate([cross_b[0][i], cross_b[1][i]]) for i in range(2)]
    cq = shift_earlier(((mm(h2, cq_w) + cb[0]) * SCORE).astype(BF))
    kv_b = jnp.concatenate([jnp.zeros((d,), F32), cb[1]])
    nbr_own = nbr_own.reshape(-1, d)
    ckv_own = (mm(nbr_own, kv_w) + kv_b).astype(BF)
    cq, ckv_own, third = tie(cq, ckv_own, third)
    third = link.spread(third, 0)
    half_rows = ckv_own.shape[0] // 2
    nbr_a = nbr_a.reshape(-1, d)
    ckv_a = (mm(nbr_a, kv_w) + kv_b).astype(BF)
    cq_rows = cutoff * SPAN
    c_a = cross_fwd(cq[:cq_rows], ckv_own[:half_rows], ckv_a)
    c_a, third, nbr_b = tie(c_a, third, nbr_b)
    third = link.spread(third, 1)
    nbr_b = nbr_b.reshape(-1, d)
    ckv_b = (mm(nbr_b, kv_w) + kv_b).astype(BF)
    c_b = cross_fwd(cq[cq_rows:], ckv_own[half_rows:], ckv_b)
    c_b, third = tie(c_b, third)
    third = link.spread(third, 2)
    cctx = shift_later(jnp.concatenate([c_a, c_b], axis=0))
    r2 = r1 + mm(cctx, co_w) + out_b[1]
    h3 = norm(r2, gains[2], shifts[2]).astype(BF)
    turn = lambda x: link.joined(x[:, :hc], x[:, hc:], half, 1)
    win_oth = jnp.concatenate(
        [third[:, i * f8 : (i + 1) * f8].reshape(hc, d) for i in range(ff // d)], axis=1
    )
    wout_oth = third[:, (ff // d) * f8 :].reshape(ffh, d)
    block_out, d_h3, fc_keep, fc_send, gb_low, gb_high = feed(
        jnp.stack([half, core]), turn(h3), cotangent, r2, fc_in, win_oth, b_in, fc_out, wout_oth, b_out
    )

    plane, share = link.plane_sum, link.plane_share

    share_steps = list(share())

    def sum_flow(keep, send):
        steps = list(plane())
        steps[3:3] = [link.meet]
        return Flow((keep, send), steps + [lambda x: share_steps[0](add(*x)[0])] + share_steps[1:])

    fc = sum_flow(fc_keep, fc_send)
    fc.next()
    cot = cotangent.astype(F32)
    back3, gain3, shift3 = norm_back(r2, gains[2], turn(d_h3))
    d_r2 = cot + back3
    z2 = d_r2.astype(BF)
    e = mm(z2, co_w, NT).astype(BF)
    e, z2 = advance([fc], e, z2)
    d_cq, d_own, d_oth = cross_bwd(cq, ckv_own, ckv_a, ckv_b, shift_earlier(e))
    g_co = mm(cctx, z2, TN).astype(BF)
    d_cq, d_own, d_oth, g_co = advance([fc], d_cq, d_own, d_oth, g_co)
    n_oth = mm(d_oth, kv_w, NT).astype(BF).reshape(spans, -1, d)
    d_cq = shift_later(d_cq)
    back2, gain2, shift2 = norm_back(r1, gains[1], mm(d_cq, cq_w, NT))
    d_r1 = d_r2 + back2
    z1 = d_r1.astype(BF)
    f = mm(z1, wo, NT).astype(BF)
    n_oth, f, d_own = advance([fc], n_oth, f, d_own)
    n_back = link.other(n_oth)
    o_rows = d_oth.shape[0] // 2
    g_kv = (
        mm(nbr_own, d_own, TN) + mm(nbr_a, d_oth[:o_rows], TN) + mm(nbr_b, d_oth[o_rows:], TN)
    ).astype(BF)
    g_kv, d_cq, z1, d_own, f = advance([fc], g_kv, d_cq, z1, d_own, f)
    g_cq = mm(h2, d_cq, TN).astype(BF)
    g_wo = mm(ctx, z1, TN).astype(BF)
    sides = (slice(0, hc), slice(hc, d))
    both = lambda parts: jnp.stack([jnp.concatenate(p, axis=0) for p in parts])
    g_cross = both([[g_kv[:, s], g_kv[:, d:][:, s]] for s in sides]), both(
        [[g_cq[:, s], g_co[s][:, :hc], g_co[s][:, hc:]] for s in sides]
    )
    g_cross, g_wo, f, d_own = tie(link.halves(*g_cross), g_wo, f, d_own)
    cross = sum_flow(*g_cross)
    cross.next()
    n_own = mm(d_own, kv_w, NT).reshape(spans, -1, d)
    wide = lambda x: jnp.sum(x.astype(F32), axis=0)
    cqs, cvs = wide(d_cq), wide(d_own[:, d:]) + wide(d_oth[:, d:])
    early = jnp.concatenate(
        [gb_low[0], gb_high[0], wide(cot), wide(d_r1), wide(d_r2), gain2, gain3, shift2, shift3]
        + [link.joined(x[:hc], x[hc:], half) for x in (cqs, cvs)]
    )
    n_own, g_wo, f, early = advance([fc, cross], n_own, g_wo, f, early)
    dq_oth = self_bwd(p_oth, f[:, hc:], ctx_oth, lse_oth, length)
    dq_oth, f = advance([fc, cross], dq_oth, f)
    dq_own = self_bwd(p_own, f[:, :hc], ctx_own, lse_own, length)
    dq_own, d_own, g_wo = advance([fc, cross], dq_own, d_own, g_wo)
    g_qkv = [[mm(h1, part[i], TN).astype(BF) for part in (dq_own, dq_oth)] for i in range(3)]
    g_self = both([[q, k] for q, k in zip(g_qkv[0], g_qkv[1])]), both(
        [[v, g_wo[s][:, :hc], g_wo[s][:, hc:]] for v, s in zip(g_qkv[2], sides)]
    )
    g_self, dq_own, dq_oth = tie(link.halves(*g_self), dq_own, dq_oth)
    own = sum_flow(*g_self)
    own.next()
    flat = lambda x: jnp.concatenate([x[0], x[1], x[2]], axis=1)
    d_h1 = mm(flat(dq_own), qkv_own, NT) + mm(flat(dq_oth), qkv_oth, NT)
    d_h1, n_own, early = advance([own], d_h1, n_own, early)
    nbr_grad = place_blocks(order_of(keep, send), n_own, n_back)
    back1, gain1, shift1 = norm_back(tok, gains[0], d_h1)
    tokens_grad = d_r1 + back1

    late = [gain1, shift1] + [
        link.joined(wide(x), wide(y), half) for x, y in ((dq_own[0], dq_oth[0]), (dq_own[2], dq_oth[2]))
    ]
    natural = jnp.concatenate([early] + late)
    pad = -natural.shape[0] % 1024
    natural = jnp.concatenate([natural, jnp.zeros((pad,), F32)]).reshape(-1, 128)
    every = [lambda x, b=b: x + link.across(x, (b, b)) for b in range(link.bits)]
    every.append(lambda x: x + link.other(x))
    tokens_grad, natural, nbr_grad = advance([fc, cross, own], tokens_grad, natural, nbr_grad)
    while fc.todo:
        advance([fc, cross, own])
    sums = Flow(natural, every)
    sums.next()
    wide_rows = lambda x, n: jnp.concatenate(
        [x[i * (x.shape[0] // n) : (i + 1) * (x.shape[0] // n)] for i in range(n)], axis=1
    )
    s_in, s_out = link.pair(fc.x)
    steps_in = s_in.shape[0] // hc
    fc_in_grad = jnp.concatenate(
        [wide_rows(s_in[:, :hc], steps_in), wide_rows(s_in[:, hc:], steps_in)], axis=1
    ).astype(F32)
    fc_in_grad, s_out = advance([cross, own, sums], fc_in_grad, s_out)
    fc_out_grad = s_out.astype(F32)
    fc_out_grad = advance([cross, own, sums], fc_out_grad)
    while cross.todo:
        advance([cross, own, sums])
    advance([cross, own, sums])
    s_kv, s_rest = link.pair(cross.x)
    cross_kv_grad = jnp.stack([s_kv[:d], s_kv[d:]], axis=1).astype(F32)
    cross_q_grad = s_rest[:d].astype(F32)
    co_grad = wide_rows(s_rest[d:], 2).astype(F32)
    while len(own.todo) > 1 or sums.todo:
        cross_kv_grad, cross_q_grad, co_grad = advance([own, sums], cross_kv_grad, cross_q_grad, co_grad)
    total = sums.x.reshape(-1)
    gb_in = lax.dynamic_slice_in_dim(total[:ff], half * ffh, ffh)
    rest = lax.dynamic_slice_in_dim(total[ff : ff + 13 * d].reshape(-1, d), half * hc, hc, 1)
    while own.todo:
        gb_in, rest = advance([own], gb_in, rest)
    s_qk, s_vw = link.pair(own.x)
    qkv_grad = jnp.stack([s_qk[:d], s_qk[d:], s_vw[:d]], axis=1).astype(F32)
    wo_grad = wide_rows(s_vw[d:], 2).astype(F32)
    pick = lambda *rows: jnp.stack([rest[i] for i in rows])
    return (
        block_out,
        tokens_grad,
        nbr_grad,
        qkv_grad,
        rest[11:13],
        wo_grad,
        cross_q_grad,
        cross_kv_grad,
        rest[7:9],
        co_grad,
        rest[1:3],
        pick(9, 3, 4),
        pick(10, 5, 6),
        fc_in_grad,
        gb_in,
        fc_out_grad,
        rest[0],
    )


def order_of(keep, send):
    return jnp.concatenate([keep, send])


def solution(mesh):
    return jax.shard_map(
        on_device,
        mesh=mesh,
        in_specs=(
            P(("dp", "tp"), None),
            P("dp", "tp", None),
            P("dp", None),
            P("dp", None),
            P(None, None, "tp"),
            P(None, "tp"),
            P("tp", None),
            P(None, "tp"),
            P(None, None, "tp"),
            P(None, "tp"),
            P("tp", None),
            P(None, "tp"),
            P(None, "tp"),
            P(None, "tp"),
            P("tp", None),
            P("tp"),
            P("tp", None),
            P("tp"),
            P(("dp", "tp"), None),
        ),
        out_specs=(
            P(("dp", "tp"), None),
            P(("dp", "tp"), None),
            P("dp", "tp", None),
            P(None, None, "tp"),
            P(None, "tp"),
            P("tp", None),
            P(None, "tp"),
            P(None, None, "tp"),
            P(None, "tp"),
            P("tp", None),
            P(None, "tp"),
            P(None, "tp"),
            P(None, "tp"),
            P("tp", None),
            P("tp"),
            P("tp", None),
            P("tp"),
        ),
        check_vma=False,
    )
```

```python
import functools

import jax
import jax.numpy as jnp
from jax import lax
from jax.experimental import pallas as pl
from jax.experimental.pallas import tpu as pltpu
from jax.sharding import PartitionSpec as P

HEAD = 64
SPAN = 64
LEN = 1024
NBR = 256
EPS = 1e-05
BF = jnp.bfloat16
F32 = jnp.float32
DEAD = -1e30
LN2 = 0.6931471805599453
SCORE = 0.125 / LN2
VMEM_LIMIT = 60 * 1024 * 1024

NN = (((1,), (0,)), ((), ()))
NT = (((1,), (1,)), ((), ()))
TN = (((0,), (0,)), ((), ()))


def mm(a, b, dims=NN):
    return lax.dot_general(a, b, dims, preferred_element_type=F32)


def iota(shape, dim):
    return lax.broadcasted_iota(jnp.int32, shape, dim)


def cost(flops, nbytes, exps=0):
    return pl.CostEstimate(flops=flops, bytes_accessed=nbytes, transcendentals=exps)


def params(n=1):
    return pltpu.CompilerParams(
        dimension_semantics=("arbitrary",) * n, vmem_limit_bytes=VMEM_LIMIT
    )


def three(x):
    hi = x.astype(BF)
    rest = x - hi.astype(F32)
    mid = rest.astype(BF)
    return hi.astype(F32), mid.astype(F32), rest - mid.astype(F32)


def self_fwd_kernel(len_ref, q_ref, k_ref, v_ref, o_ref, lse_ref):
    bq = 512
    length = len_ref[0]
    low = iota((LEN, 128), 1) < HEAD
    lane = iota((LEN, 128), 1)
    q, k, v = (ref[...] for ref in (q_ref, k_ref, v_ref))
    one = jnp.ones((LEN, 128), BF)
    zero = jnp.zeros((LEN, 128), BF)
    dead = jnp.where(iota((LEN, 128), 0) < length, 0.0, DEAD).astype(BF)
    at = lambda x, first: jnp.where(lane == first, x, zero)
    qs = (jnp.where(low, q, at(one, HEAD)), jnp.where(low, at(one, 0), q))
    ks = (jnp.where(low, k, at(dead, HEAD)), jnp.where(low, at(dead, 0), k))
    vs = (jnp.where(low, v, one), jnp.where(low, one, v))
    tri = iota((bq, bq), 1) <= iota((bq, bq), 0)
    low_q = low[:bq]
    for i in range(LEN // bq):
        lo, hi = i * bq, (i + 1) * bq
        outs, tops = [], []
        for h in range(2):
            here = jnp.where(tri, mm(qs[h][lo:hi], ks[h][lo:hi], NT), DEAD)
            m = jnp.max(here, axis=1, keepdims=True)
            if i:
                left = mm(qs[h][lo:hi], ks[h][:lo], NT)
                m = jnp.maximum(m, jnp.max(left, axis=1, keepdims=True))
            o = mm(jnp.exp2(here - m).astype(BF), vs[h][lo:hi])
            if i:
                o += mm(jnp.exp2(left - m).astype(BF), vs[h][:lo])
            outs.append(o)
            tops.append(m)
        a, b = outs
        o_ref[lo:hi, :] = (jnp.where(low_q, a, b) / pltpu.roll(jnp.where(low_q, b, a), HEAD, 1)).astype(BF)
        lse_ref[lo:hi, :] = jnp.where(low_q, tops[1], tops[0]) + jnp.log2(jnp.where(low_q, b, a))


def self_fwd(qkv, length):
    pairs = qkv.shape[1] // 3 // 128
    block = lambda part: pl.BlockSpec((LEN, 128), lambda i, n: (0, part * pairs + i))
    return pl.pallas_call(
        self_fwd_kernel,
        grid_spec=pltpu.PrefetchScalarGridSpec(
            num_scalar_prefetch=1,
            grid=(pairs,),
            in_specs=[block(0), block(1), block(2)],
            out_specs=[block(0), block(0)],
        ),
        out_shape=[
            jax.ShapeDtypeStruct((LEN, pairs * 128), BF),
            jax.ShapeDtypeStruct((LEN, pairs * 128), F32),
        ],
        compiler_params=params(),
        cost_estimate=cost(pairs * 2 * 4 * LEN * LEN * 128, pairs * 8 * LEN * 128),
    )(length, qkv, qkv, qkv)


def self_bwd_kernel(len_ref, q_ref, k_ref, v_ref, f_ref, o_ref, lse_ref, d_ref, dq_ref):
    bk = 256
    length = len_ref[0]
    lane = iota((LEN, 128), 1)
    low = lane < HEAD
    q, k, v, f = (ref[...] for ref in (q_ref, k_ref, v_ref, f_ref))
    zero = jnp.zeros((LEN, 128), BF)
    place = lax.rem(lane, HEAD)
    prod = f.astype(F32) * o_ref[...].astype(F32)
    crossed = jnp.where((iota((128, 128), 0) < HEAD) == (iota((128, 128), 1) < HEAD), 0.0, 1.0).astype(BF)
    prod_hi = prod.astype(BF)
    delta = mm(prod_hi, crossed) + mm((prod - prod_hi.astype(F32)).astype(BF), crossed)

    def free(x, last):
        hi, mid, rest = three(-x)
        out = jnp.where(place == 0, hi, jnp.where(place == 1, mid, jnp.where(place == 2, rest, last)))
        return out.astype(BF)

    q_free = free(lse_ref[...], jnp.where(place == 3, 1.0, 0.0))
    f_free = free(delta, jnp.zeros((LEN, 128), F32))
    dead = jnp.where(iota((LEN, 128), 0) < length, 0.0, DEAD)
    ones = jnp.where(place < 3, 1.0, 0.0)
    k_free = jnp.where(place == 3, dead, ones).astype(BF)
    v_free = ones.astype(BF)
    pick = lambda x, y: (jnp.where(low, x, y), jnp.where(low, y, x))
    qx, fx, kx, vx = pick(q, q_free), pick(f, f_free), pick(k, k_free), pick(v, v_free)
    qs, fs, ks = pick(q, zero), pick(f, zero), pick(k, zero)
    tri = iota((bk, bk), 0) <= iota((bk, bk), 1)
    for j in range(LEN // bk):
        lo, hi = j * bk, (j + 1) * bk
        ps, dss = [], []
        for h in range(2):
            p = jnp.exp2(mm(kx[h][lo:hi], qx[h][lo:], NT))
            first = jnp.where(tri, p[:, :bk], 0.0)
            p = jnp.concatenate([first, p[:, bk:]], axis=1) if hi < LEN else first
            ds = (p * mm(vx[h][lo:hi], fx[h][lo:], NT)).astype(BF)
            ps.append(p.astype(BF))
            dss.append(ds)
        dv = mm(jnp.concatenate(ps, axis=1), jnp.concatenate([fs[0][lo:], fs[1][lo:]], axis=0))
        dk = mm(jnp.concatenate(dss, axis=1), jnp.concatenate([qs[0][lo:], qs[1][lo:]], axis=0))
        kk = jnp.concatenate([ks[0][lo:hi], ks[1][lo:hi]], axis=0)
        part = mm(jnp.concatenate(dss, axis=0), kk, TN)
        if j:
            dq_ref[lo:, :] += part
        else:
            dq_ref[...] = part
        d_ref[1, lo:hi, :] = (dk * LN2).astype(BF)
        d_ref[2, lo:hi, :] = dv.astype(BF)
    d_ref[0] = (dq_ref[...] * 0.125).astype(BF)


def self_bwd(qkv, back, ctx, lse, length):
    pairs = qkv.shape[1] // 3 // 128
    block = lambda part: pl.BlockSpec((LEN, 128), lambda i, n: (0, part * pairs + i))
    return pl.pallas_call(
        self_bwd_kernel,
        grid_spec=pltpu.PrefetchScalarGridSpec(
            num_scalar_prefetch=1,
            grid=(pairs,),
            in_specs=[block(0), block(1), block(2), block(0), block(0), block(0)],
            out_specs=pl.BlockSpec((3, LEN, 128), lambda i, n: (0, 0, i)),
            scratch_shapes=[pltpu.VMEM((LEN, 128), F32)],
        ),
        out_shape=jax.ShapeDtypeStruct((3, LEN, pairs * 128), BF),
        compiler_params=params(),
        cost_estimate=cost(pairs * 2 * 10 * LEN * LEN * 128, pairs * 16 * LEN * 128),
    )(length, qkv, qkv, qkv, back, ctx, lse)


PER_STEP = 4


def own_heads():
    return jnp.where(iota((256, 256), 0) // SPAN == iota((256, 256), 1) // HEAD, 1.0, 0.0).astype(BF)


def spread(rows, mask):
    return jnp.concatenate([rows] * 4, axis=0) * mask


def gathered(rows, lanes):
    out = jnp.where(lanes == 0, rows[:SPAN], 0.0)
    for g in range(1, 4):
        out = jnp.where(lanes == g, rows[g * SPAN : (g + 1) * SPAN], out)
    return out


def fours(count, width, rows):
    for u in range(count):
        for t in range(width // 256):
            yield slice(u * SPAN, (u + 1) * SPAN), slice(u * rows, (u + 1) * rows), t * 256


def cross_fwd_kernel(q_ref, own_ref, oth_ref, o_ref):
    width = q_ref.shape[1]
    rows = own_ref.shape[0] // PER_STEP
    mask = own_heads()
    lanes = iota((SPAN, 256), 1) // HEAD
    one = jnp.ones((2 * rows, 128), BF)
    both = lambda at, lo: jnp.concatenate(
        [own_ref[at, lo : lo + 256], oth_ref[at, lo : lo + 256]], axis=0
    )
    jobs = list(fours(PER_STEP, width, rows))
    scores = [mm(spread(q_ref[q, lo : lo + 256], mask), both(kv, lo), NT) for q, kv, lo in jobs]
    probs = [jnp.exp2(s - jnp.max(s, axis=1, keepdims=True)).astype(BF) for s in scores]
    for p, (q, kv, lo) in zip(probs, jobs):
        o = mm(p, both(kv, width + lo))
        total = 1.0 / mm(p, one)
        o = o * jnp.concatenate([total, total], axis=1)
        o_ref[q, lo : lo + 256] = gathered(o, lanes).astype(BF)


def cross_fwd(q, own, oth):
    width = q.shape[1]
    spans = q.shape[0] // SPAN
    rows = own.shape[0] // spans
    row = pl.BlockSpec((PER_STEP * SPAN, width), lambda i: (i, 0))
    kv = pl.BlockSpec((PER_STEP * rows, 2 * width), lambda i: (i, 0))
    return pl.pallas_call(
        cross_fwd_kernel,
        grid=(spans // PER_STEP,),
        in_specs=[row, kv, kv],
        out_specs=row,
        out_shape=jax.ShapeDtypeStruct(q.shape, BF),
        compiler_params=params(),
        cost_estimate=cost(spans * 3 * 4 * 256**3, spans * 1000000),
    )(q, own, oth)


def cross_bwd_kernel(q_ref, own_ref, oth_a_ref, oth_b_ref, e_ref, dq_ref, down_ref, doth_ref):
    width = q_ref.shape[1]
    rows = own_ref.shape[0] // PER_STEP
    early = pl.program_id(0) < pl.num_programs(0) // 2
    oth = jnp.where(early, oth_a_ref[...], oth_b_ref[...])
    mask = own_heads()
    lanes = iota((SPAN, 256), 1) // HEAD
    both = lambda at, lo: jnp.concatenate([own_ref[at, lo : lo + 256], oth[at, lo : lo + 256]], axis=0)
    jobs = list(fours(PER_STEP, width, rows))
    q4 = [spread(q_ref[q, lo : lo + 256], mask) for q, kv, lo in jobs]
    e4 = [spread(e_ref[q, lo : lo + 256], mask) for q, kv, lo in jobs]
    scores = [mm(both(kv, lo), x, NT) for x, (q, kv, lo) in zip(q4, jobs)]
    backs = [mm(both(kv, width + lo), x, NT) for x, (q, kv, lo) in zip(e4, jobs)]
    for s, dp, x, y, (q, kv, lo) in zip(scores, backs, q4, e4, jobs):
        p = jnp.exp2(s - jnp.max(s, axis=0, keepdims=True))
        p = p * (1.0 / jnp.sum(p, axis=0, keepdims=True))
        delta = jnp.sum(p * dp, axis=0, keepdims=True)
        ds = (p * (dp - delta)).astype(BF)
        dk = (mm(ds, x) * LN2).astype(BF)
        dv = mm(p.astype(BF), y).astype(BF)
        down_ref[kv, lo : lo + 256] = dk[:rows]
        doth_ref[kv, lo : lo + 256] = dk[rows:]
        down_ref[kv, width + lo : width + lo + 256] = dv[:rows]
        doth_ref[kv, width + lo : width + lo + 256] = dv[rows:]
        dq_ref[q, lo : lo + 256] = (gathered(mm(ds, both(kv, lo), TN), lanes) * 0.125).astype(BF)


def cross_bwd(q, own, oth_a, oth_b, e):
    width = q.shape[1]
    spans = q.shape[0] // SPAN
    rows = own.shape[0] // spans
    steps = spans // PER_STEP
    row = pl.BlockSpec((PER_STEP * SPAN, width), lambda i: (i, 0))
    shape = (PER_STEP * rows, 2 * width)
    kv = pl.BlockSpec(shape, lambda i: (i, 0))
    return pl.pallas_call(
        cross_bwd_kernel,
        grid=(steps,),
        in_specs=[
            row,
            kv,
            pl.BlockSpec(shape, lambda i: (jnp.minimum(i, steps // 2 - 1), 0)),
            pl.BlockSpec(shape, lambda i: (jnp.maximum(i - steps // 2, 0), 0)),
            row,
        ],
        out_specs=[row, kv, kv],
        out_shape=[
            jax.ShapeDtypeStruct(q.shape, BF),
            jax.ShapeDtypeStruct(own.shape, BF),
            jax.ShapeDtypeStruct(own.shape, BF),
        ],
        compiler_params=params(),
        cost_estimate=cost(spans * 3 * 10 * 256**3, spans * 2000000),
    )(q, own, oth_a, oth_b, e)


def pick_kernel(keep_ref, send_ref, blocks_ref, keep_out, send_out, sems):
    count = keep_out.shape[0]
    copies = []
    for i in range(count):
        copies.append(
            pltpu.make_async_copy(blocks_ref.at[send_ref[i]], send_out.at[i], sems.at[0, i])
        )
    for i in range(count):
        copies.append(
            pltpu.make_async_copy(blocks_ref.at[keep_ref[i]], keep_out.at[i], sems.at[1, i])
        )
    for copy in copies:
        copy.start()
    for copy in copies:
        copy.wait()


def pick_blocks(neighbours, keep, send):
    count = keep.shape[0]
    smem = pl.BlockSpec(memory_space=pltpu.SMEM)
    anywhere = pl.BlockSpec(memory_space=pl.ANY)
    vmem = pl.BlockSpec(memory_space=pltpu.VMEM)
    return pl.pallas_call(
        pick_kernel,
        in_specs=[smem, smem, anywhere],
        out_specs=[vmem, vmem],
        out_shape=[jax.ShapeDtypeStruct((count,) + neighbours.shape[1:], BF)] * 2,
        scratch_shapes=[pltpu.SemaphoreType.DMA((2, count))],
        compiler_params=pltpu.CompilerParams(vmem_limit_bytes=VMEM_LIMIT),
        cost_estimate=cost(0, 4 * neighbours.size),
    )(keep, send, neighbours)


def pack_kernel(where_ref, qkv, kv, cq, wo, co, fin, fout, first, second, third, sems):
    core, p = where_ref[0], where_ref[1]
    d, hc = cq.shape
    e8, w8, o8 = d // 8, wo.shape[0] // 8, fout.shape[0] // 8
    take = lambda at, n: pl.ds(pl.multiple_of(at * n, 16), n)
    jobs = [(qkv.at[take(core, d // 2)], first)]
    to = 0
    for ref, count, n in ((kv, 2, e8), (cq, 1, e8), (wo, 2, w8), (co, 2, w8)):
        for i in range(count):
            jobs.append((ref.at[take(p, n), pl.ds(i * hc, hc)], second.at[pl.ds(to, n)]))
            to += n
    to = 0
    for i in range(fin.shape[1] // d):
        jobs.append((fin.at[take(p, w8), pl.ds(i * d, d)], third.at[pl.ds(to, w8)]))
        to += w8
    jobs.append((fout.at[take(p, o8)], third.at[pl.ds(to, o8)]))
    copies = [pltpu.make_async_copy(a, b, sems.at[i]) for i, (a, b) in enumerate(jobs)]
    for copy in copies:
        copy.start()
    for copy in copies:
        copy.wait()


def pack_weights(where, qkv, kv, cq, wo, co, fin, fout):
    anywhere = pl.BlockSpec(memory_space=pl.ANY)
    vmem = pl.BlockSpec(memory_space=pltpu.VMEM)
    d, hc = cq.shape
    n_in = fin.shape[1] // d
    return pl.pallas_call(
        pack_kernel,
        in_specs=[pl.BlockSpec(memory_space=pltpu.SMEM)] + [anywhere] * 7,
        out_specs=[vmem, vmem, vmem],
        out_shape=[
            jax.ShapeDtypeStruct((d // 2, 3 * hc), BF),
            jax.ShapeDtypeStruct((3 * (d // 8) + 4 * (wo.shape[0] // 8), hc), BF),
            jax.ShapeDtypeStruct((n_in * (fin.shape[0] // 8) + fout.shape[0] // 8, d), BF),
        ],
        scratch_shapes=[pltpu.SemaphoreType.DMA((9 + n_in,))],
        compiler_params=pltpu.CompilerParams(vmem_limit_bytes=VMEM_LIMIT),
        cost_estimate=cost(0, 4 * 1024 * 1024),
    )(where, qkv, kv, cq, wo, co, fin, fout)


def place_kernel(order_ref, mine_ref, theirs_ref, out_ref, wide, sems):
    count = mine_ref.shape[0]
    copies = []
    for i in range(count):
        copy = pltpu.make_async_copy(mine_ref.at[i], out_ref.at[order_ref[i]], sems.at[i])
        copy.start()
        copies.append(copy)
    for i in range(count):
        wide[i] = theirs_ref[i].astype(F32)
        copy = pltpu.make_async_copy(
            wide.at[i], out_ref.at[order_ref[count + i]], sems.at[count + i]
        )
        copy.start()
        copies.append(copy)
    for copy in copies:
        copy.wait()


def place_blocks(order, mine, theirs):
    count = order.shape[0]
    return pl.pallas_call(
        place_kernel,
        in_specs=[
            pl.BlockSpec(memory_space=pltpu.SMEM),
            pl.BlockSpec(memory_space=pltpu.VMEM),
            pl.BlockSpec(memory_space=pltpu.VMEM),
        ],
        out_specs=pl.BlockSpec(memory_space=pl.ANY),
        out_shape=jax.ShapeDtypeStruct((count,) + mine.shape[1:], F32),
        scratch_shapes=[
            pltpu.VMEM(mine.shape, F32),
            pltpu.SemaphoreType.DMA((count,)),
        ],
        compiler_params=pltpu.CompilerParams(vmem_limit_bytes=VMEM_LIMIT),
        cost_estimate=cost(0, 8 * mine.size),
    )(order, mine, theirs)


GELU_A = 0.7978845608028654
GELU_B = 0.044715


def feed_kernel(
    half_ref, h_ref, g_ref, r_ref, aa_ref, ab_ref, ba_ref, bb_ref, bina_ref, binb_ref,
    wouta_ref, woutb_ref, bout_ref,
    out_ref, dh_ref, keep_ref, send_ref, gbina_ref, gbinb_ref, h_t, acc, dacc, act_s, dpre_s,
):
    step = pl.program_id(0)
    hc = aa_ref.shape[0]
    bf = aa_ref.shape[1]

    @pl.when(step == 0)
    def _():
        h_t[...] = h_ref[...].T

    win = jnp.concatenate(
        [
            jnp.concatenate([aa_ref[...], ab_ref[...]], axis=1),
            jnp.concatenate([ba_ref[...], bb_ref[...]], axis=1),
        ],
        axis=0,
    )
    here = half_ref[0] == 0
    wa, wb = wouta_ref[...], woutb_ref[...]
    wout = jnp.concatenate([jnp.where(here, wa, wb), jnp.where(here, wb, wa)], axis=0)
    bias = jnp.concatenate([bina_ref[...], binb_ref[...]], axis=1)
    rows = h_ref.shape[0]
    first = step == 0
    total = jnp.zeros(bias.shape, F32)
    for lo in range(0, rows, 256):
        at = slice(lo, lo + 256)
        pre = mm(h_ref[at], win) + bias
        dact = mm(g_ref[at], wout, NT)
        square = pre * pre
        th = jnp.tanh(pre * (GELU_A + GELU_A * GELU_B * square))
        half = 0.5 + 0.5 * th
        act = (pre * half).astype(BF)
        slope = half + pre * (half - half * th) * (GELU_A + 3.0 * GELU_A * GELU_B * square)
        dpre = (dact * slope).astype(BF)
        total += jnp.sum(dpre.astype(F32), axis=0, keepdims=True)
        act_s[at] = act
        dpre_s[at] = dpre
        acc[at] = jnp.where(first, 0.0, acc[at]) + mm(act, wout)
        dacc[at] = jnp.where(first, 0.0, dacc[at]) + mm(dpre, win, NT)
    gbina_ref[0:1, :] = total[:, :bf]
    gbinb_ref[0:1, :] = total[:, bf:]
    gout = mm(act_s[...], g_ref[...], TN).astype(BF)
    gin = mm(h_t[...], dpre_s[...]).astype(BF)

    def put(into_in, into_out):
        into_in[0], into_in[1] = gin[:hc], gin[hc:]
        into_out[0] = jnp.where(here, gout[:bf], gout[bf:])
        into_out[1] = jnp.where(here, gout[bf:], gout[:bf])

    @pl.when(half_ref[1] == 0)
    def _():
        put(keep_ref, send_ref)

    @pl.when(half_ref[1] != 0)
    def _():
        put(send_ref, keep_ref)

    @pl.when(step == pl.num_programs(0) - 1)
    def _():
        out_ref[...] = (r_ref[...] + acc[...] + bout_ref[...]).astype(BF)
        dh_ref[...] = dacc[...]


def feed(where, h, g, r, win_own, win_oth, b_in, wout_own, wout_oth, b_out):
    rows, d = h.shape
    hc = win_own.shape[0]
    ff = win_own.shape[1]
    bf = 384
    n = ff // 2 // bf
    lower = lambda i, p: i
    upper = lambda i, p: n + i
    whole = pl.BlockSpec((rows, d), lambda i, p: (0, 0))
    side = lambda height, which: pl.BlockSpec((height, bf), lambda i, p: (0, which(i, p)))
    grad = pl.BlockSpec((2, bf, d), lambda i, p: (0, i, 0))
    wout = pl.BlockSpec((bf, d), lambda i, p: (i, 0))
    gb = pl.BlockSpec((8, bf), lambda i, p: (0, i))
    return pl.pallas_call(
        feed_kernel,
        grid_spec=pltpu.PrefetchScalarGridSpec(
            num_scalar_prefetch=1,
            grid=(n,),
            in_specs=[
                whole, whole, whole,
                side(hc, lower), side(hc, upper), side(hc, lower), side(hc, upper), side(1, lower), side(1, upper),
                wout, wout,
                pl.BlockSpec((1, d), lambda i, p: (0, 0)),
            ],
            out_specs=[whole, whole, grad, grad, gb, gb],
            scratch_shapes=[
                pltpu.VMEM((d, rows), BF),
                pltpu.VMEM((rows, d), F32),
                pltpu.VMEM((rows, d), F32),
                pltpu.VMEM((rows, 2 * bf), BF),
                pltpu.VMEM((rows, 2 * bf), BF),
            ],
        ),
        out_shape=[
            jax.ShapeDtypeStruct((rows, d), BF),
            jax.ShapeDtypeStruct((rows, d), F32),
            jax.ShapeDtypeStruct((2, ff // 2, d), BF),
            jax.ShapeDtypeStruct((2, ff // 2, d), BF),
            jax.ShapeDtypeStruct((8, ff // 2), F32),
            jax.ShapeDtypeStruct((8, ff // 2), F32),
        ],
        compiler_params=params(),
        cost_estimate=cost(12 * rows * d * ff, 8 * d * ff),
    )(where, h, g, r, win_own, win_own, win_oth, win_oth, b_in, b_in, wout_own, wout_oth, b_out)


def norm(rows, gain, bias):
    mean = jnp.mean(rows, axis=-1, keepdims=True)
    centred = rows - mean
    spread_ = jnp.mean(centred * centred, axis=-1, keepdims=True)
    return centred * lax.rsqrt(spread_ + EPS) * gain + bias


def norm_back(rows, gain, grad):
    mean = jnp.mean(rows, axis=-1, keepdims=True)
    centred = rows - mean
    rstd = lax.rsqrt(jnp.mean(centred * centred, axis=-1, keepdims=True) + EPS)
    hat = centred * rstd
    scaled = grad * gain
    inner = jnp.mean(scaled * hat, axis=-1, keepdims=True)
    back = rstd * (scaled - jnp.mean(scaled, axis=-1, keepdims=True) - hat * inner)
    return back, jnp.sum(grad * hat, axis=0), jnp.sum(grad, axis=0)


class Links:
    def __init__(self, dp, tp):
        self.dp = dp
        self.bits = dp.bit_length() - 1
        self.me = lax.axis_index("dp")
        self.core = self.me & 1
        self.half = lax.axis_index("tp")
        self.swap = [(i, tp - 1 - i) for i in range(tp)]
        rest = list(range(1, self.bits))
        turned = [2, 1] + rest[2:] if self.bits > 2 else rest
        self.steps = list(zip(rest, turned))

    def other(self, x):
        return lax.ppermute(x, "tp", self.swap)

    def across(self, x, step):
        return lax.ppermute(x, "dp", [(i, i ^ (1 << step[i & 1])) for i in range(self.dp)])

    def flag(self, step):
        return (self.me >> jnp.where(self.core == 0, step[0], step[1])) & 1

    def joined(self, mine, theirs, flag, axis=0):
        first = flag == 0
        return jnp.concatenate(
            [jnp.where(first, mine, theirs), jnp.where(first, theirs, mine)], axis=axis
        )

    def piece(self):
        return self.core * 4 + self.flag(self.steps[1]) * 2 + self.flag(self.steps[0])

    def spread(self, x, i):
        step = ([*self.steps[:2], (0, 0)])[i]
        return self.joined(x, self.across(x, step), self.flag(step))

    def fold(self, x, step):
        flag = self.flag(step)
        rows = x[0].shape[1] // 2
        part = lambda at: add(*(lax.dynamic_slice_in_dim(y, at * rows, rows, 1) for y in x))
        return part(flag), self.across(part(1 - flag), step)

    def meet(self, x):
        send = add(*(y[1:] for y in x))
        return add(*(y[:1] for y in x)), self.other(send)

    def halves(self, a, b):
        return jnp.where(self.core == 0, a, b), jnp.where(self.core == 0, b, a)

    def plane_sum(self):
        yield lambda x: (x[0], self.across(x[1], (0, 0)))
        for step in self.steps:
            yield functools.partial(self.fold, step=step)

    def plane_share(self):
        before = None
        for step in (*reversed(self.steps), (0, 0)):
            yield functools.partial(self.widen, before=before, step=step)
            before = step

    def widen(self, x, before, step):
        if before is not None:
            x = self.joined(*x, self.flag(before))
        return x, self.across(x, step)

    def pair(self, x):
        mine, theirs = x
        return jnp.where(self.core == 0, mine, theirs), jnp.where(self.core == 0, theirs, mine)


def add(a, b):
    return (a.astype(F32) + b.astype(F32)).astype(BF)


def tie(*arrays):
    return lax.optimization_barrier(arrays)


class Flow:
    def __init__(self, x, todo):
        self.x, self.todo = x, list(todo)

    def next(self):
        if self.todo:
            self.x = self.todo.pop(0)(self.x)


def advance(flows, *arrays):
    done = lax.optimization_barrier(([f.x for f in flows], *arrays))
    for f, x in zip(flows, done[0]):
        f.x = x
        f.next()
    return done[1] if len(arrays) == 1 else done[1:]


def shift_earlier(x):
    pad = jnp.zeros((SPAN - 1, x.shape[1]), x.dtype)
    return jnp.concatenate([x[SPAN - 1 :], pad], axis=0)


def shift_later(x):
    pad = jnp.zeros((SPAN - 1, x.shape[1]), x.dtype)
    return jnp.concatenate([pad, x[: x.shape[0] - SPAN + 1]], axis=0)


def on_device(
    tokens, neighbours, nbr_index, lengths, w_qkv, qv_bias, w_out, cross_q, cross_kv,
    cross_bias, cross_out, out_bias, ln_gain, ln_bias, fc_in, fc_in_bias, fc_out,
    fc_out_bias, cotangent,
):
    tp = lax.axis_size("tp")
    link = Links(lax.axis_size("dp"), tp)
    half = link.half
    d = tokens.shape[1]
    hc = w_qkv.shape[2]
    ffh = fc_in_bias.shape[0]
    ff = ffh * tp
    spans = nbr_index.shape[1] // tp
    length = lax.dynamic_slice_in_dim(lengths[0], half, 1)
    core = link.core

    small = jnp.concatenate(
        [fc_in_bias.reshape(-1, hc), fc_out_bias.reshape(1, hc), out_bias, ln_gain, ln_bias, qv_bias, cross_bias],
        axis=0,
    )
    small_oth = link.other(small)
    qkv_own = w_qkv.reshape(d, 3 * hc)
    eighth, w8, f8 = d // 8, hc // 8, hc // 8
    place = jnp.stack([core, link.piece()])
    first, second, third = pack_weights(
        place, qkv_own, cross_kv.reshape(d, 2 * hc), cross_q, w_out, cross_out, fc_in, fc_out
    )
    first = link.other(first)
    second = link.other(second)[None]

    order = nbr_index[0]
    keep = lax.dynamic_slice_in_dim(order, half * spans, spans)
    send = lax.dynamic_slice_in_dim(order, (1 - half) * spans, spans)
    nbr_own, nbr_send = pick_blocks(neighbours, keep, send)

    def whole(at, count, natural=True):
        a, b = small[at : at + count], small_oth[at : at + count]
        if natural:
            return link.joined(a, b, half, 1).astype(F32)
        return a.astype(F32), b.astype(F32)

    at = ffh // hc
    b_in = link.joined(small[:at].reshape(1, ffh), small_oth[:at].reshape(1, ffh), half, 1).astype(F32)
    b_out = whole(at, 1)
    out_b = whole(at + 1, 2)
    gains = whole(at + 3, 3)
    shifts = whole(at + 6, 3)
    qv_b = whole(at + 9, 2, False)
    cross_b = whole(at + 11, 2, False)

    tok = tokens.astype(F32)
    h1 = norm(tok, gains[0], shifts[0]).astype(BF)

    def project(w, which):
        bias = jnp.concatenate([qv_b[which][0], jnp.zeros((hc,), F32), qv_b[which][1]])
        scale = jnp.concatenate([jnp.full((hc,), SCORE, F32), jnp.ones((2 * hc,), F32)])
        return ((mm(h1, w) + bias) * scale).astype(BF)

    p_own = project(qkv_own, 0)
    ctx_own, lse_own = self_fwd(p_own, length)
    first, ctx_own, second, third, nbr_send = tie(first, ctx_own, second, third, nbr_send)
    qkv_pair = link.across(first, (0, 0))
    second = link.spread(second, 0)
    cutoff = spans // 2
    nbr_a = link.other(nbr_send[:cutoff])
    qkv_oth = link.joined(first, qkv_pair, core)
    p_oth = project(qkv_oth, 1)
    p_oth, second = tie(p_oth, second)
    second = link.spread(second, 1)
    ctx_oth, lse_oth = self_fwd(p_oth, length)
    ctx_oth, second, nbr_a, nbr_send, third = tie(ctx_oth, second, nbr_a, nbr_send, third)
    second = link.spread(second, 2)
    third = link.other(third)[None]
    nbr_b = link.other(nbr_send[cutoff:])

    rows = lambda lo, n: second[:, lo : lo + n].reshape(8 * n, hc)
    ctx = jnp.concatenate([ctx_own, ctx_oth], axis=1)
    pair = lambda at: jnp.concatenate([rows(at, w8), rows(at + w8, w8)], axis=1)
    wo = jnp.concatenate([w_out, pair(3 * eighth)], axis=0)
    co_w = jnp.concatenate([cross_out, pair(3 * eighth + 2 * w8)], axis=0)
    cq_w = jnp.concatenate([cross_q, rows(2 * eighth, eighth)], axis=1)
    kv_w = jnp.concatenate(
        [cross_kv[:, 0], rows(0, eighth), cross_kv[:, 1], rows(eighth, eighth)], axis=1
    )
    r1 = tok + mm(ctx, wo) + out_b[0]
    h2 = norm(r1, gains[1], shifts[1]).astype(BF)
    cb = [jnp.concatenate([cross_b[0][i], cross_b[1][i]]) for i in range(2)]
    cq = shift_earlier(((mm(h2, cq_w) + cb[0]) * SCORE).astype(BF))
    kv_b = jnp.concatenate([jnp.zeros((d,), F32), cb[1]])
    nbr_own = nbr_own.reshape(-1, d)
    ckv_own = (mm(nbr_own, kv_w) + kv_b).astype(BF)
    cq, ckv_own, third = tie(cq, ckv_own, third)
    third = link.spread(third, 0)
    half_rows = ckv_own.shape[0] // 2
    nbr_a = nbr_a.reshape(-1, d)
    ckv_a = (mm(nbr_a, kv_w) + kv_b).astype(BF)
    cq_rows = cutoff * SPAN
    c_a = cross_fwd(cq[:cq_rows], ckv_own[:half_rows], ckv_a)
    c_a, third, nbr_b = tie(c_a, third, nbr_b)
    third = link.spread(third, 1)
    nbr_b = nbr_b.reshape(-1, d)
    ckv_b = (mm(nbr_b, kv_w) + kv_b).astype(BF)
    c_b = cross_fwd(cq[cq_rows:], ckv_own[half_rows:], ckv_b)
    c_b, third = tie(c_b, third)
    third = link.spread(third, 2)
    cctx = shift_later(jnp.concatenate([c_a, c_b], axis=0))
    r2 = r1 + mm(cctx, co_w) + out_b[1]
    h3 = norm(r2, gains[2], shifts[2]).astype(BF)
    turn = lambda x: link.joined(x[:, :hc], x[:, hc:], half, 1)
    win_oth = jnp.concatenate(
        [third[:, i * f8 : (i + 1) * f8].reshape(hc, d) for i in range(ff // d)], axis=1
    )
    wout_oth = third[:, (ff // d) * f8 :].reshape(ffh, d)
    block_out, d_h3, fc_keep, fc_send, gb_low, gb_high = feed(
        jnp.stack([half, core]), turn(h3), cotangent, r2, fc_in, win_oth, b_in, fc_out, wout_oth, b_out
    )

    plane, share = link.plane_sum, link.plane_share

    share_steps = list(share())

    def sum_flow(keep, send):
        steps = list(plane())
        steps[3:3] = [link.meet]
        return Flow((keep, send), steps + [lambda x: share_steps[0](add(*x)[0])] + share_steps[1:])

    fc = sum_flow(fc_keep, fc_send)
    fc.next()
    cot = cotangent.astype(F32)
    back3, gain3, shift3 = norm_back(r2, gains[2], turn(d_h3))
    d_r2 = cot + back3
    z2 = d_r2.astype(BF)
    e = mm(z2, co_w, NT).astype(BF)
    e, z2 = advance([fc], e, z2)
    d_cq, d_own, d_oth = cross_bwd(cq, ckv_own, ckv_a, ckv_b, shift_earlier(e))
    g_co = mm(cctx, z2, TN).astype(BF)
    d_cq, d_own, d_oth, g_co = advance([fc], d_cq, d_own, d_oth, g_co)
    n_oth = mm(d_oth, kv_w, NT).astype(BF).reshape(spans, -1, d)
    d_cq = shift_later(d_cq)
    back2, gain2, shift2 = norm_back(r1, gains[1], mm(d_cq, cq_w, NT))
    d_r1 = d_r2 + back2
    z1 = d_r1.astype(BF)
    f = mm(z1, wo, NT).astype(BF)
    n_oth, f, d_own = advance([fc], n_oth, f, d_own)
    n_back = link.other(n_oth)
    o_rows = d_oth.shape[0] // 2
    g_kv = (
        mm(nbr_own, d_own, TN) + mm(nbr_a, d_oth[:o_rows], TN) + mm(nbr_b, d_oth[o_rows:], TN)
    ).astype(BF)
    g_kv, d_cq, z1, d_own, f = advance([fc], g_kv, d_cq, z1, d_own, f)
    g_cq = mm(h2, d_cq, TN).astype(BF)
    g_wo = mm(ctx, z1, TN).astype(BF)
    sides = (slice(0, hc), slice(hc, d))
    both = lambda parts: jnp.stack([jnp.concatenate(p, axis=0) for p in parts])
    g_cross = both([[g_kv[:, s], g_kv[:, d:][:, s]] for s in sides]), both(
        [[g_cq[:, s], g_co[s][:, :hc], g_co[s][:, hc:]] for s in sides]
    )
    g_cross, g_wo, f, d_own = tie(link.halves(*g_cross), g_wo, f, d_own)
    cross = sum_flow(*g_cross)
    cross.next()
    n_own = mm(d_own, kv_w, NT).reshape(spans, -1, d)
    wide = lambda x: jnp.sum(x.astype(F32), axis=0)
    cqs, cvs = wide(d_cq), wide(d_own[:, d:]) + wide(d_oth[:, d:])
    early = jnp.concatenate(
        [gb_low[0], gb_high[0], wide(cot), wide(d_r1), wide(d_r2), gain2, gain3, shift2, shift3]
        + [link.joined(x[:hc], x[hc:], half) for x in (cqs, cvs)]
    )
    n_own, g_wo, f, early = advance([fc, cross], n_own, g_wo, f, early)
    dq_oth = self_bwd(p_oth, f[:, hc:], ctx_oth, lse_oth, length)
    dq_oth, f = advance([fc, cross], dq_oth, f)
    dq_own = self_bwd(p_own, f[:, :hc], ctx_own, lse_own, length)
    dq_own, d_own, g_wo = advance([fc, cross], dq_own, d_own, g_wo)
    g_qkv = [[mm(h1, part[i], TN).astype(BF) for part in (dq_own, dq_oth)] for i in range(3)]
    g_self = both([[q, k] for q, k in zip(g_qkv[0], g_qkv[1])]), both(
        [[v, g_wo[s][:, :hc], g_wo[s][:, hc:]] for v, s in zip(g_qkv[2], sides)]
    )
    g_self, dq_own, dq_oth = tie(link.halves(*g_self), dq_own, dq_oth)
    own = sum_flow(*g_self)
    own.next()
    flat = lambda x: jnp.concatenate([x[0], x[1], x[2]], axis=1)
    d_h1 = mm(flat(dq_own), qkv_own, NT) + mm(flat(dq_oth), qkv_oth, NT)
    d_h1, n_own, early = advance([own], d_h1, n_own, early)
    nbr_grad = place_blocks(order_of(keep, send), n_own, n_back)
    back1, gain1, shift1 = norm_back(tok, gains[0], d_h1)
    tokens_grad = d_r1 + back1

    late = [gain1, shift1] + [
        link.joined(wide(x), wide(y), half) for x, y in ((dq_own[0], dq_oth[0]), (dq_own[2], dq_oth[2]))
    ]
    natural = jnp.concatenate([early] + late)
    pad = -natural.shape[0] % 1024
    natural = jnp.concatenate([natural, jnp.zeros((pad,), F32)]).reshape(-1, 128)
    def total_of(x, move):
        x = x[0] + x[1] if isinstance(x, tuple) else x
        return x, move(x)

    every = [
        functools.partial(total_of, move=functools.partial(link.across, step=(b, b))) for b in range(link.bits)
    ] + [functools.partial(total_of, move=link.other)]
    tokens_grad, natural, nbr_grad = advance([fc, cross, own], tokens_grad, natural, nbr_grad)
    while fc.todo:
        advance([fc, cross, own])
    sums = Flow(natural, every)
    sums.next()
    wide_rows = lambda x, n: jnp.concatenate(
        [x[i * (x.shape[0] // n) : (i + 1) * (x.shape[0] // n)] for i in range(n)], axis=1
    )
    s_in, s_out = link.pair(fc.x)
    steps_in = s_in.shape[0] // hc
    fc_in_grad = jnp.concatenate(
        [wide_rows(s_in[:, :hc], steps_in), wide_rows(s_in[:, hc:], steps_in)], axis=1
    ).astype(F32)
    fc_in_grad, s_out = advance([cross, own, sums], fc_in_grad, s_out)
    fc_out_grad = s_out.astype(F32)
    fc_out_grad = advance([cross, own, sums], fc_out_grad)
    while cross.todo:
        advance([cross, own, sums])
    advance([cross, own, sums])
    s_kv, s_rest = link.pair(cross.x)
    cross_kv_grad = jnp.stack([s_kv[:d], s_kv[d:]], axis=1).astype(F32)
    cross_q_grad = s_rest[:d].astype(F32)
    co_grad = wide_rows(s_rest[d:], 2).astype(F32)
    while len(own.todo) > 1 or sums.todo:
        cross_kv_grad, cross_q_grad, co_grad = advance([own, sums], cross_kv_grad, cross_q_grad, co_grad)
    total = (sums.x[0] + sums.x[1]).reshape(-1)
    gb_in = lax.dynamic_slice_in_dim(total[:ff], half * ffh, ffh)
    rest = lax.dynamic_slice_in_dim(total[ff : ff + 13 * d].reshape(-1, d), half * hc, hc, 1)
    while own.todo:
        gb_in, rest = advance([own], gb_in, rest)
    s_qk, s_vw = link.pair(own.x)
    qkv_grad = jnp.stack([s_qk[:d], s_qk[d:], s_vw[:d]], axis=1).astype(F32)
    wo_grad = wide_rows(s_vw[d:], 2).astype(F32)
    pick = lambda *rows: jnp.stack([rest[i] for i in rows])
    return (
        block_out,
        tokens_grad,
        nbr_grad,
        qkv_grad,
        rest[11:13],
        wo_grad,
        cross_q_grad,
        cross_kv_grad,
        rest[7:9],
        co_grad,
        rest[1:3],
        pick(9, 3, 4),
        pick(10, 5, 6),
        fc_in_grad,
        gb_in,
        fc_out_grad,
        rest[0],
    )


def order_of(keep, send):
    return jnp.concatenate([keep, send])


def solution(mesh):
    return jax.shard_map(
        on_device,
        mesh=mesh,
        in_specs=(
            P(("dp", "tp"), None),
            P("dp", "tp", None),
            P("dp", None),
            P("dp", None),
            P(None, None, "tp"),
            P(None, "tp"),
            P("tp", None),
            P(None, "tp"),
            P(None, None, "tp"),
            P(None, "tp"),
            P("tp", None),
            P(None, "tp"),
            P(None, "tp"),
            P(None, "tp"),
            P("tp", None),
            P("tp"),
            P("tp", None),
            P("tp"),
            P(("dp", "tp"), None),
        ),
        out_specs=(
            P(("dp", "tp"), None),
            P(("dp", "tp"), None),
            P("dp", "tp", None),
            P(None, None, "tp"),
            P(None, "tp"),
            P("tp", None),
            P(None, "tp"),
            P(None, None, "tp"),
            P(None, "tp"),
            P("tp", None),
            P(None, "tp"),
            P(None, "tp"),
            P(None, "tp"),
            P("tp", None),
            P("tp"),
            P("tp", None),
            P("tp"),
        ),
        check_vma=False,
    )
```

```python
import functools

import jax
import jax.numpy as jnp
from jax import lax
from jax.experimental import pallas as pl
from jax.experimental.pallas import tpu as pltpu
from jax.sharding import PartitionSpec as P

HEAD = 64
SPAN = 64
LEN = 1024
NBR = 256
EPS = 1e-05
BF = jnp.bfloat16
F32 = jnp.float32
DEAD = -1e30
LN2 = 0.6931471805599453
SCORE = 0.125 / LN2
VMEM_LIMIT = 60 * 1024 * 1024

NN = (((1,), (0,)), ((), ()))
NT = (((1,), (1,)), ((), ()))
TN = (((0,), (0,)), ((), ()))


def mm(a, b, dims=NN):
    return lax.dot_general(a, b, dims, preferred_element_type=F32)


def iota(shape, dim):
    return lax.broadcasted_iota(jnp.int32, shape, dim)


def cost(flops, nbytes, exps=0):
    return pl.CostEstimate(flops=flops, bytes_accessed=nbytes, transcendentals=exps)


def params(n=1):
    return pltpu.CompilerParams(
        dimension_semantics=("arbitrary",) * n, vmem_limit_bytes=VMEM_LIMIT
    )


def three(x):
    hi = x.astype(BF)
    rest = x - hi.astype(F32)
    mid = rest.astype(BF)
    return hi.astype(F32), mid.astype(F32), rest - mid.astype(F32)


def self_fwd_kernel(len_ref, q_ref, k_ref, v_ref, o_ref, lse_ref):
    bq = 512
    length = len_ref[0]
    low = iota((LEN, 128), 1) < HEAD
    lane = iota((LEN, 128), 1)
    q, k, v = (ref[...] for ref in (q_ref, k_ref, v_ref))
    one = jnp.ones((LEN, 128), BF)
    zero = jnp.zeros((LEN, 128), BF)
    dead = jnp.where(iota((LEN, 128), 0) < length, 0.0, DEAD).astype(BF)
    at = lambda x, first: jnp.where(lane == first, x, zero)
    qs = (jnp.where(low, q, at(one, HEAD)), jnp.where(low, at(one, 0), q))
    ks = (jnp.where(low, k, at(dead, HEAD)), jnp.where(low, at(dead, 0), k))
    vs = (jnp.where(low, v, one), jnp.where(low, one, v))
    tri = iota((bq, bq), 1) <= iota((bq, bq), 0)
    low_q = low[:bq]
    for i in range(LEN // bq):
        lo, hi = i * bq, (i + 1) * bq
        outs, tops = [], []
        for h in range(2):
            here = jnp.where(tri, mm(qs[h][lo:hi], ks[h][lo:hi], NT), DEAD)
            m = jnp.max(here, axis=1, keepdims=True)
            if i:
                left = mm(qs[h][lo:hi], ks[h][:lo], NT)
                m = jnp.maximum(m, jnp.max(left, axis=1, keepdims=True))
            o = mm(jnp.exp2(here - m).astype(BF), vs[h][lo:hi])
            if i:
                o += mm(jnp.exp2(left - m).astype(BF), vs[h][:lo])
            outs.append(o)
            tops.append(m)
        a, b = outs
        o_ref[lo:hi, :] = (jnp.where(low_q, a, b) / pltpu.roll(jnp.where(low_q, b, a), HEAD, 1)).astype(BF)
        lse_ref[lo:hi, :] = jnp.where(low_q, tops[1], tops[0]) + jnp.log2(jnp.where(low_q, b, a))


def self_fwd(qkv, length):
    pairs = qkv.shape[1] // 3 // 128
    block = lambda part: pl.BlockSpec((LEN, 128), lambda i, n: (0, part * pairs + i))
    return pl.pallas_call(
        self_fwd_kernel,
        grid_spec=pltpu.PrefetchScalarGridSpec(
            num_scalar_prefetch=1,
            grid=(pairs,),
            in_specs=[block(0), block(1), block(2)],
            out_specs=[block(0), block(0)],
        ),
        out_shape=[
            jax.ShapeDtypeStruct((LEN, pairs * 128), BF),
            jax.ShapeDtypeStruct((LEN, pairs * 128), F32),
        ],
        compiler_params=params(),
        cost_estimate=cost(pairs * 2 * 4 * LEN * LEN * 128, pairs * 8 * LEN * 128),
    )(length, qkv, qkv, qkv)


def self_bwd_kernel(len_ref, q_ref, k_ref, v_ref, f_ref, o_ref, lse_ref, d_ref, dq_ref):
    bk = 256
    length = len_ref[0]
    lane = iota((LEN, 128), 1)
    low = lane < HEAD
    q, k, v, f = (ref[...] for ref in (q_ref, k_ref, v_ref, f_ref))
    zero = jnp.zeros((LEN, 128), BF)
    place = lax.rem(lane, HEAD)
    prod = f.astype(F32) * o_ref[...].astype(F32)
    crossed = jnp.where((iota((128, 128), 0) < HEAD) == (iota((128, 128), 1) < HEAD), 0.0, 1.0).astype(BF)
    prod_hi = prod.astype(BF)
    delta = mm(prod_hi, crossed) + mm((prod - prod_hi.astype(F32)).astype(BF), crossed)

    def free(x, last):
        hi, mid, rest = three(-x)
        out = jnp.where(place == 0, hi, jnp.where(place == 1, mid, jnp.where(place == 2, rest, last)))
        return out.astype(BF)

    q_free = free(lse_ref[...], jnp.where(place == 3, 1.0, 0.0))
    f_free = free(delta, jnp.zeros((LEN, 128), F32))
    dead = jnp.where(iota((LEN, 128), 0) < length, 0.0, DEAD)
    ones = jnp.where(place < 3, 1.0, 0.0)
    k_free = jnp.where(place == 3, dead, ones).astype(BF)
    v_free = ones.astype(BF)
    pick = lambda x, y: (jnp.where(low, x, y), jnp.where(low, y, x))
    qx, fx, kx, vx = pick(q, q_free), pick(f, f_free), pick(k, k_free), pick(v, v_free)
    qs, fs, ks = pick(q, zero), pick(f, zero), pick(k, zero)
    tri = iota((bk, bk), 0) <= iota((bk, bk), 1)
    for j in range(LEN // bk):
        lo, hi = j * bk, (j + 1) * bk
        ps, dss = [], []
        for h in range(2):
            p = jnp.exp2(mm(kx[h][lo:hi], qx[h][lo:], NT))
            first = jnp.where(tri, p[:, :bk], 0.0)
            p = jnp.concatenate([first, p[:, bk:]], axis=1) if hi < LEN else first
            ds = (p * mm(vx[h][lo:hi], fx[h][lo:], NT)).astype(BF)
            ps.append(p.astype(BF))
            dss.append(ds)
        dv = mm(jnp.concatenate(ps, axis=1), jnp.concatenate([fs[0][lo:], fs[1][lo:]], axis=0))
        dk = mm(jnp.concatenate(dss, axis=1), jnp.concatenate([qs[0][lo:], qs[1][lo:]], axis=0))
        kk = jnp.concatenate([ks[0][lo:hi], ks[1][lo:hi]], axis=0)
        part = mm(jnp.concatenate(dss, axis=0), kk, TN)
        if j:
            dq_ref[lo:, :] += part
        else:
            dq_ref[...] = part
        d_ref[1, lo:hi, :] = (dk * LN2).astype(BF)
        d_ref[2, lo:hi, :] = dv.astype(BF)
    d_ref[0] = (dq_ref[...] * 0.125).astype(BF)


def self_bwd(qkv, back, ctx, lse, length):
    pairs = qkv.shape[1] // 3 // 128
    block = lambda part: pl.BlockSpec((LEN, 128), lambda i, n: (0, part * pairs + i))
    return pl.pallas_call(
        self_bwd_kernel,
        grid_spec=pltpu.PrefetchScalarGridSpec(
            num_scalar_prefetch=1,
            grid=(pairs,),
            in_specs=[block(0), block(1), block(2), block(0), block(0), block(0)],
            out_specs=pl.BlockSpec((3, LEN, 128), lambda i, n: (0, 0, i)),
            scratch_shapes=[pltpu.VMEM((LEN, 128), F32)],
        ),
        out_shape=jax.ShapeDtypeStruct((3, LEN, pairs * 128), BF),
        compiler_params=params(),
        cost_estimate=cost(pairs * 2 * 10 * LEN * LEN * 128, pairs * 16 * LEN * 128),
    )(length, qkv, qkv, qkv, back, ctx, lse)


PER_STEP = 4


def own_heads():
    return jnp.where(iota((256, 256), 0) // SPAN == iota((256, 256), 1) // HEAD, 1.0, 0.0).astype(BF)


def spread(rows, mask):
    return jnp.concatenate([rows] * 4, axis=0) * mask


def gathered(rows, lanes):
    out = jnp.where(lanes == 0, rows[:SPAN], 0.0)
    for g in range(1, 4):
        out = jnp.where(lanes == g, rows[g * SPAN : (g + 1) * SPAN], out)
    return out


def fours(count, width, rows):
    for u in range(count):
        for t in range(width // 256):
            yield slice(u * SPAN, (u + 1) * SPAN), slice(u * rows, (u + 1) * rows), t * 256


def cross_fwd_kernel(q_ref, own_ref, oth_ref, o_ref):
    width = q_ref.shape[1]
    rows = own_ref.shape[0] // PER_STEP
    mask = own_heads()
    lanes = iota((SPAN, 256), 1) // HEAD
    one = jnp.ones((2 * rows, 128), BF)
    both = lambda at, lo: jnp.concatenate(
        [own_ref[at, lo : lo + 256], oth_ref[at, lo : lo + 256]], axis=0
    )
    jobs = list(fours(PER_STEP, width, rows))
    scores = [mm(spread(q_ref[q, lo : lo + 256], mask), both(kv, lo), NT) for q, kv, lo in jobs]
    probs = [jnp.exp2(s - jnp.max(s, axis=1, keepdims=True)).astype(BF) for s in scores]
    for p, (q, kv, lo) in zip(probs, jobs):
        o = mm(p, both(kv, width + lo))
        total = 1.0 / mm(p, one)
        o = o * jnp.concatenate([total, total], axis=1)
        o_ref[q, lo : lo + 256] = gathered(o, lanes).astype(BF)


def cross_fwd(q, own, oth):
    width = q.shape[1]
    spans = q.shape[0] // SPAN
    rows = own.shape[0] // spans
    row = pl.BlockSpec((PER_STEP * SPAN, width), lambda i: (i, 0))
    kv = pl.BlockSpec((PER_STEP * rows, 2 * width), lambda i: (i, 0))
    return pl.pallas_call(
        cross_fwd_kernel,
        grid=(spans // PER_STEP,),
        in_specs=[row, kv, kv],
        out_specs=row,
        out_shape=jax.ShapeDtypeStruct(q.shape, BF),
        compiler_params=params(),
        cost_estimate=cost(spans * 3 * 4 * 256**3, spans * 1000000),
    )(q, own, oth)


def cross_bwd_kernel(q_ref, own_ref, oth_a_ref, oth_b_ref, e_ref, dq_ref, down_ref, doth_ref):
    width = q_ref.shape[1]
    rows = own_ref.shape[0] // PER_STEP
    early = pl.program_id(0) < pl.num_programs(0) // 2
    oth = jnp.where(early, oth_a_ref[...], oth_b_ref[...])
    mask = own_heads()
    lanes = iota((SPAN, 256), 1) // HEAD
    both = lambda at, lo: jnp.concatenate([own_ref[at, lo : lo + 256], oth[at, lo : lo + 256]], axis=0)
    jobs = list(fours(PER_STEP, width, rows))
    q4 = [spread(q_ref[q, lo : lo + 256], mask) for q, kv, lo in jobs]
    e4 = [spread(e_ref[q, lo : lo + 256], mask) for q, kv, lo in jobs]
    scores = [mm(both(kv, lo), x, NT) for x, (q, kv, lo) in zip(q4, jobs)]
    backs = [mm(both(kv, width + lo), x, NT) for x, (q, kv, lo) in zip(e4, jobs)]
    for s, dp, x, y, (q, kv, lo) in zip(scores, backs, q4, e4, jobs):
        p = jnp.exp2(s - jnp.max(s, axis=0, keepdims=True))
        p = p * (1.0 / jnp.sum(p, axis=0, keepdims=True))
        delta = jnp.sum(p * dp, axis=0, keepdims=True)
        ds = (p * (dp - delta)).astype(BF)
        dk = (mm(ds, x) * LN2).astype(BF)
        dv = mm(p.astype(BF), y).astype(BF)
        down_ref[kv, lo : lo + 256] = dk[:rows]
        doth_ref[kv, lo : lo + 256] = dk[rows:]
        down_ref[kv, width + lo : width + lo + 256] = dv[:rows]
        doth_ref[kv, width + lo : width + lo + 256] = dv[rows:]
        dq_ref[q, lo : lo + 256] = (gathered(mm(ds, both(kv, lo), TN), lanes) * 0.125).astype(BF)


def cross_bwd(q, own, oth_a, oth_b, e):
    width = q.shape[1]
    spans = q.shape[0] // SPAN
    rows = own.shape[0] // spans
    steps = spans // PER_STEP
    row = pl.BlockSpec((PER_STEP * SPAN, width), lambda i: (i, 0))
    shape = (PER_STEP * rows, 2 * width)
    kv = pl.BlockSpec(shape, lambda i: (i, 0))
    return pl.pallas_call(
        cross_bwd_kernel,
        grid=(steps,),
        in_specs=[
            row,
            kv,
            pl.BlockSpec(shape, lambda i: (jnp.minimum(i, steps // 2 - 1), 0)),
            pl.BlockSpec(shape, lambda i: (jnp.maximum(i - steps // 2, 0), 0)),
            row,
        ],
        out_specs=[row, kv, kv],
        out_shape=[
            jax.ShapeDtypeStruct(q.shape, BF),
            jax.ShapeDtypeStruct(own.shape, BF),
            jax.ShapeDtypeStruct(own.shape, BF),
        ],
        compiler_params=params(),
        cost_estimate=cost(spans * 3 * 10 * 256**3, spans * 2000000),
    )(q, own, oth_a, oth_b, e)


def pick_kernel(keep_ref, send_ref, blocks_ref, keep_out, send_out, sems):
    count = keep_out.shape[0]
    copies = []
    for i in range(count):
        copies.append(
            pltpu.make_async_copy(blocks_ref.at[send_ref[i]], send_out.at[i], sems.at[0, i])
        )
    for i in range(count):
        copies.append(
            pltpu.make_async_copy(blocks_ref.at[keep_ref[i]], keep_out.at[i], sems.at[1, i])
        )
    for copy in copies:
        copy.start()
    for copy in copies:
        copy.wait()


def pick_blocks(neighbours, keep, send):
    count = keep.shape[0]
    smem = pl.BlockSpec(memory_space=pltpu.SMEM)
    anywhere = pl.BlockSpec(memory_space=pl.ANY)
    vmem = pl.BlockSpec(memory_space=pltpu.VMEM)
    return pl.pallas_call(
        pick_kernel,
        in_specs=[smem, smem, anywhere],
        out_specs=[vmem, vmem],
        out_shape=[jax.ShapeDtypeStruct((count,) + neighbours.shape[1:], BF)] * 2,
        scratch_shapes=[pltpu.SemaphoreType.DMA((2, count))],
        compiler_params=pltpu.CompilerParams(vmem_limit_bytes=VMEM_LIMIT),
        cost_estimate=cost(0, 4 * neighbours.size),
    )(keep, send, neighbours)


def pack_kernel(where_ref, qkv, kv, cq, wo, co, fin, fout, first, second, third, sems):
    core, p = where_ref[0], where_ref[1]
    d, hc = cq.shape
    e8, w8, o8 = d // 8, wo.shape[0] // 8, fout.shape[0] // 8
    take = lambda at, n: pl.ds(pl.multiple_of(at * n, 16), n)
    jobs = [(qkv.at[take(core, d // 2)], first)]
    to = 0
    for ref, count, n in ((kv, 2, e8), (cq, 1, e8), (wo, 2, w8), (co, 2, w8)):
        for i in range(count):
            jobs.append((ref.at[take(p, n), pl.ds(i * hc, hc)], second.at[pl.ds(to, n)]))
            to += n
    to = 0
    for i in range(fin.shape[1] // d):
        jobs.append((fin.at[take(p, w8), pl.ds(i * d, d)], third.at[pl.ds(to, w8)]))
        to += w8
    jobs.append((fout.at[take(p, o8)], third.at[pl.ds(to, o8)]))
    copies = [pltpu.make_async_copy(a, b, sems.at[i]) for i, (a, b) in enumerate(jobs)]
    for copy in copies:
        copy.start()
    for copy in copies:
        copy.wait()


def pack_weights(where, qkv, kv, cq, wo, co, fin, fout):
    anywhere = pl.BlockSpec(memory_space=pl.ANY)
    vmem = pl.BlockSpec(memory_space=pltpu.VMEM)
    d, hc = cq.shape
    n_in = fin.shape[1] // d
    return pl.pallas_call(
        pack_kernel,
        in_specs=[pl.BlockSpec(memory_space=pltpu.SMEM)] + [anywhere] * 7,
        out_specs=[vmem, vmem, vmem],
        out_shape=[
            jax.ShapeDtypeStruct((d // 2, 3 * hc), BF),
            jax.ShapeDtypeStruct((3 * (d // 8) + 4 * (wo.shape[0] // 8), hc), BF),
            jax.ShapeDtypeStruct((n_in * (fin.shape[0] // 8) + fout.shape[0] // 8, d), BF),
        ],
        scratch_shapes=[pltpu.SemaphoreType.DMA((9 + n_in,))],
        compiler_params=pltpu.CompilerParams(vmem_limit_bytes=VMEM_LIMIT),
        cost_estimate=cost(0, 4 * 1024 * 1024),
    )(where, qkv, kv, cq, wo, co, fin, fout)


def place_kernel(order_ref, mine_ref, theirs_ref, out_ref, wide, sems):
    count = mine_ref.shape[0]
    copies = []
    for i in range(count):
        copy = pltpu.make_async_copy(mine_ref.at[i], out_ref.at[order_ref[i]], sems.at[i])
        copy.start()
        copies.append(copy)
    for i in range(count):
        wide[i] = theirs_ref[i].astype(F32)
        copy = pltpu.make_async_copy(
            wide.at[i], out_ref.at[order_ref[count + i]], sems.at[count + i]
        )
        copy.start()
        copies.append(copy)
    for copy in copies:
        copy.wait()


def place_blocks(order, mine, theirs):
    count = order.shape[0]
    return pl.pallas_call(
        place_kernel,
        in_specs=[
            pl.BlockSpec(memory_space=pltpu.SMEM),
            pl.BlockSpec(memory_space=pltpu.VMEM),
            pl.BlockSpec(memory_space=pltpu.VMEM),
        ],
        out_specs=pl.BlockSpec(memory_space=pl.ANY),
        out_shape=jax.ShapeDtypeStruct((count,) + mine.shape[1:], F32),
        scratch_shapes=[
            pltpu.VMEM(mine.shape, F32),
            pltpu.SemaphoreType.DMA((count,)),
        ],
        compiler_params=pltpu.CompilerParams(vmem_limit_bytes=VMEM_LIMIT),
        cost_estimate=cost(0, 8 * mine.size),
    )(order, mine, theirs)


GELU_A = 0.7978845608028654
GELU_B = 0.044715


def feed_kernel(
    half_ref, h_ref, g_ref, r_ref, aa_ref, ab_ref, ba_ref, bb_ref, bina_ref, binb_ref,
    wouta_ref, woutb_ref, bout_ref,
    out_ref, dh_ref, keep_ref, send_ref, gbina_ref, gbinb_ref, h_t, acc, dacc, act_s, dpre_s,
):
    step = pl.program_id(0)
    hc = aa_ref.shape[0]
    bf = aa_ref.shape[1]

    @pl.when(step == 0)
    def _():
        h_t[...] = h_ref[...].T

    win = jnp.concatenate(
        [
            jnp.concatenate([aa_ref[...], ab_ref[...]], axis=1),
            jnp.concatenate([ba_ref[...], bb_ref[...]], axis=1),
        ],
        axis=0,
    )
    here = half_ref[0] == 0
    wa, wb = wouta_ref[...], woutb_ref[...]
    wout = jnp.concatenate([jnp.where(here, wa, wb), jnp.where(here, wb, wa)], axis=0)
    bias = jnp.concatenate([bina_ref[...], binb_ref[...]], axis=1)
    rows = h_ref.shape[0]
    first = step == 0
    total = jnp.zeros(bias.shape, F32)
    for lo in range(0, rows, 256):
        at = slice(lo, lo + 256)
        pre = mm(h_ref[at], win) + bias
        dact = mm(g_ref[at], wout, NT)
        square = pre * pre
        th = jnp.tanh(pre * (GELU_A + GELU_A * GELU_B * square))
        half = 0.5 + 0.5 * th
        act = (pre * half).astype(BF)
        slope = half + pre * (half - half * th) * (GELU_A + 3.0 * GELU_A * GELU_B * square)
        dpre = (dact * slope).astype(BF)
        total += jnp.sum(dpre.astype(F32), axis=0, keepdims=True)
        act_s[at] = act
        dpre_s[at] = dpre
        acc[at] = jnp.where(first, 0.0, acc[at]) + mm(act, wout)
        dacc[at] = jnp.where(first, 0.0, dacc[at]) + mm(dpre, win, NT)
    gbina_ref[0:1, :] = total[:, :bf]
    gbinb_ref[0:1, :] = total[:, bf:]
    gout = mm(act_s[...], g_ref[...], TN).astype(BF)
    gin = mm(h_t[...], dpre_s[...]).astype(BF)

    def put(into_in, into_out):
        into_in[0], into_in[1] = gin[:hc], gin[hc:]
        into_out[0] = jnp.where(here, gout[:bf], gout[bf:])
        into_out[1] = jnp.where(here, gout[bf:], gout[:bf])

    @pl.when(half_ref[1] == 0)
    def _():
        put(keep_ref, send_ref)

    @pl.when(half_ref[1] != 0)
    def _():
        put(send_ref, keep_ref)

    @pl.when(step == pl.num_programs(0) - 1)
    def _():
        out_ref[...] = (r_ref[...] + acc[...] + bout_ref[...]).astype(BF)
        dh_ref[...] = dacc[...]


def feed(where, h, g, r, win_own, win_oth, b_in, wout_own, wout_oth, b_out):
    rows, d = h.shape
    hc = win_own.shape[0]
    ff = win_own.shape[1]
    bf = 384
    n = ff // 2 // bf
    lower = lambda i, p: i
    upper = lambda i, p: n + i
    whole = pl.BlockSpec((rows, d), lambda i, p: (0, 0))
    side = lambda height, which: pl.BlockSpec((height, bf), lambda i, p: (0, which(i, p)))
    grad = pl.BlockSpec((2, bf, d), lambda i, p: (0, i, 0))
    wout = pl.BlockSpec((bf, d), lambda i, p: (i, 0))
    gb = pl.BlockSpec((8, bf), lambda i, p: (0, i))
    return pl.pallas_call(
        feed_kernel,
        grid_spec=pltpu.PrefetchScalarGridSpec(
            num_scalar_prefetch=1,
            grid=(n,),
            in_specs=[
                whole, whole, whole,
                side(hc, lower), side(hc, upper), side(hc, lower), side(hc, upper), side(1, lower), side(1, upper),
                wout, wout,
                pl.BlockSpec((1, d), lambda i, p: (0, 0)),
            ],
            out_specs=[whole, whole, grad, grad, gb, gb],
            scratch_shapes=[
                pltpu.VMEM((d, rows), BF),
                pltpu.VMEM((rows, d), F32),
                pltpu.VMEM((rows, d), F32),
                pltpu.VMEM((rows, 2 * bf), BF),
                pltpu.VMEM((rows, 2 * bf), BF),
            ],
        ),
        out_shape=[
            jax.ShapeDtypeStruct((rows, d), BF),
            jax.ShapeDtypeStruct((rows, d), F32),
            jax.ShapeDtypeStruct((2, ff // 2, d), BF),
            jax.ShapeDtypeStruct((2, ff // 2, d), BF),
            jax.ShapeDtypeStruct((8, ff // 2), F32),
            jax.ShapeDtypeStruct((8, ff // 2), F32),
        ],
        compiler_params=params(),
        cost_estimate=cost(12 * rows * d * ff, 8 * d * ff),
    )(where, h, g, r, win_own, win_own, win_oth, win_oth, b_in, b_in, wout_own, wout_oth, b_out)


def norm(rows, gain, bias):
    mean = jnp.mean(rows, axis=-1, keepdims=True)
    centred = rows - mean
    spread_ = jnp.mean(centred * centred, axis=-1, keepdims=True)
    return centred * lax.rsqrt(spread_ + EPS) * gain + bias


def norm_back(rows, gain, grad):
    mean = jnp.mean(rows, axis=-1, keepdims=True)
    centred = rows - mean
    rstd = lax.rsqrt(jnp.mean(centred * centred, axis=-1, keepdims=True) + EPS)
    hat = centred * rstd
    scaled = grad * gain
    inner = jnp.mean(scaled * hat, axis=-1, keepdims=True)
    back = rstd * (scaled - jnp.mean(scaled, axis=-1, keepdims=True) - hat * inner)
    return back, jnp.sum(grad * hat, axis=0), jnp.sum(grad, axis=0)


class Links:
    def __init__(self, dp, tp):
        self.dp = dp
        self.bits = dp.bit_length() - 1
        self.me = lax.axis_index("dp")
        self.core = self.me & 1
        self.half = lax.axis_index("tp")
        self.swap = [(i, tp - 1 - i) for i in range(tp)]
        rest = list(range(1, self.bits))
        turned = [2, 1] + rest[2:] if self.bits > 2 else rest
        self.steps = list(zip(rest, turned))

    def other(self, x):
        return lax.ppermute(x, "tp", self.swap)

    def across(self, x, step):
        return lax.ppermute(x, "dp", [(i, i ^ (1 << step[i & 1])) for i in range(self.dp)])

    def flag(self, step):
        return (self.me >> jnp.where(self.core == 0, step[0], step[1])) & 1

    def joined(self, mine, theirs, flag, axis=0):
        first = flag == 0
        return jnp.concatenate(
            [jnp.where(first, mine, theirs), jnp.where(first, theirs, mine)], axis=axis
        )

    def piece(self):
        return self.core * 4 + self.flag(self.steps[1]) * 2 + self.flag(self.steps[0])

    def spread(self, x, i):
        step = ([*self.steps[:2], (0, 0)])[i]
        return self.joined(x, self.across(x, step), self.flag(step))

    def fold(self, x, step):
        flag = self.flag(step)
        rows = x[0].shape[1] // 2
        part = lambda at: add(*(lax.dynamic_slice_in_dim(y, at * rows, rows, 1) for y in x))
        return part(flag), self.across(part(1 - flag), step)

    def meet(self, x):
        send = add(*(y[1:] for y in x))
        return add(*(y[:1] for y in x)), self.other(send)

    def halves(self, a, b):
        return jnp.where(self.core == 0, a, b), jnp.where(self.core == 0, b, a)

    def plane_sum(self):
        yield lambda x: (x[0], self.across(x[1], (0, 0)))
        for step in self.steps:
            yield functools.partial(self.fold, step=step)

    def plane_share(self):
        before = None
        for step in (*reversed(self.steps), (0, 0)):
            yield functools.partial(self.widen, before=before, step=step)
            before = step

    def widen(self, x, before, step):
        if before is not None:
            x = self.joined(*x, self.flag(before))
        return x, self.across(x, step)

    def pair(self, x):
        mine, theirs = x
        return jnp.where(self.core == 0, mine, theirs), jnp.where(self.core == 0, theirs, mine)


def add(a, b):
    return (a.astype(F32) + b.astype(F32)).astype(BF)


def tie(*arrays):
    return lax.optimization_barrier(arrays)


class Flow:
    def __init__(self, x, todo):
        self.x, self.todo = x, list(todo)

    def next(self):
        if self.todo:
            self.x = self.todo.pop(0)(self.x)


def advance(flows, *arrays):
    done = lax.optimization_barrier(([f.x for f in flows], *arrays))
    for f, x in zip(flows, done[0]):
        f.x = x
        f.next()
    return done[1] if len(arrays) == 1 else done[1:]


def shift_earlier(x):
    pad = jnp.zeros((SPAN - 1, x.shape[1]), x.dtype)
    return jnp.concatenate([x[SPAN - 1 :], pad], axis=0)


def shift_later(x):
    pad = jnp.zeros((SPAN - 1, x.shape[1]), x.dtype)
    return jnp.concatenate([pad, x[: x.shape[0] - SPAN + 1]], axis=0)


def on_device(
    tokens, neighbours, nbr_index, lengths, w_qkv, qv_bias, w_out, cross_q, cross_kv,
    cross_bias, cross_out, out_bias, ln_gain, ln_bias, fc_in, fc_in_bias, fc_out,
    fc_out_bias, cotangent,
):
    tp = lax.axis_size("tp")
    link = Links(lax.axis_size("dp"), tp)
    half = link.half
    d = tokens.shape[1]
    hc = w_qkv.shape[2]
    ffh = fc_in_bias.shape[0]
    ff = ffh * tp
    spans = nbr_index.shape[1] // tp
    length = lax.dynamic_slice_in_dim(lengths[0], half, 1)
    core = link.core

    small = jnp.concatenate(
        [fc_in_bias.reshape(-1, hc), fc_out_bias.reshape(1, hc), out_bias, ln_gain, ln_bias, qv_bias, cross_bias],
        axis=0,
    )
    small_oth = link.other(small)
    qkv_own = w_qkv.reshape(d, 3 * hc)
    eighth, w8, f8 = d // 8, hc // 8, hc // 8
    place = jnp.stack([core, link.piece()])
    first, second, third = pack_weights(
        place, qkv_own, cross_kv.reshape(d, 2 * hc), cross_q, w_out, cross_out, fc_in, fc_out
    )
    first = link.other(first)
    second = link.other(second)[None]

    order = nbr_index[0]
    keep = lax.dynamic_slice_in_dim(order, half * spans, spans)
    send = lax.dynamic_slice_in_dim(order, (1 - half) * spans, spans)
    nbr_own, nbr_send = pick_blocks(neighbours, keep, send)

    def whole(at, count, natural=True):
        a, b = small[at : at + count], small_oth[at : at + count]
        if natural:
            return link.joined(a, b, half, 1).astype(F32)
        return a.astype(F32), b.astype(F32)

    at = ffh // hc
    b_in = link.joined(small[:at].reshape(1, ffh), small_oth[:at].reshape(1, ffh), half, 1).astype(F32)
    b_out = whole(at, 1)
    out_b = whole(at + 1, 2)
    gains = whole(at + 3, 3)
    shifts = whole(at + 6, 3)
    qv_b = whole(at + 9, 2, False)
    cross_b = whole(at + 11, 2, False)

    tok = tokens.astype(F32)
    h1 = norm(tok, gains[0], shifts[0]).astype(BF)

    def project(w, which):
        bias = jnp.concatenate([qv_b[which][0], jnp.zeros((hc,), F32), qv_b[which][1]])
        scale = jnp.concatenate([jnp.full((hc,), SCORE, F32), jnp.ones((2 * hc,), F32)])
        return ((mm(h1, w) + bias) * scale).astype(BF)

    p_own = project(qkv_own, 0)
    ctx_own, lse_own = self_fwd(p_own, length)
    first, ctx_own, second, third, nbr_send = tie(first, ctx_own, second, third, nbr_send)
    qkv_pair = link.across(first, (0, 0))
    second = link.spread(second, 0)
    cutoff = spans // 2
    nbr_a = link.other(nbr_send[:cutoff])
    qkv_oth = link.joined(first, qkv_pair, core)
    p_oth = project(qkv_oth, 1)
    p_oth, second = tie(p_oth, second)
    second = link.spread(second, 1)
    ctx_oth, lse_oth = self_fwd(p_oth, length)
    ctx_oth, second, nbr_a, nbr_send, third = tie(ctx_oth, second, nbr_a, nbr_send, third)
    second = link.spread(second, 2)
    nbr_b = link.other(nbr_send[cutoff:])

    rows = lambda lo, n: second[:, lo : lo + n].reshape(8 * n, hc)
    ctx = jnp.concatenate([ctx_own, ctx_oth], axis=1)
    pair = lambda at: jnp.concatenate([rows(at, w8), rows(at + w8, w8)], axis=1)
    wo = jnp.concatenate([w_out, pair(3 * eighth)], axis=0)
    co_w = jnp.concatenate([cross_out, pair(3 * eighth + 2 * w8)], axis=0)
    cq_w = jnp.concatenate([cross_q, rows(2 * eighth, eighth)], axis=1)
    kv_w = jnp.concatenate(
        [cross_kv[:, 0], rows(0, eighth), cross_kv[:, 1], rows(eighth, eighth)], axis=1
    )
    r1 = tok + mm(ctx, wo) + out_b[0]
    h2 = norm(r1, gains[1], shifts[1]).astype(BF)
    cb = [jnp.concatenate([cross_b[0][i], cross_b[1][i]]) for i in range(2)]
    cq = shift_earlier(((mm(h2, cq_w) + cb[0]) * SCORE).astype(BF))
    kv_b = jnp.concatenate([jnp.zeros((d,), F32), cb[1]])
    nbr_own = nbr_own.reshape(-1, d)
    ckv_own = (mm(nbr_own, kv_w) + kv_b).astype(BF)
    cq, ckv_own, third = tie(cq, ckv_own, third)
    third = link.other(third)[None]
    half_rows = ckv_own.shape[0] // 2
    nbr_a = nbr_a.reshape(-1, d)
    ckv_a = (mm(nbr_a, kv_w) + kv_b).astype(BF)
    cq_rows = cutoff * SPAN
    c_a = cross_fwd(cq[:cq_rows], ckv_own[:half_rows], ckv_a)
    c_a, third, nbr_b = tie(c_a, third, nbr_b)
    third = link.spread(third, 0)
    nbr_b = nbr_b.reshape(-1, d)
    ckv_b = (mm(nbr_b, kv_w) + kv_b).astype(BF)
    ckv_b, third = tie(ckv_b, third)
    third = link.spread(third, 1)
    c_b = cross_fwd(cq[cq_rows:], ckv_own[half_rows:], ckv_b)
    cctx = shift_later(jnp.concatenate([c_a, c_b], axis=0))
    r2 = r1 + mm(cctx, co_w) + out_b[1]
    h3 = norm(r2, gains[2], shifts[2]).astype(BF)
    h3, third = tie(h3, third)
    third = link.spread(third, 2)
    turn = lambda x: link.joined(x[:, :hc], x[:, hc:], half, 1)
    win_oth = jnp.concatenate(
        [third[:, i * f8 : (i + 1) * f8].reshape(hc, d) for i in range(ff // d)], axis=1
    )
    wout_oth = third[:, (ff // d) * f8 :].reshape(ffh, d)
    block_out, d_h3, fc_keep, fc_send, gb_low, gb_high = feed(
        jnp.stack([half, core]), turn(h3), cotangent, r2, fc_in, win_oth, b_in, fc_out, wout_oth, b_out
    )

    plane, share = link.plane_sum, link.plane_share

    share_steps = list(share())

    def sum_flow(keep, send):
        steps = list(plane())
        steps[3:3] = [link.meet]
        return Flow((keep, send), steps + [lambda x: share_steps[0](add(*x)[0])] + share_steps[1:])

    fc = sum_flow(fc_keep, fc_send)
    fc.next()
    cot = cotangent.astype(F32)
    back3, gain3, shift3 = norm_back(r2, gains[2], turn(d_h3))
    d_r2 = cot + back3
    z2 = d_r2.astype(BF)
    e = mm(z2, co_w, NT).astype(BF)
    e, z2 = advance([fc], e, z2)
    d_cq, d_own, d_oth = cross_bwd(cq, ckv_own, ckv_a, ckv_b, shift_earlier(e))
    g_co = mm(cctx, z2, TN).astype(BF)
    d_cq, d_own, d_oth, g_co = advance([fc], d_cq, d_own, d_oth, g_co)
    n_oth = mm(d_oth, kv_w, NT).astype(BF).reshape(spans, -1, d)
    d_cq = shift_later(d_cq)
    back2, gain2, shift2 = norm_back(r1, gains[1], mm(d_cq, cq_w, NT))
    d_r1 = d_r2 + back2
    z1 = d_r1.astype(BF)
    f = mm(z1, wo, NT).astype(BF)
    n_oth, f, d_own = advance([fc], n_oth, f, d_own)
    n_back = link.other(n_oth)
    o_rows = d_oth.shape[0] // 2
    g_kv = (
        mm(nbr_own, d_own, TN) + mm(nbr_a, d_oth[:o_rows], TN) + mm(nbr_b, d_oth[o_rows:], TN)
    ).astype(BF)
    g_kv, d_cq, z1, d_own, f = advance([fc], g_kv, d_cq, z1, d_own, f)
    g_cq = mm(h2, d_cq, TN).astype(BF)
    g_wo = mm(ctx, z1, TN).astype(BF)
    sides = (slice(0, hc), slice(hc, d))
    both = lambda parts: jnp.stack([jnp.concatenate(p, axis=0) for p in parts])
    g_cross = both([[g_kv[:, s], g_kv[:, d:][:, s]] for s in sides]), both(
        [[g_cq[:, s], g_co[s][:, :hc], g_co[s][:, hc:]] for s in sides]
    )
    g_cross, g_wo, f, d_own = tie(link.halves(*g_cross), g_wo, f, d_own)
    cross = sum_flow(*g_cross)
    cross.next()
    n_own = mm(d_own, kv_w, NT).reshape(spans, -1, d)
    wide = lambda x: jnp.sum(x.astype(F32), axis=0)
    cqs, cvs = wide(d_cq), wide(d_own[:, d:]) + wide(d_oth[:, d:])
    early = jnp.concatenate(
        [gb_low[0], gb_high[0], wide(cot), wide(d_r1), wide(d_r2), gain2, gain3, shift2, shift3]
        + [link.joined(x[:hc], x[hc:], half) for x in (cqs, cvs)]
    )
    n_own, g_wo, f, early = advance([fc, cross], n_own, g_wo, f, early)
    dq_oth = self_bwd(p_oth, f[:, hc:], ctx_oth, lse_oth, length)
    dq_oth, f = advance([fc, cross], dq_oth, f)
    dq_own = self_bwd(p_own, f[:, :hc], ctx_own, lse_own, length)
    dq_own, d_own, g_wo = advance([fc, cross], dq_own, d_own, g_wo)
    g_qkv = [[mm(h1, part[i], TN).astype(BF) for part in (dq_own, dq_oth)] for i in range(3)]
    g_self = both([[q, k] for q, k in zip(g_qkv[0], g_qkv[1])]), both(
        [[v, g_wo[s][:, :hc], g_wo[s][:, hc:]] for v, s in zip(g_qkv[2], sides)]
    )
    g_self, dq_own, dq_oth = tie(link.halves(*g_self), dq_own, dq_oth)
    own = sum_flow(*g_self)
    own.next()
    flat = lambda x: jnp.concatenate([x[0], x[1], x[2]], axis=1)
    d_h1 = mm(flat(dq_own), qkv_own, NT) + mm(flat(dq_oth), qkv_oth, NT)
    d_h1, n_own, early = advance([own], d_h1, n_own, early)
    nbr_grad = place_blocks(order_of(keep, send), n_own, n_back)
    back1, gain1, shift1 = norm_back(tok, gains[0], d_h1)
    tokens_grad = d_r1 + back1

    late = [gain1, shift1] + [
        link.joined(wide(x), wide(y), half) for x, y in ((dq_own[0], dq_oth[0]), (dq_own[2], dq_oth[2]))
    ]
    natural = jnp.concatenate([early] + late)
    pad = -natural.shape[0] % 1024
    natural = jnp.concatenate([natural, jnp.zeros((pad,), F32)]).reshape(-1, 128)
    def total_of(x, move):
        x = x[0] + x[1] if isinstance(x, tuple) else x
        return x, move(x)

    every = [
        functools.partial(total_of, move=functools.partial(link.across, step=(b, b))) for b in range(link.bits)
    ] + [functools.partial(total_of, move=link.other)]
    tokens_grad, natural, nbr_grad = advance([fc, cross, own], tokens_grad, natural, nbr_grad)
    while fc.todo:
        advance([fc, cross, own])
    sums = Flow(natural, every)
    sums.next()
    wide_rows = lambda x, n: jnp.concatenate(
        [x[i * (x.shape[0] // n) : (i + 1) * (x.shape[0] // n)] for i in range(n)], axis=1
    )
    s_in, s_out = link.pair(fc.x)
    steps_in = s_in.shape[0] // hc
    fc_in_grad = jnp.concatenate(
        [wide_rows(s_in[:, :hc], steps_in), wide_rows(s_in[:, hc:], steps_in)], axis=1
    ).astype(F32)
    fc_in_grad, s_out = advance([cross, own, sums], fc_in_grad, s_out)
    fc_out_grad = s_out.astype(F32)
    fc_out_grad = advance([cross, own, sums], fc_out_grad)
    while cross.todo:
        advance([cross, own, sums])
    advance([cross, own, sums])
    s_kv, s_rest = link.pair(cross.x)
    cross_kv_grad = jnp.stack([s_kv[:d], s_kv[d:]], axis=1).astype(F32)
    cross_q_grad = s_rest[:d].astype(F32)
    co_grad = wide_rows(s_rest[d:], 2).astype(F32)
    while len(own.todo) > 1 or sums.todo:
        cross_kv_grad, cross_q_grad, co_grad = advance([own, sums], cross_kv_grad, cross_q_grad, co_grad)
    total = (sums.x[0] + sums.x[1]).reshape(-1)
    gb_in = lax.dynamic_slice_in_dim(total[:ff], half * ffh, ffh)
    rest = lax.dynamic_slice_in_dim(total[ff : ff + 13 * d].reshape(-1, d), half * hc, hc, 1)
    while own.todo:
        gb_in, rest = advance([own], gb_in, rest)
    s_qk, s_vw = link.pair(own.x)
    qkv_grad = jnp.stack([s_qk[:d], s_qk[d:], s_vw[:d]], axis=1).astype(F32)
    wo_grad = wide_rows(s_vw[d:], 2).astype(F32)
    pick = lambda *rows: jnp.stack([rest[i] for i in rows])
    return (
        block_out,
        tokens_grad,
        nbr_grad,
        qkv_grad,
        rest[11:13],
        wo_grad,
        cross_q_grad,
        cross_kv_grad,
        rest[7:9],
        co_grad,
        rest[1:3],
        pick(9, 3, 4),
        pick(10, 5, 6),
        fc_in_grad,
        gb_in,
        fc_out_grad,
        rest[0],
    )


def order_of(keep, send):
    return jnp.concatenate([keep, send])


def solution(mesh):
    return jax.shard_map(
        on_device,
        mesh=mesh,
        in_specs=(
            P(("dp", "tp"), None),
            P("dp", "tp", None),
            P("dp", None),
            P("dp", None),
            P(None, None, "tp"),
            P(None, "tp"),
            P("tp", None),
            P(None, "tp"),
            P(None, None, "tp"),
            P(None, "tp"),
            P("tp", None),
            P(None, "tp"),
            P(None, "tp"),
            P(None, "tp"),
            P("tp", None),
            P("tp"),
            P("tp", None),
            P("tp"),
            P(("dp", "tp"), None),
        ),
        out_specs=(
            P(("dp", "tp"), None),
            P(("dp", "tp"), None),
            P("dp", "tp", None),
            P(None, None, "tp"),
            P(None, "tp"),
            P("tp", None),
            P(None, "tp"),
            P(None, None, "tp"),
            P(None, "tp"),
            P("tp", None),
            P(None, "tp"),
            P(None, "tp"),
            P(None, "tp"),
            P("tp", None),
            P("tp"),
            P("tp", None),
            P("tp"),
        ),
        check_vma=False,
    )
```
